512 devices in a mesh: lon: 64 (over z, x), lat: 8 (over y, core).
Axes of the slice: x: 4, y: 4, z: 16, core: 2. Of those that a mesh axis runs over, the one named last changes fastest.
Arguments:
- right_side: float32 [4, 256, 8192], P(None, 'lat', 'lon'), may hold values from -40 to 40
- diagonal: float32 [256, 8192], P('lat', 'lon'), may hold values from 0.02 to 0.5
- east_face: float32 [256, 8192], P('lat', 'lon'), may hold values from 0.5 to 4
- north_face: float32 [256, 8192], P('lat', 'lon'), may hold values from 0.5 to 4
- wet: int32 [256, 8192], P('lat', 'lon'), may hold values 0 or 1
- active: int32 [8, 64, 32], P('lat', 'lon'), may hold values 0 or 1
- coupling: float32 [8, 64, 3, 32, 32], P('lat', 'lon'), may hold values from -0.625 to 0.625
- pivots: float32 [8, 2048, 2048], P('lat', 'lon'), may hold values from -1 to 1, as said below
Outputs:
- solution: float32 [4, 256, 8192], P(None, 'lat', 'lon')
The draws below stay inside these ranges and needn't reach their ends.
Inputs may be any that keep to these rules, and one draw needn't show every extreme that they name: `pivots`: each band's block is symmetric.
All inputs are finite; a program needn't handle non-finite values. No bound on the sum of `wet` or of `active` on one device may be relied on, other than what follows from the above.
Results may differ from the reference program's by a relative error of at most 0.0011.
Values sent between devices are 32-bit elements; how exact they have to be, the bound alone decides.
No kernel may reach another device: no remote copies, remote signals or barrier semaphores. Data moves between devices by JAX's collectives and lax.ppermute only.
A program may use at most 128 MiB of HBM per device.

```python
import math
import jax
import jax.numpy as jnp
from jax import lax

MEMBERS = 4
KLAT = 4
KLON = 8
ITERS = 2
K = 32
BANDS = 8
TILES = 64
NLAT = 256
NLON = 8192
NC = 2048
N_LON = 64
N_LAT = 8


def draw_right_side(key, part):
    key = jax.random.fold_in(key, 11)
    lat_frac = (jnp.arange(NLAT, dtype=jnp.float32) / NLAT)[None, :, None]
    lon_frac = (jnp.arange(NLON, dtype=jnp.float32) / NLON)[None, None, :]
    full_shape = (MEMBERS, NLAT, NLON)
    amplitude = 10.0 ** lat_frac * 3.0 ** lon_frac / 3.0
    return jax.random.truncated_normal(key, -4.0, 4.0, full_shape, jnp.float32) * amplitude


def draw_pivots(key, part):
    key = jax.random.fold_in(key, 23)
    rough_key, leading_key = jax.random.split(key)
    full_shape = (N_LAT, NC, NC)
    block_cells = NLAT // (N_LAT * KLAT) * (NLON // (N_LON * KLON))
    magnitude = 1.0 / (6.0 * block_cells ** 0.5)
    roughness = jax.random.normal(rough_key, full_shape, jnp.float32) * 0.45
    leading = jax.random.uniform(leading_key, (N_LAT, NC), jnp.float32, 1.0, 1.6)
    symmetric = (roughness + jnp.swapaxes(roughness, 1, 2)) * (0.5 / NC ** 0.5)
    counter = jnp.arange(NC)
    identity = (counter[:, None] == counter[None, :]).astype(jnp.float32)
    return magnitude * (symmetric + identity[None] * leading[:, :, None])


def touch_ends(result, key, low, top_value):
    longest = result.shape.index(max(result.shape))
    spots = []
    for shift in (0, 1):
        where = [jax.random.randint(jax.random.fold_in(key, axis), (), 0, length) for axis, length in enumerate(result.shape)]
        where[longest] = (where[longest] + shift) % result.shape[longest]
        spots.append(tuple(where))
    return result.at[spots[0]].set(low).at[spots[1]].set(top_value)


def block_levels(own_key, dims, cuts, least, top_value):
    loudness, own = 1.0, jax.random.fold_in(own_key, 6)
    for axis_at, parts in cuts:
        draws = jnp.exp(jax.random.uniform(jax.random.fold_in(own, axis_at), (parts,), jnp.float32, least / len(cuts), top_value / len(cuts)))
        loudness = loudness * jnp.repeat(draws, dims[axis_at] // parts).reshape([-1 if axis == axis_at else 1 for axis in range(len(dims))])
    return loudness


def centred(rng, extent, scale, most, cuts=(), held_as=jnp.bfloat16):
    values = scale * jax.random.normal(rng, extent, jnp.float32)
    if cuts:
        values = values * block_levels(rng, extent, cuts, -0.22, 0.18)
    return jnp.clip(values, -most, most).astype(held_as)


def setup_inputs(seed: int = 0) -> dict:
    splits = jax.random.split(jax.random.key(seed), 9)
    right_side = draw_right_side(jax.random.fold_in(splits[8], 71), 0)
    diagonal = jnp.clip(jnp.exp(math.log(0.5) - 3.218876 * jax.random.uniform(splits[1], (NLAT, NLON), jnp.float32) ** block_levels(splits[1], (NLAT, NLON), ((0, 8), (1, 64)), -0.2, 0.2)), 0.02, 0.5)
    east_face = jnp.clip(jnp.exp(math.log(4.0) - 2.0794415 * jax.random.uniform(splits[2], (NLAT, NLON), jnp.float32) ** block_levels(splits[2], (NLAT, NLON), ((0, 8), (1, 64)), -0.2, 0.2)), 0.5, 4.0)
    north_face = jnp.clip(jnp.exp(math.log(4.0) - 2.0794415 * jax.random.uniform(splits[3], (NLAT, NLON), jnp.float32) ** block_levels(splits[3], (NLAT, NLON), ((0, 8), (1, 64)), -0.2, 0.2)), 0.5, 4.0)
    wet = touch_ends((jax.random.randint(splits[4], (NLAT, NLON), 0, 5) < 4).astype(jnp.int32), jax.random.fold_in(splits[4], 1), 0, 1)
    active = touch_ends((jax.random.randint(splits[5], (BANDS, TILES, K), 0, 4) < 3).astype(jnp.int32), jax.random.fold_in(splits[5], 1), 0, 1)
    coupling = centred(splits[6], (BANDS, TILES, 3, K, K), (3 * K) ** -0.5, 0.625, ((0, 8), (1, 64)), jnp.float32)
    pivots = draw_pivots(jax.random.fold_in(splits[8], 71), 0)
    return {"right_side": right_side, "diagonal": diagonal, "east_face": east_face, "north_face": north_face, "wet": wet, "active": active, "coupling": coupling, "pivots": pivots}


PRECISE = lax.Precision.HIGHEST


def reference(right_side, diagonal, east_face, north_face, wet, active, coupling, pivots):
    wet_mask = wet.astype(jnp.float32)
    row_count = wet_mask.shape[0]
    has_north = (jnp.arange(row_count) < row_count - 1).astype(jnp.float32)[:, None]
    face_east = east_face * wet_mask * jnp.roll(wet_mask, -1, 1)
    face_west = jnp.roll(face_east, 1, 1)
    face_north = north_face * wet_mask * jnp.roll(wet_mask, -1, 0) * has_north
    face_south = jnp.concatenate([jnp.zeros((1, wet_mask.shape[1]), jnp.float32), face_north[:-1]], 0)
    centre = wet_mask * diagonal + (1.0 - wet_mask)
    inverse = 1.0 / (centre + face_east + face_west + face_north + face_south)

    def operate(values):
        return (centre * values + face_east * (values - jnp.roll(values, -1, 2))
                + face_west * (values - jnp.roll(values, 1, 2))
                + face_north * (values - jnp.roll(values, -1, 1))
                + face_south * (values - jnp.roll(values, 1, 1)))

    member_count = right_side.shape[0]
    block_lat = NLAT // (N_LAT * KLAT)
    block_lon = NLON // (N_LON * KLON)
    live = active.astype(jnp.float32)[..., None]

    def precondition(residual):
        sums = jnp.sum((residual * wet_mask).reshape(member_count, N_LAT, KLAT, block_lat, N_LON, KLON, block_lon), axis=(3, 6))
        coarse = jnp.transpose(sums, (1, 3, 2, 4, 0)).reshape(N_LAT, N_LON, K, member_count) * live
        forward_list = [coarse[0]]
        for band_index in range(1, N_LAT):
            earlier = forward_list[-1]
            carried = jnp.zeros_like(earlier)
            for slot in range(3):
                carried = carried + jnp.einsum("ikl,ilm->ikm", coupling[band_index, :, slot], jnp.roll(earlier, 1 - slot, 0), precision=PRECISE)
            forward_list.append(coarse[band_index] - carried)
        pivoted = []
        for band_index in range(N_LAT):
            product = jnp.dot(pivots[band_index], forward_list[band_index].reshape(NC, member_count), precision=PRECISE, preferred_element_type=jnp.float32)
            pivoted.append(product.reshape(N_LON, K, member_count))
        backward_list = [pivoted[-1]]
        for band_index in range(N_LAT - 2, -1, -1):
            later = backward_list[0]
            arriving = jnp.zeros_like(later)
            for slot in range(3):
                products = jnp.einsum("ilk,ilm->ikm", coupling[band_index + 1, :, slot], later, precision=PRECISE)
                arriving = arriving + jnp.roll(products, slot - 1, 0)
            backward_list.insert(0, pivoted[band_index] - arriving)
        settled = jnp.stack(backward_list) * live
        shaped = jnp.transpose(settled.reshape(N_LAT, N_LON, KLAT, KLON, member_count), (4, 0, 2, 1, 3))
        spread = jnp.broadcast_to(shaped[:, :, :, None, :, :, None], (member_count, N_LAT, KLAT, block_lat, N_LON, KLON, block_lon))
        spread = spread.reshape(member_count, NLAT, NLON)
        return residual * inverse + spread * wet_mask

    solution = jnp.zeros_like(right_side)
    residual = right_side
    preconditioned = precondition(residual)
    direction = preconditioned
    weight = jnp.sum(residual * preconditioned, axis=(1, 2))
    for iteration in range(ITERS):
        image = operate(direction)
        step_size = weight / jnp.sum(direction * image, axis=(1, 2))
        solution = solution + step_size[:, None, None] * direction
        if iteration + 1 < ITERS:
            residual = residual - step_size[:, None, None] * image
            preconditioned = precondition(residual)
            renewed = jnp.sum(residual * preconditioned, axis=(1, 2))
            direction = preconditioned + (renewed / weight)[:, None, None] * direction
            weight = renewed
    return solution
```

```python
import functools

import jax
import jax.numpy as jnp
from jax import lax
from jax.experimental import pallas as pl
from jax.experimental.pallas import tpu as pltpu
from jax.sharding import Mesh
from jax.sharding import PartitionSpec as P

F32 = jnp.float32
BF16 = jnp.bfloat16
M = 4
NB = 8
NX = 4
NZ = 16
NG = 5
ROWS = 32
COLS = 128
HALO = 3
EXT_ROWS = 40
EXT_COLS = 256
NT = (((1,), (1,)), ((), ()))
NN = (((1,), (0,)), ((), ()))
VMEM_BYTES = 40 * 1024 * 1024


def call(kernel, outs, pos, *arrays):
    vmem = pl.BlockSpec(memory_space=pltpu.VMEM)
    return pl.pallas_call(
        kernel,
        out_shape=[jax.ShapeDtypeStruct(s, F32) for s in outs],
        in_specs=[pl.BlockSpec(memory_space=pltpu.SMEM)] + [vmem] * len(arrays),
        out_specs=[vmem] * len(outs),
        compiler_params=pltpu.CompilerParams(vmem_limit_bytes=VMEM_BYTES),
    )(pos, *arrays)


def iota(shape, dim):
    return lax.broadcasted_iota(jnp.int32, shape, dim)


def roll(value, shift, axis):
    shift = shift % value.shape[axis]
    return value if shift == 0 else pltpu.roll(value, shift, axis)


def mm(a, b, dims):
    return lax.dot_general(a, b, dims, preferred_element_type=F32)


def halves(value):
    hi = value.astype(BF16)
    return hi, (value - hi.astype(F32)).astype(BF16)


def dot3(a, b_hi, b_lo, dims):
    hi = a.astype(BF16).astype(F32)
    both = jnp.concatenate([hi, a - hi], axis=0).astype(BF16)
    n = a.shape[0]
    top = mm(both, b_hi, dims)
    low = mm(both, b_lo, dims)
    return top[:n] + top[n:] + low[:n]


def dot_exact(a, b):
    hi = a.astype(BF16).astype(F32)
    rest = a - hi
    mid = rest.astype(BF16).astype(F32)
    parts = jnp.concatenate([hi, mid, rest - mid], axis=0).astype(BF16)
    out = mm(parts, b, NN)
    n = a.shape[0]
    return out[:n] + out[n : 2 * n] + out[2 * n :]


def lane_group():
    return iota((8, 128), 1) // 32


def pick(values):
    group = lane_group()
    out = values[-1]
    for i in range(len(values) - 2, -1, -1):
        out = jnp.where(group == i, values[i], out)
    return out


def block_sums(fields):
    rows = [jnp.sum(f.reshape(4, 8, COLS), axis=1) for f in fields]
    stacked = jnp.concatenate(rows, axis=0)
    pad = -stacked.shape[0] % 16
    if pad:
        stacked = jnp.concatenate([stacked, jnp.zeros((pad, COLS), F32)], axis=0)
    gather = (iota((COLS, COLS), 0) // 16 == iota((COLS, COLS), 1) % 8).astype(F32).astype(BF16)
    sums = dot_exact(stacked, gather)
    kr = (iota((1, COLS), 1) // 8) % 4
    out = []
    for i in range(len(fields)):
        row = jnp.zeros((1, COLS), F32)
        for j in range(4):
            row = jnp.where(kr == j, sums[4 * i + j : 4 * i + j + 1], row)
        out.append(row)
    return out


def member_rows(rows):
    sub = iota((8, 128), 0)
    out = jnp.zeros((8, 128), F32)
    for m, row in enumerate(rows):
        out = jnp.where(sub == m, row, out)
    return out


def full_sum(value):
    return jnp.sum(jnp.sum(value, axis=1, keepdims=True), axis=0, keepdims=True)


def operate(v, fields):
    fe, fw, fn, fs, centre = fields
    return (
        centre * v
        + fe * (v - roll(v, -1, 1))
        + fw * (v - roll(v, 1, 1))
        + fn * (v - roll(v, -1, 0))
        + fs * (v - roll(v, 1, 0))
    )


def main(value):
    return value[:ROWS, :COLS]


def coarse_kernel(pos, right, wet, act, out):
    mask = wet[...]
    rows = block_sums([right[m] * mask for m in range(M)])
    own = lane_group() == pos[1]
    out[...] = jnp.where(own, member_rows(rows) * act[...], 0.0)


def fields_kernel(pos, ext, act, consts, early):
    b = pos[2]
    diag, east, north, wet = (ext[4 + i] for i in range(4))
    row = iota((EXT_ROWS, EXT_COLS), 0)
    grid_row = b * ROWS + jnp.where(row >= 36, row - EXT_ROWS, row)
    inside = jnp.logical_and(grid_row >= 0, grid_row < NB * ROWS - 1)
    fe = east * wet * roll(wet, -1, 1)
    fw = roll(fe, 1, 1)
    fn = jnp.where(inside, north * wet * roll(wet, -1, 0), 0.0)
    fs = roll(fn, 1, 0)
    own = wet * diag
    centre = own + (1.0 - wet)
    inverse = 1.0 / (centre + fe + fw + fn + fs)
    for i, v in enumerate((fe, fw, fn, fs, centre, inverse, wet)):
        consts[i] = v
    mask = main(wet)
    row = iota((ROWS, COLS), 0)
    col = iota((ROWS, COLS), 1)
    sums = [
        jnp.where(col % 16 == 15, main(fe), 0.0),
        jnp.where(col % 16 == 0, main(fw), 0.0),
        jnp.where(row % 8 == 7, main(fn), 0.0),
        jnp.where(row % 8 == 0, main(fs), 0.0),
        main(own),
    ]
    energy, smooth = [], []
    for m in range(M):
        r = ext[m]
        y = inverse * r
        image = main(operate(y, (fe, fw, fn, fs, centre)))
        sums.append(mask * image)
        energy.append(full_sum(main(y) * image))
        smooth.append(full_sum(main(y) * main(r)))
    rows = block_sums(sums)
    lane = iota((8, 128), 1) % 32
    scalars = jnp.where(lane == 0, member_rows(energy), jnp.where(lane == 1, member_rows(smooth), 0.0))
    early[0] = pick([member_rows(rows[5:])] * 2 + [jnp.broadcast_to(rows[0], (8, 128)), jnp.broadcast_to(rows[1], (8, 128))])
    early[1] = pick([jnp.broadcast_to(rows[i], (8, 128)) for i in (2, 3, 4)] + [jnp.broadcast_to(act[...], (8, 128))])
    early[2] = scalars


def weights(blocks, b, g):
    c, y = b % 2, b // 2
    block = jnp.concatenate([blocks[c * 16 + x * 4 + y, 32 * g : 32 * g + 32, :] for x in range(NX)], axis=0)
    return halves(block)


def forward_sweep(coarse, blocks, mine):
    group = lane_group()
    zero = jnp.zeros((8, 128), F32)
    s = [zero, zero, coarse[0], zero, zero]
    out = s
    for b in range(1, NB):
        new = []
        for g in range(NG):
            left = s[g - 1] if g > 0 else zero
            right = s[g + 1] if g < NG - 1 else zero
            lhs = jnp.concatenate(
                [jnp.where(group == 3, left, s[g]), s[g], s[g], jnp.where(group == 0, right, s[g])], axis=0
            )
            hi, lo = weights(blocks, b, g)
            o = dot3(lhs, hi, lo, NT)
            carried = pick([o[8 * x : 8 * x + 8] for x in range(NX)])
            new.append(coarse[b] - carried if g == 2 else -carried)
        s = new
        out = [jnp.where(mine == b, s[g], out[g]) for g in range(NG)]
    return out


def backward_sweep(pivoted, blocks):
    group = lane_group()
    zero = jnp.zeros((8, 128), F32)
    s = pivoted[NB - 1]
    out = [None] * NB
    out[NB - 1] = s
    for b in range(NB - 2, -1, -1):
        o = []
        for g in range(NG):
            lhs = jnp.concatenate([jnp.where(group == x, s[g], 0.0) for x in range(NX)], axis=0)
            hi, lo = weights(blocks, b + 1, g)
            o.append(dot3(lhs, hi, lo, NN))
        s = []
        for g in range(NG):
            own = o[g][8:16] + o[g][16:24]
            own = own + jnp.where(group == 3, 0.0, o[g][0:8]) + jnp.where(group == 0, 0.0, o[g][24:32])
            after = o[g + 1][0:8] if g < NG - 1 else zero
            before = o[g - 1][24:32] if g > 0 else zero
            own = own + jnp.where(group == 3, after, 0.0) + jnp.where(group == 0, before, 0.0)
            s.append(pivoted[b][g] - own)
        out[b] = s
    return out


def pack_window(s, extra, out):
    upper = iota((8, 128), 0) >= 4
    parts = list(s) + [extra]
    for i in range(3):
        out[8 * i : 8 * i + 8, :] = jnp.where(upper, roll(parts[2 * i + 1], 4, 0), parts[2 * i])


def unpack_swept(got):
    out = []
    for z in range(NZ):
        even = got[(z + 2) % NZ, 0:8, :] + got[z, 8:16, :] + got[(z - 2) % NZ, 16:24, :]
        odd = got[(z + 1) % NZ, 0:8, :] + got[(z - 1) % NZ, 8:16, :]
        out.append(even + roll(odd, 4, 0))
    return jnp.concatenate(out, axis=1)


def pivot_product(swept, pivots):
    rows = jnp.concatenate([p[...] for p in pivots], axis=0)
    hi, lo = halves(rows)
    out = dot3(swept, hi, lo, NT)
    return out[:, :128], jnp.concatenate([out[:, 128:160]] * 4, axis=1)


def unpack_plane(got, field):
    group = iota((64, 128), 1) // 32
    half = field // 4 * 128
    out = None
    for x in range(NX):
        piece = roll(got[64 * x : 64 * x + 64, half : half + 128], 32 * (x - field % 4), 1)
        out = piece if out is None else jnp.where(group == x, piece, out)
    return out


def coarse_operate(s, before, after, t):
    fe, fw, fn, fs, dg = t
    lane = iota((64, 128), 1)
    kc, kr = lane % 8, (lane // 8) % 4
    east = jnp.where(kc < 7, roll(s, -1, 1), jnp.where(lane < 96, roll(s, -25, 1), roll(after, -25, 1)))
    west = jnp.where(kc > 0, roll(s, 1, 1), jnp.where(lane >= 32, roll(s, 25, 1), roll(before, 25, 1)))
    north = jnp.where(kr < 3, roll(s, -8, 1), roll(roll(s, 24, 1), -8, 0))
    south = jnp.where(kr > 0, roll(s, 8, 1), roll(roll(s, -24, 1), 8, 0))
    return dg * s + fe * (s - east) + fw * (s - west) + fn * (s - north) + fs * (s - south)


def band_sum(value):
    acc = value[0:8]
    for b in range(1, NB):
        acc = acc + value[8 * b : 8 * b + 8]
    return jnp.sum(acc, axis=1, keepdims=True)


def forward_kernel(pos, blocks, act, out, coarse_out):
    coarse = []
    for b in range(NB):
        c, y = b % 2, b // 2
        acc = blocks[c * 16 + y, 160:168, :]
        for x in range(1, NX):
            acc = acc + blocks[c * 16 + x * 4 + y, 160:168, :]
        coarse.append(acc)
        coarse_out[8 * b : 8 * b + 8, :] = acc
    s = forward_sweep(coarse, blocks, pos[2])
    pack_window(s, jnp.broadcast_to(act[...], (8, 128)), out)


def pivot_kernel(pos, got, early, p0, p1, p2, p3, p4, out):
    z = pos[0]
    first, last = pivot_product(unpack_swept(got), (p0, p1, p2, p3, p4))
    act_before = jnp.broadcast_to(got[lax.rem(z + NZ - 1, NZ), 20:21, :], (8, 128))
    act_after = jnp.broadcast_to(got[lax.rem(z + 1, NZ), 20:21, :], (8, 128))
    group = lane_group()
    upper = iota((8, 128), 0) >= 4
    second = jnp.where(group == 0, last, early[0])
    fourth = pick([act_before, act_after, early[2], jnp.zeros((8, 128), F32)])
    out[:, :128] = jnp.where(upper, roll(early[1], 4, 0), first)
    out[:, 128:] = jnp.where(upper, roll(fourth, 4, 0), second)


def upper_half(value):
    return roll(value, -4, 0)


def middle_kernel(pos, got, blocks, coarse_right, out, s_out, coarse_image_out, t_out):
    windows = [unpack_plane(got, f) for f in range(8)]
    pivoted = [[windows[g][8 * b : 8 * b + 8] for g in range(NG)] for b in range(NB)]
    settled = backward_sweep(pivoted, blocks)
    act = upper_half(windows[3])
    s1, s2, s3 = (
        jnp.concatenate([settled[b][g] for b in range(NB)], axis=0) * a
        for g, a in ((1, upper_half(windows[4])), (2, act), (3, upper_half(windows[5])))
    )
    t = (windows[6], windows[7], upper_half(windows[0]), upper_half(windows[1]), upper_half(windows[2]))
    t_s = coarse_operate(s2, s1, s3, t)
    smooth = windows[5]
    coarse_image = act * (smooth + t_s)
    scalars = upper_half(windows[6])
    lane = iota((64, 128), 1) % 32
    c_r = coarse_right[...]
    weight = band_sum(c_r * s2 + jnp.where(lane == 1, scalars, 0.0))
    energy = band_sum((2.0 * smooth + t_s) * s2 + jnp.where(lane == 0, scalars, 0.0))
    lane8 = iota((8, 128), 1)
    extra = jnp.where(lane8 == 0, weight, jnp.where(lane8 == 1, energy, 0.0))
    for i, v in enumerate((s1, s2, s3)):
        s_out[i] = v
    coarse_image_out[...] = coarse_image
    for i, v in enumerate(t + (act, windows[4], windows[5])):
        t_out[i] = v
    t_out[6] = upper_half(windows[4])
    t_out[7] = upper_half(windows[5])
    s = forward_sweep([coarse_image[8 * b : 8 * b + 8] for b in range(NB)], blocks, pos[2])
    pack_window(s, extra, out)


def spread_rows(s, x, kr):
    lane = iota((8, 128), 1)
    return jnp.take_along_axis(s, x * 32 + kr * 8 + lane // 16, axis=1)


def spread_sides(s1, s2, s3, x, kr):
    lane = iota((8, 128), 1)
    east = jnp.take_along_axis(jnp.where(x < 3, s2, s3), jnp.zeros_like(lane) + lax.rem(x + 1, 4) * 32 + kr * 8, axis=1)
    west = jnp.take_along_axis(jnp.where(x > 0, s2, s1), jnp.zeros_like(lane) + lax.rem(x + 3, 4) * 32 + kr * 8 + 7, axis=1)
    return jnp.where(lane < 64, east, west)


def image_kernel(pos, ext, consts, s_ref, pre_out, image_out):
    x, b = pos[1], pos[2]
    north_band, south_band = lax.rem(b + 1, NB), lax.rem(b + NB - 1, NB)
    own = [s_ref[g, b] for g in range(3)]
    up = [s_ref[g, north_band] for g in range(3)]
    down = [s_ref[g, south_band] for g in range(3)]
    mains = [spread_rows(own[1], x, kr) for kr in range(4)]
    sides = [spread_sides(*own, x, kr) for kr in range(4)]
    first = iota((8, 128), 0) < 4
    up_main, up_side = spread_rows(up[1], x, 0), spread_sides(*up, x, 0)
    down_main, down_side = spread_rows(down[1], x, 3), spread_sides(*down, x, 3)
    fields = tuple(consts[i] for i in range(5))
    inverse, wet = consts[5], consts[6]
    for m in range(M):
        wide = lambda v: jnp.broadcast_to(v[m : m + 1], (8, 128))
        left = [wide(v) for v in mains] + [jnp.where(first, wide(up_main), wide(down_main))]
        right = [wide(v) for v in sides] + [jnp.where(first, wide(up_side), wide(down_side))]
        spread = jnp.concatenate([jnp.concatenate(left, axis=0), jnp.concatenate(right, axis=0)], axis=1)
        pre = inverse * ext[m] + wet * spread
        pre_out[m] = main(pre)
        image_out[m] = operate(pre, fields)


def step_kernel(pos, got, ext, consts, image, p0, p1, p2, p3, p4, out, smooth_out, scalar_out):
    first, last = pivot_product(unpack_swept(got), (p0, p1, p2, p3, p4))
    sums = got[0, 16:24, :]
    for z in range(1, NZ):
        sums = sums + got[z, 16:24, :]
    sums = upper_half(sums)
    weight, energy = sums[:, 0:1], sums[:, 1:2]
    step = weight / energy
    fields = tuple(consts[i] for i in range(5))
    inverse, wet = consts[5], consts[6]
    mask = main(wet)
    blocks, dots = [], ([], [], [])
    for m in range(M):
        residual = ext[m] - step[m : m + 1] * image[m]
        smooth = inverse * residual
        applied = main(operate(smooth, fields))
        smooth = main(smooth)
        smooth_out[m] = smooth
        blocks.append(mask * applied)
        dots[0].append(full_sum(smooth * main(residual)))
        dots[1].append(full_sum(smooth * applied))
        dots[2].append(full_sum(smooth * main(image[m])))
    rows = member_rows(block_sums(blocks))
    lane = iota((8, 128), 1) % 32
    scalars = jnp.zeros((8, 128), F32)
    for i in range(3):
        scalars = jnp.where(lane == i, member_rows(dots[i]), scalars)
    out[:, :128] = first
    out[:, 128:] = pick([last, rows, scalars, jnp.zeros((8, 128), F32)])
    lane = iota((8, 128), 1)
    scalar_out[...] = jnp.where(lane == 0, weight, jnp.where(lane == 1, energy, jnp.where(lane == 2, step, 0.0)))


def last_kernel(pos, got, blocks, s_ref, coarse_right, coarse_image, t_ref, scalar, out, s_out):
    windows = [unpack_plane(got, f) for f in range(7)]
    pivoted = [[windows[g][8 * b : 8 * b + 8] for g in range(NG)] for b in range(NB)]
    settled = backward_sweep(pivoted, blocks)
    t = tuple(t_ref[i] for i in range(5))
    step = jnp.concatenate([scalar[:, 2:3]] * NB, axis=0)
    s1, s2, s3 = (
        s_ref[g - 1] - step * (jnp.concatenate([settled[b][g] for b in range(NB)], axis=0) * t_ref[a])
        for g, a in ((1, 6), (2, 5), (3, 7))
    )
    s_out[...] = s2
    t_s = coarse_operate(s2, s1, s3, t)
    smooth, scalars = windows[5], windows[6]
    lane = iota((64, 128), 1) % 32
    dots = (
        band_sum((coarse_right[...] - step * coarse_image[...]) * s2 + jnp.where(lane == 0, scalars, 0.0)),
        band_sum((2.0 * smooth + t_s) * s2 + jnp.where(lane == 1, scalars, 0.0)),
        band_sum(coarse_image[...] * s2 + jnp.where(lane == 2, scalars, 0.0)),
    )
    lane = iota((8, 128), 1)
    res = jnp.zeros((8, 128), F32)
    for i in range(3):
        res = jnp.where(lane == i, dots[i], res)
    out[...] = res


def finish_kernel(pos, got, scalar, pre, smooth, wet_ref, s_ref, out):
    x, b = pos[1], pos[2]
    sums = got[0]
    for z in range(1, NZ):
        sums = sums + got[z]
    renewed, energy, cross = sums[:, 0:1], sums[:, 1:2], sums[:, 2:3]
    weight, first_energy, step = scalar[:, 0:1], scalar[:, 1:2], scalar[:, 2:3]
    ratio = renewed / weight
    second = renewed / (energy + 2.0 * ratio * cross + ratio * ratio * first_energy)
    own = s_ref[b]
    mains = [spread_rows(own, x, kr) for kr in range(4)]
    mask = wet_ref[...]
    for m in range(M):
        spread = jnp.concatenate([jnp.broadcast_to(v[m : m + 1], (8, 128)) for v in mains], axis=0)
        z1 = smooth[m] + mask * spread
        z0 = pre[m]
        out[m] = step[m : m + 1] * z0 + second[m : m + 1] * (z1 + ratio[m : m + 1] * z0)


def shift(value, axes, count, by):
    return lax.ppermute(value, axes, [(i, (i + by) % count) for i in range(count)])


def to_all(value, axes, count):
    return lax.all_to_all(jnp.broadcast_to(value[None], (count,) + value.shape), axes, 0, 0)


def body(right_side, diagonal, east_face, north_face, wet, active, coupling, pivots):
    z, x = lax.axis_index("z"), lax.axis_index("x")
    b = 2 * lax.axis_index("y") + lax.axis_index("c")
    pos = jnp.stack([z, x, b, b]).astype(jnp.int32)
    mask = wet.astype(F32)
    act = jnp.tile(active[0].astype(F32), (1, 4))
    run = functools.partial(call)

    (coarse,) = run(coarse_kernel, [(8, 128)], pos, right_side, mask, act)
    own = jnp.transpose(coupling[0, 0], (1, 0, 2)).reshape(32, 96)
    own = jnp.roll(jnp.pad(own, ((0, 0), (0, 32))), 32 * (x - 1), axis=1)
    window = [own if g == 2 else shift(own, "z", NZ, 2 - g) for g in range(NG)]
    pivot_rows = [pivots[0] if g == 2 else shift(pivots[0], "z", NZ, 2 - g) for g in range(NG)]
    plane = to_all(jnp.concatenate(window + [coarse], axis=0), ("x", "y"), NX * 4)
    blocks = to_all(plane, "c", 2).reshape(32, 168, 128)

    stack = jnp.concatenate([right_side, jnp.stack([diagonal, east_face, north_face, mask])], axis=0)
    south = shift(stack[:, ROWS - HALO :], ("y", "c"), NB, 1)
    north = shift(stack[:, :HALO], ("y", "c"), NB, -1)
    gap = jnp.zeros((8, EXT_ROWS - ROWS - 2 * HALO, COLS), F32)
    tall = jnp.concatenate([stack, north, gap, south], axis=1)
    west = shift(tall[:, :, COLS - HALO :], ("z", "x"), NZ * NX, 1)
    east = shift(tall[:, :, :HALO], ("z", "x"), NZ * NX, -1)
    gap = jnp.zeros((8, EXT_ROWS, EXT_COLS - COLS - 2 * HALO), F32)
    ext = jnp.concatenate([tall, east, gap, west], axis=2)

    swept, coarse_right = run(forward_kernel, [(24, 128), (64, 128)], pos, blocks, act)
    got = to_all(swept, "z", NZ)
    consts, early = run(fields_kernel, [(7, EXT_ROWS, EXT_COLS), (3, 8, 128)], pos, ext, act)
    (message,) = run(pivot_kernel, [(8, 256)], pos, got, early, *pivot_rows)
    got = to_all(message, ("x", "y", "c"), 32).reshape(256, 256)
    swept, s0, coarse_image, t = run(
        middle_kernel, [(24, 128), (3, 64, 128), (64, 128), (8, 64, 128)], pos, got, blocks, coarse_right
    )
    got = to_all(swept, "z", NZ)
    pre, image = run(
        image_kernel, [(M, ROWS, COLS), (M, EXT_ROWS, EXT_COLS)], pos, ext, consts, s0.reshape(3, NB, 8, 128)
    )
    message, smooth, scalar = run(
        step_kernel, [(8, 256), (M, ROWS, COLS), (8, 128)], pos, got, ext, consts, image, *pivot_rows
    )
    got = to_all(message, ("x", "y", "c"), 32).reshape(256, 256)
    dots, s1 = run(last_kernel, [(8, 128), (64, 128)], pos, got, blocks, s0, coarse_right, coarse_image, t, scalar)
    got = to_all(dots, "z", NZ)
    (out,) = run(
        finish_kernel, [(M, ROWS, COLS)], pos, got, scalar, pre, smooth, mask, s1.reshape(NB, 8, 128)
    )
    return out


def solution(mesh):
    fine = Mesh(mesh.devices.reshape(NZ, NX, 4, 2), ("z", "x", "y", "c"))
    lat, lon = ("y", "c"), ("z", "x")
    in_specs = (
        P(None, lat, lon),
        P(lat, lon),
        P(lat, lon),
        P(lat, lon),
        P(lat, lon),
        P(lat, lon, None),
        P(lat, lon, None, None, None),
        P(lat, lon, None),
    )
    return jax.shard_map(body, mesh=fine, in_specs=in_specs, out_specs=P(None, lat, lon), check_vma=False)
```

```python
import jax
import jax.numpy as jnp
from jax import lax
from jax.experimental import pallas as pl
from jax.experimental.pallas import tpu as pltpu
from jax.sharding import Mesh
from jax.sharding import PartitionSpec as P

F32 = jnp.float32
BF16 = jnp.bfloat16
M = 4
NB = 8
NX = 4
NZ = 16
NG = 5
ROWS = 32
COLS = 128
HALO = 3
EXT_ROWS = 40
EXT_COLS = 256
NT = (((1,), (1,)), ((), ()))
NN = (((1,), (0,)), ((), ()))
VMEM_BYTES = 12 * 1024 * 1024


def call(kernel, outs, pos, *arrays):
    outs = [o if o[1] == BF16 else (o, F32) for o in outs]
    vmem = pl.BlockSpec(memory_space=pltpu.VMEM)
    return pl.pallas_call(
        kernel,
        out_shape=[jax.ShapeDtypeStruct(s, d) for s, d in outs],
        in_specs=[pl.BlockSpec(memory_space=pltpu.SMEM)] + [vmem] * len(arrays),
        out_specs=[vmem] * len(outs),
        compiler_params=pltpu.CompilerParams(vmem_limit_bytes=VMEM_BYTES),
    )(pos, *arrays)


def iota(shape, dim):
    return lax.broadcasted_iota(jnp.int32, shape, dim)


def roll(value, shift, axis):
    shift = shift % value.shape[axis]
    return value if shift == 0 else pltpu.roll(value, shift, axis)


def mm(a, b, dims):
    return lax.dot_general(a, b, dims, preferred_element_type=F32)


def halves(value):
    hi = value.astype(BF16)
    return hi, (value - hi.astype(F32)).astype(BF16)


def dot3(a, b_hi, b_lo, dims):
    hi = a.astype(BF16).astype(F32)
    both = jnp.concatenate([hi, a - hi], axis=0).astype(BF16)
    n = a.shape[0]
    top = mm(both, b_hi, dims)
    low = mm(both, b_lo, dims)
    return top[:n] + top[n:] + low[:n]


def dot_exact(a, b):
    hi = a.astype(BF16).astype(F32)
    rest = a - hi
    mid = rest.astype(BF16).astype(F32)
    parts = jnp.concatenate([hi, mid, rest - mid], axis=0).astype(BF16)
    out = mm(parts, b, NN)
    n = a.shape[0]
    return out[:n] + out[n : 2 * n] + out[2 * n :]


def lane_group():
    return iota((8, 128), 1) // 32


def pick(values):
    group = lane_group()
    out = values[-1]
    for i in range(len(values) - 2, -1, -1):
        out = jnp.where(group == i, values[i], out)
    return out


def block_sums(fields):
    rows = [jnp.sum(f.reshape(4, 8, COLS), axis=1) for f in fields]
    stacked = jnp.concatenate(rows, axis=0)
    pad = -stacked.shape[0] % 16
    if pad:
        stacked = jnp.concatenate([stacked, jnp.zeros((pad, COLS), F32)], axis=0)
    gather = (iota((COLS, COLS), 0) // 16 == iota((COLS, COLS), 1) % 8).astype(F32).astype(BF16)
    sums = dot_exact(stacked, gather)
    kr = (iota((1, COLS), 1) // 8) % 4
    out = []
    for i in range(len(fields)):
        row = jnp.zeros((1, COLS), F32)
        for j in range(4):
            row = jnp.where(kr == j, sums[4 * i + j : 4 * i + j + 1], row)
        out.append(row)
    return out


def member_rows(rows):
    sub = iota((8, 128), 0)
    out = jnp.zeros((8, 128), F32)
    for m, row in enumerate(rows):
        out = jnp.where(sub == m, row, out)
    return out


def full_sum(value):
    return jnp.sum(jnp.sum(value, axis=1, keepdims=True), axis=0, keepdims=True)


def operate(v, fields):
    fe, fw, fn, fs, centre = fields
    return (
        centre * v
        + fe * (v - roll(v, -1, 1))
        + fw * (v - roll(v, 1, 1))
        + fn * (v - roll(v, -1, 0))
        + fs * (v - roll(v, 1, 0))
    )


def main(value):
    return value[:ROWS, :COLS]


def start_kernel(pos, right, diag, east, north, wet, active, coupling, stack, act_out, tile, coarse):
    mask = wet[...].astype(F32)
    act = jnp.concatenate([jnp.broadcast_to(active[...].astype(F32), (8, 32))] * 4, axis=1)
    act_out[...] = act
    fields = [right[m] for m in range(M)] + [diag[...], east[...], north[...], mask]
    for f, v in enumerate(fields):
        stack[f] = v
    tail = jnp.concatenate([coupling[e, 24:, :] for e in range(3)], axis=0)
    tile[:24, :] = jnp.concatenate([coupling[e, :24, :] for e in range(3)] + [tail], axis=1)
    every = jnp.concatenate(fields, axis=0)
    hi = every.astype(BF16).astype(F32)
    mid = (every - hi).astype(BF16).astype(F32)
    parts = jnp.concatenate([hi, mid, every - hi - mid], axis=0).astype(BF16)
    row, lane = iota((16, COLS), 0), iota((16, COLS), 1)
    column = jnp.where(row < 8, row, row - 8 + COLS - HALO)
    chosen = jnp.logical_and(lane == column, row % 8 < HALO).astype(F32).astype(BF16)
    columns = mm(chosen, parts, NT)
    columns = columns[:, :256] + columns[:, 256:512] + columns[:, 512:]
    upper = iota((8, 128), 0) >= 4
    for i in range(2):
        part = columns[8 * i : 8 * i + 8]
        tile[24 + 8 * i : 32 + 8 * i, :] = jnp.where(upper, roll(part[:, 128:], 4, 0), part[:, :128])
    rows = block_sums([fields[m] * mask for m in range(M)])
    coarse[...] = jnp.where(lane_group() == pos[1], member_rows(rows) * act, 0.0)


def gather_kernel(pos, t0, t1, t2, t3, t4, coarse, out):
    x = pos[1]
    onward = jnp.where(x == NX - 1, t1[32:40, :], t2[32:40, :])
    back = jnp.where(x == 0, t3[24:32, :], t2[24:32, :])
    tiles = [t[:24, :] for t in (t0, t1, t2, t3, t4)]
    rows = jnp.concatenate(tiles + [coarse[...]], axis=0)
    for d in range(NX * 4):
        out[d, :128, :] = rows
        out[d, 128:, :] = jnp.where(lax.rem(x + 1, NX) == d // 4, onward, back)


def side(blocks, band, sender):
    return blocks[lax.rem(band, 2) * 16 + sender * 4 + lax.div(band, 2), 128:136, :]


def fields_kernel(pos, stack, north_rows, south_rows, blocks, act, ext, consts, early):
    x, b = pos[1], pos[2]
    after, before = lax.rem(x + 1, NX), lax.rem(x + NX - 1, NX)
    sides = []
    for band in (b, lax.rem(b + 1, NB), lax.rem(b + NB - 1, NB)):
        sides += [side(blocks, band, after), side(blocks, band, before)]
    turned = jnp.transpose(jnp.concatenate(sides + [jnp.zeros((80, 128), F32)], axis=0))
    first = iota((8, 128), 0) < 4

    def columns(rows, slot, h):
        lane = iota(rows.shape, 1)
        east_part = roll(rows, -(16 * slot + 4 * h), 1)
        west_part = roll(rows, 128 - HALO - (16 * slot + 8 + 4 * h), 1)
        return jnp.where(lane < HALO, east_part, jnp.where(lane >= 128 - HALO, west_part, 0.0))

    fields = []
    for f in range(8):
        rows = turned[32 * (f % 4) : 32 * (f % 4) + 32]
        h = f // 4
        corner = jnp.where(first, columns(rows[:8], 1, h), columns(rows[24:], 2, h))
        left = jnp.concatenate([stack[f], jnp.where(first, north_rows[f], south_rows[f])], axis=0)
        right = jnp.concatenate([columns(rows, 0, h), corner], axis=0)
        fields.append(jnp.concatenate([left, right], axis=1))
    for m in range(M):
        ext[m] = fields[m]
    diag, east, north, wet = fields[4:]
    row = iota((EXT_ROWS, EXT_COLS), 0)
    grid_row = b * ROWS + jnp.where(row >= 36, row - EXT_ROWS, row)
    inside = jnp.logical_and(grid_row >= 0, grid_row < NB * ROWS - 1)
    fe = east * wet * roll(wet, -1, 1)
    fw = roll(fe, 1, 1)
    fn = jnp.where(inside, north * wet * roll(wet, -1, 0), 0.0)
    fs = roll(fn, 1, 0)
    own = wet * diag
    centre = own + (1.0 - wet)
    inverse = 1.0 / (centre + fe + fw + fn + fs)
    for i, v in enumerate((fe, fw, fn, fs, centre, inverse, wet)):
        consts[i] = v
    mask = main(wet)
    row = iota((ROWS, COLS), 0)
    col = iota((ROWS, COLS), 1)
    sums = [
        jnp.where(col % 16 == 15, main(fe), 0.0),
        jnp.where(col % 16 == 0, main(fw), 0.0),
        jnp.where(row % 8 == 7, main(fn), 0.0),
        jnp.where(row % 8 == 0, main(fs), 0.0),
        main(own),
    ]
    energy, smooth = [], []
    for m in range(M):
        r = fields[m]
        y = inverse * r
        image = main(operate(y, (fe, fw, fn, fs, centre)))
        sums.append(mask * image)
        energy.append(full_sum(main(y) * image))
        smooth.append(full_sum(main(y) * main(r)))
    rows = block_sums(sums)
    lane = iota((8, 128), 1) % 32
    scalars = jnp.where(lane == 0, member_rows(energy), jnp.where(lane == 1, member_rows(smooth), 0.0))
    early[0] = pick([member_rows(rows[5:])] * 2 + [jnp.broadcast_to(rows[0], (8, 128)), jnp.broadcast_to(rows[1], (8, 128))])
    early[1] = pick([jnp.broadcast_to(rows[i], (8, 128)) for i in (2, 3, 4)] + [act[...]])
    early[2] = scalars


def unpack_tile(tile, x):
    group = iota((24, 128), 1) // 32
    top = roll(jnp.where(group < 3, tile, 0.0), 32 * (x - 1), 1)
    group = lane_group()
    rest = jnp.zeros((8, 128), F32)
    for e in range(3):
        to = (e + x - 1) % 4
        rest = jnp.where(group == to, roll(tile[8 * e : 8 * e + 8], 32 * (to - 3), 1), rest)
    return jnp.concatenate([top, rest], axis=0)


def unpack_weights(blocks, b, g):
    c, y = b % 2, b // 2
    tiles = [unpack_tile(blocks[c * 16 + x * 4 + y, 24 * g : 24 * g + 24, :], x) for x in range(NX)]
    return halves(jnp.concatenate(tiles, axis=0))


def forward_sweep(coarse, weights, mine):
    group = lane_group()
    zero = jnp.zeros((8, 128), F32)
    s = [zero, zero, coarse[0], zero, zero]
    out = s
    for b in range(1, NB):
        new = []
        for g in range(NG):
            left = s[g - 1] if g > 0 else zero
            right = s[g + 1] if g < NG - 1 else zero
            lhs = jnp.concatenate(
                [jnp.where(group == 3, left, s[g]), s[g], s[g], jnp.where(group == 0, right, s[g])], axis=0
            )
            hi, lo = weights(b, g)
            o = dot3(lhs, hi, lo, NT)
            carried = pick([o[8 * x : 8 * x + 8] for x in range(NX)])
            new.append(coarse[b] - carried if g == 2 else -carried)
        s = new
        out = [jnp.where(mine == b, s[g], out[g]) for g in range(NG)]
    return out


def backward_sweep(pivoted, weights):
    group = lane_group()
    zero = jnp.zeros((8, 128), F32)
    s = pivoted[NB - 1]
    out = [None] * NB
    out[NB - 1] = s
    for b in range(NB - 2, -1, -1):
        o = []
        for g in range(NG):
            lhs = jnp.concatenate([jnp.where(group == x, s[g], 0.0) for x in range(NX)], axis=0)
            hi, lo = weights(b + 1, g)
            o.append(dot3(lhs, hi, lo, NN))
        s = []
        for g in range(NG):
            own = o[g][8:16] + o[g][16:24]
            own = own + jnp.where(group == 3, 0.0, o[g][0:8]) + jnp.where(group == 0, 0.0, o[g][24:32])
            after = o[g + 1][0:8] if g < NG - 1 else zero
            before = o[g - 1][24:32] if g > 0 else zero
            own = own + jnp.where(group == 3, after, 0.0) + jnp.where(group == 0, before, 0.0)
            s.append(pivoted[b][g] - own)
        out[b] = s
    return out


def pack_window(s, extra, out):
    parts = [jnp.where(lane_group() == 0, extra, s[0])] + list(s[1:])
    for g in range(NG):
        rows = parts[g][:4]
        for z in range(NZ):
            out[z, g] = rows


def to_plane(first, second, out):
    rows = out.shape[1]
    for i in range(NX * NB):
        out[i, :, :128] = first[:rows]
        out[i, :, 128:] = second[:rows]


def unpack_swept(got):
    reached = iota((4, 128), 1) >= 32
    out = []
    for z in range(NZ):
        acc = jnp.where(reached, got[(z + 2) % NZ, 0], 0.0)
        for g in range(1, NG):
            acc = acc + got[(z + 2 - g) % NZ, g]
        out.append(acc)
    out = jnp.concatenate(out, axis=1)
    return jnp.concatenate([out, jnp.zeros_like(out)], axis=0)


def pivot_product(swept, pivots):
    rows = jnp.concatenate([p[...] for p in pivots], axis=0)
    hi, lo = halves(rows)
    out = dot3(swept, hi, lo, NT)
    return out[:, :128], jnp.concatenate([out[:, 128:160]] * 4, axis=1)


def unpack_plane(got, field):
    group = iota((64, 128), 1) // 32
    half = field // 4 * 128
    out = None
    for x in range(NX):
        bands = [got[x * NB + b, :, half : half + 128] for b in range(NB)]
        if got.shape[1] == 4:
            bands = [jnp.concatenate([v, jnp.zeros_like(v)], axis=0) for v in bands]
        piece = roll(jnp.concatenate(bands, axis=0), 32 * (x - field % 4), 1)
        out = piece if out is None else jnp.where(group == x, piece, out)
    return out


def coarse_operate(s, before, after, t):
    fe, fw, fn, fs, dg = t
    lane = iota((64, 128), 1)
    kc, kr = lane % 8, (lane // 8) % 4
    east = jnp.where(kc < 7, roll(s, -1, 1), jnp.where(lane < 96, roll(s, -25, 1), roll(after, -25, 1)))
    west = jnp.where(kc > 0, roll(s, 1, 1), jnp.where(lane >= 32, roll(s, 25, 1), roll(before, 25, 1)))
    north = jnp.where(kr < 3, roll(s, -8, 1), roll(roll(s, 24, 1), -8, 0))
    south = jnp.where(kr > 0, roll(s, 8, 1), roll(roll(s, -24, 1), 8, 0))
    return dg * s + fe * (s - east) + fw * (s - west) + fn * (s - north) + fs * (s - south)


def band_sum(value):
    acc = value[0:8]
    for b in range(1, NB):
        acc = acc + value[8 * b : 8 * b + 8]
    return jnp.sum(acc, axis=1, keepdims=True)


def stored(w_hi, w_lo):
    return lambda b, g: (w_hi[b * NG + g], w_lo[b * NG + g])


def forward_kernel(pos, blocks, act, out, coarse_out, w_hi, w_lo):
    coarse = []
    for b in range(NB):
        c, y = b % 2, b // 2
        acc = blocks[c * 16 + y, 120:128, :]
        for x in range(1, NX):
            acc = acc + blocks[c * 16 + x * 4 + y, 120:128, :]
        coarse.append(acc)
        coarse_out[8 * b : 8 * b + 8, :] = acc

    def weights(b, g):
        hi, lo = unpack_weights(blocks, b, g)
        w_hi[b * NG + g] = hi
        w_lo[b * NG + g] = lo
        return hi, lo

    s = forward_sweep(coarse, weights, pos[2])
    pack_window(s, act[...], out)


def pivot_kernel(pos, got, early, p0, p1, p2, p3, p4, out):
    z = pos[0]
    first, last = pivot_product(unpack_swept(got), (p0, p1, p2, p3, p4))
    act_before, act_after = (
        jnp.broadcast_to(got[lax.rem(z + by, NZ), 0][:1], (8, 128)) for by in (NZ - 1, 1)
    )
    group = lane_group()
    upper = iota((8, 128), 0) >= 4
    second = jnp.where(group == 0, last, early[0])
    fourth = pick([act_before, roll(act_after, 32, 1), early[2], jnp.zeros((8, 128), F32)])
    to_plane(jnp.where(upper, roll(early[1], 4, 0), first), jnp.where(upper, roll(fourth, 4, 0), second), out)


def upper_half(value):
    return roll(value, -4, 0)


def middle_kernel(pos, got, w_hi, w_lo, coarse_right, out, s_out, coarse_image_out, t_out):
    windows = [unpack_plane(got, f) for f in range(8)]
    pivoted = [[windows[g][8 * b : 8 * b + 8] for g in range(NG)] for b in range(NB)]
    settled = backward_sweep(pivoted, stored(w_hi, w_lo))
    act = upper_half(windows[3])
    s1, s2, s3 = (
        jnp.concatenate([settled[b][g] for b in range(NB)], axis=0) * a
        for g, a in ((1, upper_half(windows[4])), (2, act), (3, upper_half(windows[5])))
    )
    t = (windows[6], windows[7], upper_half(windows[0]), upper_half(windows[1]), upper_half(windows[2]))
    t_s = coarse_operate(s2, s1, s3, t)
    smooth = windows[5]
    coarse_image = act * (smooth + t_s)
    scalars = upper_half(windows[6])
    lane = iota((64, 128), 1) % 32
    c_r = coarse_right[...]
    weight = band_sum(c_r * s2 + jnp.where(lane == 1, scalars, 0.0))
    energy = band_sum((2.0 * smooth + t_s) * s2 + jnp.where(lane == 0, scalars, 0.0))
    lane8 = iota((8, 128), 1)
    extra = jnp.where(lane8 == 0, weight, jnp.where(lane8 == 1, energy, 0.0))
    for i, v in enumerate((s1, s2, s3)):
        s_out[i] = v
    coarse_image_out[...] = coarse_image
    for i, v in enumerate(t + (act, windows[4], windows[5])):
        t_out[i] = v
    t_out[6] = upper_half(windows[4])
    t_out[7] = upper_half(windows[5])
    s = forward_sweep([coarse_image[8 * b : 8 * b + 8] for b in range(NB)], stored(w_hi, w_lo), pos[2])
    pack_window(s, extra, out)


def spread_rows(s, x, kr):
    lane = iota((8, 128), 1)
    return jnp.take_along_axis(s, x * 32 + kr * 8 + lane // 16, axis=1)


def spread_sides(s1, s2, s3, x, kr):
    lane = iota((8, 128), 1)
    east = jnp.take_along_axis(jnp.where(x < 3, s2, s3), jnp.zeros_like(lane) + lax.rem(x + 1, 4) * 32 + kr * 8, axis=1)
    west = jnp.take_along_axis(jnp.where(x > 0, s2, s1), jnp.zeros_like(lane) + lax.rem(x + 3, 4) * 32 + kr * 8 + 7, axis=1)
    return jnp.where(lane < 64, east, west)


def image_kernel(pos, ext, consts, s_ref, pre_out, image_out):
    x, b = pos[1], pos[2]
    north_band, south_band = lax.rem(b + 1, NB), lax.rem(b + NB - 1, NB)
    own = [s_ref[g, b] for g in range(3)]
    up = [s_ref[g, north_band] for g in range(3)]
    down = [s_ref[g, south_band] for g in range(3)]
    mains = [spread_rows(own[1], x, kr) for kr in range(4)]
    sides = [spread_sides(*own, x, kr) for kr in range(4)]
    first = iota((8, 128), 0) < 4
    up_main, up_side = spread_rows(up[1], x, 0), spread_sides(*up, x, 0)
    down_main, down_side = spread_rows(down[1], x, 3), spread_sides(*down, x, 3)
    fields = tuple(consts[i] for i in range(5))
    inverse, wet = consts[5], consts[6]
    for m in range(M):
        wide = lambda v: jnp.broadcast_to(v[m : m + 1], (8, 128))
        left = [wide(v) for v in mains] + [jnp.where(first, wide(up_main), wide(down_main))]
        right = [wide(v) for v in sides] + [jnp.where(first, wide(up_side), wide(down_side))]
        spread = jnp.concatenate([jnp.concatenate(left, axis=0), jnp.concatenate(right, axis=0)], axis=1)
        pre = inverse * ext[m] + wet * spread
        pre_out[m] = main(pre)
        image_out[m] = operate(pre, fields)


def step_kernel(pos, got, ext, consts, image, p0, p1, p2, p3, p4, out, smooth_out, scalar_out):
    first, last = pivot_product(unpack_swept(got), (p0, p1, p2, p3, p4))
    sums = got[0, 0]
    for z in range(1, NZ):
        sums = sums + got[z, 0]
    sums = jnp.concatenate([sums, jnp.ones_like(sums)], axis=0)
    weight, energy = sums[:, 0:1], sums[:, 1:2]
    step = weight / energy
    fields = tuple(consts[i] for i in range(5))
    inverse, wet = consts[5], consts[6]
    mask = main(wet)
    blocks, dots = [], ([], [], [])
    for m in range(M):
        residual = ext[m] - step[m : m + 1] * image[m]
        smooth = inverse * residual
        applied = main(operate(smooth, fields))
        smooth = main(smooth)
        smooth_out[m] = smooth
        blocks.append(mask * applied)
        dots[0].append(full_sum(smooth * main(residual)))
        dots[1].append(full_sum(smooth * applied))
        dots[2].append(full_sum(smooth * main(image[m])))
    rows = member_rows(block_sums(blocks))
    lane = iota((8, 128), 1) % 32
    scalars = jnp.zeros((8, 128), F32)
    for i in range(3):
        scalars = jnp.where(lane == i, member_rows(dots[i]), scalars)
    to_plane(first, pick([last, rows, scalars, jnp.zeros((8, 128), F32)]), out)
    lane = iota((8, 128), 1)
    scalar_out[...] = jnp.where(lane == 0, weight, jnp.where(lane == 1, energy, jnp.where(lane == 2, step, 0.0)))


def last_kernel(pos, got, w_hi, w_lo, s_ref, coarse_right, coarse_image, t_ref, scalar, out, s_out):
    windows = [unpack_plane(got, f) for f in range(7)]
    pivoted = [[windows[g][8 * b : 8 * b + 8] for g in range(NG)] for b in range(NB)]
    settled = backward_sweep(pivoted, stored(w_hi, w_lo))
    t = tuple(t_ref[i] for i in range(5))
    step = jnp.concatenate([scalar[:, 2:3]] * NB, axis=0)
    s1, s2, s3 = (
        s_ref[g - 1] - step * (jnp.concatenate([settled[b][g] for b in range(NB)], axis=0) * t_ref[a])
        for g, a in ((1, 6), (2, 5), (3, 7))
    )
    s_out[...] = s2
    t_s = coarse_operate(s2, s1, s3, t)
    smooth, scalars = windows[5], windows[6]
    lane = iota((64, 128), 1) % 32
    dots = (
        band_sum((coarse_right[...] - step * coarse_image[...]) * s2 + jnp.where(lane == 0, scalars, 0.0)),
        band_sum((2.0 * smooth + t_s) * s2 + jnp.where(lane == 1, scalars, 0.0)),
        band_sum(coarse_image[...] * s2 + jnp.where(lane == 2, scalars, 0.0)),
    )
    lane = iota((8, 128), 1)
    res = jnp.zeros((8, 128), F32)
    for i in range(3):
        res = jnp.where(lane == i, dots[i], res)
    for z in range(NZ):
        out[z] = res[:4]


def finish_kernel(pos, got, scalar, pre, smooth, stack, s_ref, out):
    x, b = pos[1], pos[2]
    sums = got[0]
    for z in range(1, NZ):
        sums = sums + got[z]
    renewed, energy, cross = sums[:, 0:1], sums[:, 1:2], sums[:, 2:3]
    weight, first_energy, step = scalar[:4, 0:1], scalar[:4, 1:2], scalar[:4, 2:3]
    ratio = renewed / weight
    second = renewed / (energy + 2.0 * ratio * cross + ratio * ratio * first_energy)
    own = s_ref[b]
    mains = [spread_rows(own, x, kr) for kr in range(4)]
    mask = stack[7]
    for m in range(M):
        spread = jnp.concatenate([jnp.broadcast_to(v[m : m + 1], (8, 128)) for v in mains], axis=0)
        z1 = smooth[m] + mask * spread
        z0 = pre[m]
        out[m] = step[m : m + 1] * z0 + second[m : m + 1] * (z1 + ratio[m : m + 1] * z0)


def shift(value, axes, count, by):
    return lax.ppermute(value, axes, [(i, (i + by) % count) for i in range(count)])


def to_all(value, axes, count):
    return lax.all_to_all(jnp.broadcast_to(value[None], (count,) + value.shape), axes, 0, 0)


def body(right_side, diagonal, east_face, north_face, wet, active, coupling, pivots):
    z, x = lax.axis_index("z"), lax.axis_index("x")
    b = 2 * lax.axis_index("y") + lax.axis_index("c")
    pos = jnp.stack([z, x, b, b]).astype(jnp.int32)
    stack, act, tile, coarse = call(
        start_kernel,
        [(8, ROWS, COLS), (8, 128), (40, 128), (8, 128)],
        pos, right_side, diagonal, east_face, north_face, wet, active[0], coupling[0, 0],
    )
    window = [tile if g == 2 else shift(tile if g in (1, 3) else tile[:24], "z", NZ, 2 - g) for g in range(NG)]
    (plane,) = call(gather_kernel, [(NX * 4, 136, 128)], pos, *window, coarse)
    plane = lax.all_to_all(plane, ("x", "y"), 0, 0)
    blocks = to_all(plane, "c", 2).reshape(32, 136, 128)

    pivot_rows = [pivots[0] if g == 2 else shift(pivots[0], "z", NZ, 2 - g) for g in range(NG)]
    south = shift(stack[:, ROWS - 8 :], ("y", "c"), NB, 1)
    north = shift(stack[:, :8], ("y", "c"), NB, -1)

    ring, rim = (NZ, NG, 4, 128), (M, EXT_ROWS, EXT_COLS)
    weights = ((NB * NG, 128, 128), BF16)
    ext, consts, early = call(
        fields_kernel, [rim, (7, EXT_ROWS, EXT_COLS), (3, 8, 128)], pos, stack, north, south, blocks, act
    )
    swept, coarse_right, w_hi, w_lo = call(forward_kernel, [ring, (64, 128), weights, weights], pos, blocks, act)
    swept, early, pivot_rows = lax.optimization_barrier((swept, early, pivot_rows))
    got = lax.all_to_all(swept, "z", 0, 0)
    (message,) = call(pivot_kernel, [(32, 8, 256)], pos, got, early, *pivot_rows)
    got = lax.all_to_all(message, ("x", "y", "c"), 0, 0)
    swept, s0, coarse_image, t = call(
        middle_kernel, [ring, (3, 64, 128), (64, 128), (8, 64, 128)], pos, got, w_hi, w_lo, coarse_right
    )
    pre, image = call(image_kernel, [(M, ROWS, COLS), rim], pos, ext, consts, s0.reshape(3, NB, 8, 128))
    swept, pre, image = lax.optimization_barrier((swept, pre, image))
    got = lax.all_to_all(swept, "z", 0, 0)
    message, smooth, scalar = call(
        step_kernel, [(32, 4, 256), (M, ROWS, COLS), (8, 128)], pos, got, ext, consts, image, *pivot_rows
    )
    got = lax.all_to_all(message, ("x", "y", "c"), 0, 0)
    dots, s1 = call(
        last_kernel, [(NZ, 4, 128), (64, 128)], pos, got, w_hi, w_lo, s0, coarse_right, coarse_image, t, scalar
    )
    got = lax.all_to_all(dots, "z", 0, 0)
    (out,) = call(finish_kernel, [(M, ROWS, COLS)], pos, got, scalar, pre, smooth, stack, s1.reshape(NB, 8, 128))
    return out


def solution(mesh):
    fine = Mesh(mesh.devices.reshape(NZ, NX, 4, 2), ("z", "x", "y", "c"))
    lat, lon = ("y", "c"), ("z", "x")
    in_specs = (
        P(None, lat, lon),
        P(lat, lon),
        P(lat, lon),
        P(lat, lon),
        P(lat, lon),
        P(lat, lon, None),
        P(lat, lon, None, None, None),
        P(lat, lon, None),
    )
    return jax.shard_map(body, mesh=fine, in_specs=in_specs, out_specs=P(None, lat, lon), check_vma=False)
```

```python
import jax
import jax.numpy as jnp
from jax import lax
from jax.experimental import pallas as pl
from jax.experimental.pallas import tpu as pltpu
from jax.sharding import Mesh
from jax.sharding import PartitionSpec as P

F32 = jnp.float32
BF16 = jnp.bfloat16
M = 4
NB = 8
NX = 4
NZ = 16
NG = 5
ROWS = 32
COLS = 128
HALO = 3
EXT_ROWS = 40
EXT_COLS = 256
NT = (((1,), (1,)), ((), ()))
NN = (((1,), (0,)), ((), ()))
VMEM_BYTES = 12 * 1024 * 1024


def call(kernel, outs, pos, *arrays, fetch=False):
    outs = [o if o[1] == BF16 else (o, F32) for o in outs]
    vmem = pl.BlockSpec(memory_space=pltpu.VMEM)
    scratch = []
    if fetch:
        scratch = [pltpu.VMEM(a.shape, a.dtype) for a in arrays] + [pltpu.SemaphoreType.DMA((len(arrays),))]
    given = pl.BlockSpec(memory_space=pl.ANY) if fetch else vmem
    return pl.pallas_call(
        kernel,
        out_shape=[jax.ShapeDtypeStruct(s, d) for s, d in outs],
        in_specs=[pl.BlockSpec(memory_space=pltpu.SMEM)] + [given] * len(arrays),
        out_specs=[vmem] * len(outs),
        scratch_shapes=scratch,
        compiler_params=pltpu.CompilerParams(vmem_limit_bytes=VMEM_BYTES),
    )(pos, *arrays)


def iota(shape, dim):
    return lax.broadcasted_iota(jnp.int32, shape, dim)


def roll(value, shift, axis):
    shift = shift % value.shape[axis]
    return value if shift == 0 else pltpu.roll(value, shift, axis)


def mm(a, b, dims):
    return lax.dot_general(a, b, dims, preferred_element_type=F32)


def halves(value):
    hi = value.astype(BF16)
    return hi, (value - hi.astype(F32)).astype(BF16)


def dot3(a, b_hi, b_lo, dims):
    hi = a.astype(BF16).astype(F32)
    both = jnp.concatenate([hi, a - hi], axis=0).astype(BF16)
    n = a.shape[0]
    top = mm(both, b_hi, dims)
    low = mm(both, b_lo, dims)
    return top[:n] + top[n:] + low[:n]


def dot_exact(a, b):
    hi = a.astype(BF16).astype(F32)
    rest = a - hi
    mid = rest.astype(BF16).astype(F32)
    parts = jnp.concatenate([hi, mid, rest - mid], axis=0).astype(BF16)
    out = mm(parts, b, NN)
    n = a.shape[0]
    return out[:n] + out[n : 2 * n] + out[2 * n :]


def lane_group():
    return iota((8, 128), 1) // 32


def pick(values):
    group = lane_group()
    out = values[-1]
    for i in range(len(values) - 2, -1, -1):
        out = jnp.where(group == i, values[i], out)
    return out


def block_sums(fields):
    rows = [jnp.sum(f.reshape(4, 8, COLS), axis=1) for f in fields]
    stacked = jnp.concatenate(rows, axis=0)
    pad = -stacked.shape[0] % 16
    if pad:
        stacked = jnp.concatenate([stacked, jnp.zeros((pad, COLS), F32)], axis=0)
    gather = (iota((COLS, COLS), 0) // 16 == iota((COLS, COLS), 1) % 8).astype(F32).astype(BF16)
    sums = dot_exact(stacked, gather)
    kr = (iota((1, COLS), 1) // 8) % 4
    out = []
    for i in range(len(fields)):
        row = jnp.zeros((1, COLS), F32)
        for j in range(4):
            row = jnp.where(kr == j, sums[4 * i + j : 4 * i + j + 1], row)
        out.append(row)
    return out


def member_rows(rows):
    sub = iota((8, 128), 0)
    out = jnp.zeros((8, 128), F32)
    for m, row in enumerate(rows):
        out = jnp.where(sub == m, row, out)
    return out


def full_sum(value):
    return jnp.sum(jnp.sum(value, axis=1, keepdims=True), axis=0, keepdims=True)


def operate(v, fields):
    fe, fw, fn, fs, centre = fields
    return (
        centre * v
        + fe * (v - roll(v, -1, 1))
        + fw * (v - roll(v, 1, 1))
        + fn * (v - roll(v, -1, 0))
        + fs * (v - roll(v, 1, 0))
    )


def main(value):
    return value[:ROWS, :COLS]


def start_kernel(pos, *refs):
    given, (stack, tile), held, sems = refs[:7], refs[7:9], refs[9:16], refs[16]
    copies = [pltpu.make_async_copy(a, h, sems.at[i]) for i, (a, h) in enumerate(zip(given, held))]
    for copy in copies:
        copy.start()
    for copy in copies:
        copy.wait()
    right, diag, east, north, wet, active, coupling = held
    mask = wet[...].astype(F32)
    act = jnp.concatenate([jnp.broadcast_to(active[...].astype(F32), (8, 32))] * 4, axis=1)
    fields = [right[m] for m in range(M)] + [diag[...], east[...], north[...], mask]
    for f, v in enumerate(fields):
        stack[f] = v
    tail = jnp.concatenate([coupling[e, 24:, :] for e in range(3)], axis=0)
    tile[:24, :] = jnp.concatenate([coupling[e, :24, :] for e in range(3)] + [tail], axis=1)
    every = jnp.concatenate(fields, axis=0)
    hi = every.astype(BF16).astype(F32)
    mid = (every - hi).astype(BF16).astype(F32)
    parts = jnp.concatenate([hi, mid, every - hi - mid], axis=0).astype(BF16)
    row, lane = iota((16, COLS), 0), iota((16, COLS), 1)
    column = jnp.where(row < 8, row, row - 8 + COLS - HALO)
    chosen = jnp.logical_and(lane == column, row % 8 < HALO).astype(F32).astype(BF16)
    columns = mm(chosen, parts, NT)
    columns = columns[:, :256] + columns[:, 256:512] + columns[:, 512:]
    upper = iota((8, 128), 0) >= 4
    for i in range(2):
        part = columns[8 * i : 8 * i + 8]
        tile[32 + 8 * i : 40 + 8 * i, :] = jnp.where(upper, roll(part[:, 128:], 4, 0), part[:, :128])
    rows = block_sums([fields[m] * mask for m in range(M)])
    packed = pick([jnp.broadcast_to(r, (8, 128)) for r in rows]) * act
    row = iota((8, 128), 0)
    tile[24:32, :] = jnp.where(row == 0, packed, jnp.where(row == 1, act, 0.0))


def gather_kernel(pos, t0, t1, t2, t3, t4, out):
    x = pos[1]
    onward = jnp.where(x == NX - 1, t1[40:48, :], t2[40:48, :])
    back = jnp.where(x == 0, t3[32:40, :], t2[32:40, :])
    tiles = (t0, t1, t2, t3, t4)
    rows = [t[:24, :] for t in tiles] + [t[24:25, :] for t in tiles] + [t[25:26, :] for t in (t1, t2, t3)]
    rows = jnp.concatenate(rows, axis=0)
    for d in range(NX * 4):
        out[d, :128, :] = rows
        out[d, 128:, :] = jnp.where(lax.rem(x + 1, NX) == d // 4, onward, back)


def side(blocks, band, sender):
    return blocks[lax.rem(band, 2) * 16 + sender * 4 + lax.div(band, 2), 128:136, :]


def fields_kernel(pos, stack, north_rows, south_rows, blocks, ext, consts, early):
    x, b = pos[1], pos[2]
    after, before = lax.rem(x + 1, NX), lax.rem(x + NX - 1, NX)
    sides = []
    for band in (b, lax.rem(b + 1, NB), lax.rem(b + NB - 1, NB)):
        sides += [side(blocks, band, after), side(blocks, band, before)]
    turned = jnp.transpose(jnp.concatenate(sides + [jnp.zeros((80, 128), F32)], axis=0))
    first = iota((8, 128), 0) < 4

    def columns(rows, slot, h):
        lane = iota(rows.shape, 1)
        east_part = roll(rows, -(16 * slot + 4 * h), 1)
        west_part = roll(rows, 128 - HALO - (16 * slot + 8 + 4 * h), 1)
        return jnp.where(lane < HALO, east_part, jnp.where(lane >= 128 - HALO, west_part, 0.0))

    fields = []
    for f in range(8):
        rows = turned[32 * (f % 4) : 32 * (f % 4) + 32]
        h = f // 4
        corner = jnp.where(first, columns(rows[:8], 1, h), columns(rows[24:], 2, h))
        left = jnp.concatenate([stack[f], jnp.where(first, north_rows[f], south_rows[f])], axis=0)
        right = jnp.concatenate([columns(rows, 0, h), corner], axis=0)
        fields.append(jnp.concatenate([left, right], axis=1))
    for m in range(M):
        ext[m] = fields[m]
    diag, east, north, wet = fields[4:]
    row = iota((EXT_ROWS, EXT_COLS), 0)
    grid_row = b * ROWS + jnp.where(row >= 36, row - EXT_ROWS, row)
    inside = jnp.logical_and(grid_row >= 0, grid_row < NB * ROWS - 1)
    fe = east * wet * roll(wet, -1, 1)
    fw = roll(fe, 1, 1)
    fn = jnp.where(inside, north * wet * roll(wet, -1, 0), 0.0)
    fs = roll(fn, 1, 0)
    own = wet * diag
    centre = own + (1.0 - wet)
    inverse = 1.0 / (centre + fe + fw + fn + fs)
    for i, v in enumerate((fe, fw, fn, fs, centre, inverse, wet)):
        consts[i] = v
    mask = main(wet)
    row = iota((ROWS, COLS), 0)
    col = iota((ROWS, COLS), 1)
    sums = [
        jnp.where(col % 16 == 15, main(fe), 0.0),
        jnp.where(col % 16 == 0, main(fw), 0.0),
        jnp.where(row % 8 == 7, main(fn), 0.0),
        jnp.where(row % 8 == 0, main(fs), 0.0),
        main(own),
    ]
    energy, smooth = [], []
    for m in range(M):
        r = fields[m]
        y = inverse * r
        image = main(operate(y, (fe, fw, fn, fs, centre)))
        sums.append(mask * image)
        energy.append(full_sum(main(y) * image))
        smooth.append(full_sum(main(y) * main(r)))
    rows = block_sums(sums)
    lane = iota((8, 128), 1) % 32
    scalars = jnp.where(lane == 0, member_rows(energy), jnp.where(lane == 1, member_rows(smooth), 0.0))
    early[0] = pick([member_rows(rows[5:])] * 2 + [jnp.broadcast_to(rows[0], (8, 128)), jnp.broadcast_to(rows[1], (8, 128))])
    early[1] = pick([jnp.broadcast_to(rows[i], (8, 128)) for i in (2, 3, 4)] + [scalars])


def unpack_tile(tile, x):
    group = iota((24, 128), 1) // 32
    top = roll(jnp.where(group < 3, tile, 0.0), 32 * (x - 1), 1)
    group = lane_group()
    rest = jnp.zeros((8, 128), F32)
    for e in range(3):
        to = (e + x - 1) % 4
        rest = jnp.where(group == to, roll(tile[8 * e : 8 * e + 8], 32 * (to - 3), 1), rest)
    return jnp.concatenate([top, rest], axis=0)


def unpack_weights(blocks, b, g):
    c, y = b % 2, b // 2
    tiles = [unpack_tile(blocks[c * 16 + x * 4 + y, 24 * g : 24 * g + 24, :], x) for x in range(NX)]
    return halves(jnp.concatenate(tiles, axis=0))


def forward_sweep(coarse, weights, mine):
    group = lane_group()
    zero = jnp.zeros((8, 128), F32)
    s = [zero if v is None else v for v in coarse[0]]
    out = s
    for b in range(1, NB):
        new = []
        for g in range(NG):
            left = s[g - 1] if g > 0 else zero
            right = s[g + 1] if g < NG - 1 else zero
            lhs = jnp.concatenate(
                [jnp.where(group == 3, left, s[g]), s[g], s[g], jnp.where(group == 0, right, s[g])], axis=0
            )
            hi, lo = weights(b, g)
            o = dot3(lhs, hi, lo, NT)
            carried = pick([o[8 * x : 8 * x + 8] for x in range(NX)])
            new.append(-carried if coarse[b][g] is None else coarse[b][g] - carried)
        s = new
        out = [jnp.where(mine == b, s[g], out[g]) for g in range(NG)]
    return out


def backward_sweep(pivoted, weights):
    group = lane_group()
    zero = jnp.zeros((8, 128), F32)
    s = pivoted[NB - 1]
    out = [None] * NB
    out[NB - 1] = s
    for b in range(NB - 2, -1, -1):
        o = []
        for g in range(NG):
            lhs = jnp.concatenate([jnp.where(group == x, s[g], 0.0) for x in range(NX)], axis=0)
            hi, lo = weights(b + 1, g)
            o.append(dot3(lhs, hi, lo, NN))
        s = []
        for g in range(NG):
            own = o[g][8:16] + o[g][16:24]
            own = own + jnp.where(group == 3, 0.0, o[g][0:8]) + jnp.where(group == 0, 0.0, o[g][24:32])
            after = o[g + 1][0:8] if g < NG - 1 else zero
            before = o[g - 1][24:32] if g > 0 else zero
            own = own + jnp.where(group == 3, after, 0.0) + jnp.where(group == 0, before, 0.0)
            s.append(pivoted[b][g] - own)
        out[b] = s
    return out


def pack_window(s, extra, out):
    parts = [jnp.where(lane_group() == 0, extra, s[0])] + list(s[1:])
    for g in range(NG):
        rows = parts[g][:4]
        for z in range(NZ):
            out[z, g] = rows


def to_plane(values, out):
    for d in range(NX * NB):
        for i, v in enumerate(values):
            out[d, :, 128 * i : 128 * i + 128] = v[:4]


def unpack_swept(got):
    if len(got.shape) == 3:
        out = [got[z] for z in range(NZ)]
    else:
        reached = iota((4, 128), 1) >= 32
        out = []
        for z in range(NZ):
            acc = jnp.where(reached, got[(z + 2) % NZ, 0], 0.0)
            for g in range(1, NG):
                acc = acc + got[(z + 2 - g) % NZ, g]
            out.append(acc)
    out = jnp.concatenate(out, axis=1)
    return jnp.concatenate([out, jnp.zeros_like(out)], axis=0)


def pivot_product(swept, pivots):
    rows = jnp.concatenate([p[...] for p in pivots], axis=0)
    hi, lo = halves(rows)
    out = dot3(swept, hi, lo, NT)
    return out[:, :128], jnp.concatenate([out[:, 128:160]] * 4, axis=1)


def unpack_plane(got, field):
    group = iota((64, 128), 1) // 32
    half = field // 4 * 128
    out = None
    for x in range(NX):
        bands = [got[x * NB + b, :, half : half + 128] for b in range(NB)]
        bands = [jnp.concatenate([v, jnp.zeros_like(v)], axis=0) for v in bands]
        piece = roll(jnp.concatenate(bands, axis=0), 32 * (x - field % 4), 1)
        out = piece if out is None else jnp.where(group == x, piece, out)
    return out


def coarse_operate(s, before, after, t):
    fe, fw, fn, fs, dg = t
    lane = iota((64, 128), 1)
    kc, kr = lane % 8, (lane // 8) % 4
    east = jnp.where(kc < 7, roll(s, -1, 1), jnp.where(lane < 96, roll(s, -25, 1), roll(after, -25, 1)))
    west = jnp.where(kc > 0, roll(s, 1, 1), jnp.where(lane >= 32, roll(s, 25, 1), roll(before, 25, 1)))
    north = jnp.where(kr < 3, roll(s, -8, 1), roll(roll(s, 24, 1), -8, 0))
    south = jnp.where(kr > 0, roll(s, 8, 1), roll(roll(s, -24, 1), 8, 0))
    return dg * s + fe * (s - east) + fw * (s - west) + fn * (s - north) + fs * (s - south)


def band_sum(value):
    acc = value[0:8]
    for b in range(1, NB):
        acc = acc + value[8 * b : 8 * b + 8]
    return jnp.sum(acc, axis=1, keepdims=True)


def stored(w_hi, w_lo):
    return lambda b, g: (w_hi[b * NG + g], w_lo[b * NG + g])


def plane_rows(blocks, at):
    return [
        jnp.concatenate([blocks[b % 2 * 16 + x * 4 + b // 2, at : at + 1, :] for b in range(NB)], axis=0) for x in range(NX)
    ]


def forward_kernel(pos, blocks, out, coarse_out, acts_out, w_hi, w_lo):
    coarse = [[] for _ in range(NB)]
    for g in range(NG):
        rows = plane_rows(blocks, 120 + g)
        members = [pick([roll(rows[x], 32 * (x - m), 1) for x in range(NX)]) for m in range(M)]
        for b in range(NB):
            coarse[b].append(member_rows([v[b : b + 1] for v in members]))
    for b in range(NB):
        coarse_out[8 * b : 8 * b + 8, :] = coarse[b][2]
    for i in range(3):
        act = pick(plane_rows(blocks, 125 + i))
        for b in range(NB):
            acts_out[i, 8 * b : 8 * b + 8, :] = jnp.broadcast_to(act[b : b + 1], (8, 128))

    def weights(b, g):
        hi, lo = unpack_weights(blocks, b, g)
        w_hi[b * NG + g] = hi
        w_lo[b * NG + g] = lo
        return hi, lo

    own = forward_sweep(coarse, weights, pos[2])[2][:4]
    for z in range(NZ):
        out[z] = own


def pivot_kernel(pos, got, early, p0, p1, p2, p3, p4, out):
    first, last = pivot_product(unpack_swept(got), (p0, p1, p2, p3, p4))
    to_plane([first, jnp.where(lane_group() == 0, last, early[0]), early[1]], out)


def middle_kernel(pos, got, w_hi, w_lo, coarse_right, acts, out, s_out, coarse_image_out, t_out):
    windows = [unpack_plane(got, f) for f in range(12)]
    pivoted = [[windows[g][8 * b : 8 * b + 8] for g in range(NG)] for b in range(NB)]
    settled = backward_sweep(pivoted, stored(w_hi, w_lo))
    s1, s2, s3 = (
        jnp.concatenate([settled[b][g] for b in range(NB)], axis=0) * acts[g - 1] for g in (1, 2, 3)
    )
    smooth, t, scalars = windows[5], windows[6:11], windows[11]
    t_s = coarse_operate(s2, s1, s3, t)
    coarse_image = acts[1] * (smooth + t_s)
    lane = iota((64, 128), 1) % 32
    weight = band_sum(coarse_right[...] * s2 + jnp.where(lane == 1, scalars, 0.0))
    energy = band_sum((2.0 * smooth + t_s) * s2 + jnp.where(lane == 0, scalars, 0.0))
    lane = iota((8, 128), 1)
    extra = jnp.where(lane == 0, weight, jnp.where(lane == 1, energy, 0.0))
    for i, v in enumerate((s1, s2, s3)):
        s_out[i] = v
    coarse_image_out[...] = coarse_image
    for i, v in enumerate(t):
        t_out[i] = v
    coarse = [[None, None, coarse_image[8 * b : 8 * b + 8], None, None] for b in range(NB)]
    pack_window(forward_sweep(coarse, stored(w_hi, w_lo), pos[2]), extra, out)


def spread_rows(s, x, kr):
    lane = iota((8, 128), 1)
    return jnp.take_along_axis(s, x * 32 + kr * 8 + lane // 16, axis=1)


def spread_sides(s1, s2, s3, x, kr):
    lane = iota((8, 128), 1)
    east = jnp.take_along_axis(jnp.where(x < 3, s2, s3), jnp.zeros_like(lane) + lax.rem(x + 1, 4) * 32 + kr * 8, axis=1)
    west = jnp.take_along_axis(jnp.where(x > 0, s2, s1), jnp.zeros_like(lane) + lax.rem(x + 3, 4) * 32 + kr * 8 + 7, axis=1)
    return jnp.where(lane < 64, east, west)


def image_kernel(pos, ext, consts, s_ref, pre_out, image_out):
    x, b = pos[1], pos[2]
    north_band, south_band = lax.rem(b + 1, NB), lax.rem(b + NB - 1, NB)
    own = [s_ref[g, b] for g in range(3)]
    up = [s_ref[g, north_band] for g in range(3)]
    down = [s_ref[g, south_band] for g in range(3)]
    mains = [spread_rows(own[1], x, kr) for kr in range(4)]
    sides = [spread_sides(*own, x, kr) for kr in range(4)]
    first = iota((8, 128), 0) < 4
    up_main, up_side = spread_rows(up[1], x, 0), spread_sides(*up, x, 0)
    down_main, down_side = spread_rows(down[1], x, 3), spread_sides(*down, x, 3)
    fields = tuple(consts[i] for i in range(5))
    inverse, wet = consts[5], consts[6]
    for m in range(M):
        wide = lambda v: jnp.broadcast_to(v[m : m + 1], (8, 128))
        left = [wide(v) for v in mains] + [jnp.where(first, wide(up_main), wide(down_main))]
        right = [wide(v) for v in sides] + [jnp.where(first, wide(up_side), wide(down_side))]
        spread = jnp.concatenate([jnp.concatenate(left, axis=0), jnp.concatenate(right, axis=0)], axis=1)
        pre = inverse * ext[m] + wet * spread
        pre_out[m] = main(pre)
        image_out[m] = operate(pre, fields)


def step_kernel(pos, got, ext, consts, image, p0, p1, p2, p3, p4, out, smooth_out, scalar_out):
    first, last = pivot_product(unpack_swept(got), (p0, p1, p2, p3, p4))
    sums = got[0, 0]
    for z in range(1, NZ):
        sums = sums + got[z, 0]
    sums = jnp.concatenate([sums, jnp.ones_like(sums)], axis=0)
    weight, energy = sums[:, 0:1], sums[:, 1:2]
    step = weight / energy
    fields = tuple(consts[i] for i in range(5))
    inverse, wet = consts[5], consts[6]
    mask = main(wet)
    blocks, dots = [], ([], [], [])
    for m in range(M):
        residual = ext[m] - step[m : m + 1] * image[m]
        smooth = inverse * residual
        applied = main(operate(smooth, fields))
        smooth = main(smooth)
        smooth_out[m] = smooth
        blocks.append(mask * applied)
        dots[0].append(full_sum(smooth * main(residual)))
        dots[1].append(full_sum(smooth * applied))
        dots[2].append(full_sum(smooth * main(image[m])))
    rows = member_rows(block_sums(blocks))
    lane = iota((8, 128), 1) % 32
    scalars = jnp.zeros((8, 128), F32)
    for i in range(3):
        scalars = jnp.where(lane == i, member_rows(dots[i]), scalars)
    to_plane([first, pick([last, rows, scalars, jnp.zeros((8, 128), F32)])], out)
    lane = iota((8, 128), 1)
    scalar_out[...] = jnp.where(lane == 0, weight, jnp.where(lane == 1, energy, jnp.where(lane == 2, step, 0.0)))


def last_kernel(pos, got, w_hi, w_lo, s_ref, coarse_right, coarse_image, t_ref, acts, scalar, out, s_out):
    windows = [unpack_plane(got, f) for f in range(7)]
    pivoted = [[windows[g][8 * b : 8 * b + 8] for g in range(NG)] for b in range(NB)]
    settled = backward_sweep(pivoted, stored(w_hi, w_lo))
    t = tuple(t_ref[i] for i in range(5))
    step = jnp.concatenate([scalar[:, 2:3]] * NB, axis=0)
    s1, s2, s3 = (
        s_ref[g - 1] - step * (jnp.concatenate([settled[b][g] for b in range(NB)], axis=0) * acts[g - 1])
        for g in (1, 2, 3)
    )
    s_out[...] = s2
    t_s = coarse_operate(s2, s1, s3, t)
    smooth, scalars = windows[5], windows[6]
    lane = iota((64, 128), 1) % 32
    dots = (
        band_sum((coarse_right[...] - step * coarse_image[...]) * s2 + jnp.where(lane == 0, scalars, 0.0)),
        band_sum((2.0 * smooth + t_s) * s2 + jnp.where(lane == 1, scalars, 0.0)),
        band_sum(coarse_image[...] * s2 + jnp.where(lane == 2, scalars, 0.0)),
    )
    lane = iota((8, 128), 1)
    res = jnp.zeros((8, 128), F32)
    for i in range(3):
        res = jnp.where(lane == i, dots[i], res)
    for z in range(NZ):
        out[z] = res[:4]


def finish_kernel(pos, got, scalar, pre, smooth, stack, s_ref, out):
    x, b = pos[1], pos[2]
    sums = got[0]
    for z in range(1, NZ):
        sums = sums + got[z]
    renewed, energy, cross = sums[:, 0:1], sums[:, 1:2], sums[:, 2:3]
    weight, first_energy, step = scalar[:4, 0:1], scalar[:4, 1:2], scalar[:4, 2:3]
    ratio = renewed / weight
    second = renewed / (energy + 2.0 * ratio * cross + ratio * ratio * first_energy)
    own = s_ref[b]
    mains = [spread_rows(own, x, kr) for kr in range(4)]
    mask = stack[7]
    for m in range(M):
        spread = jnp.concatenate([jnp.broadcast_to(v[m : m + 1], (8, 128)) for v in mains], axis=0)
        z1 = smooth[m] + mask * spread
        z0 = pre[m]
        out[m] = step[m : m + 1] * z0 + second[m : m + 1] * (z1 + ratio[m : m + 1] * z0)


def shift(value, axes, count, by):
    return lax.ppermute(value, axes, [(i, (i + by) % count) for i in range(count)])


def to_all(value, axes, count):
    return lax.all_to_all(jnp.broadcast_to(value[None], (count,) + value.shape), axes, 0, 0)


def body(right_side, diagonal, east_face, north_face, wet, active, coupling, pivots):
    z, x = lax.axis_index("z"), lax.axis_index("x")
    b = 2 * lax.axis_index("y") + lax.axis_index("c")
    pos = jnp.stack([z, x, b, b]).astype(jnp.int32)
    stack, tile = call(
        start_kernel,
        [(8, ROWS, COLS), (48, 128)],
        pos, right_side, diagonal, east_face, north_face, wet, active[0], coupling[0, 0],
        fetch=True,
    )
    window = [tile if g == 2 else shift(tile if g in (1, 3) else tile[:32], "z", NZ, 2 - g) for g in range(NG)]
    (plane,) = call(gather_kernel, [(NX * 4, 136, 128)], pos, *window)
    plane = lax.all_to_all(plane, ("x", "y"), 0, 0)
    blocks = to_all(plane, "c", 2).reshape(32, 136, 128)

    pivot_rows = [pivots[0] if g == 2 else shift(pivots[0], "z", NZ, 2 - g) for g in range(NG)]
    south = shift(stack[:, ROWS - 8 :], ("y", "c"), NB, 1)
    north = shift(stack[:, :8], ("y", "c"), NB, -1)

    ring, rim = (NZ, NG, 4, 128), (M, EXT_ROWS, EXT_COLS)
    weights = ((NB * NG, 128, 128), BF16)
    ext, consts, early = call(
        fields_kernel, [rim, (7, EXT_ROWS, EXT_COLS), (2, 8, 128)], pos, stack, north, south, blocks
    )
    swept, coarse_right, acts, w_hi, w_lo = call(
        forward_kernel, [(NZ, 4, 128), (64, 128), (3, 64, 128), weights, weights], pos, blocks
    )
    swept, early, pivot_rows = lax.optimization_barrier((swept, early, pivot_rows))
    got = lax.all_to_all(swept, "z", 0, 0)
    (message,) = call(pivot_kernel, [(32, 4, 384)], pos, got, early, *pivot_rows)
    got = lax.all_to_all(message, ("x", "y", "c"), 0, 0)
    swept, s0, coarse_image, t = call(
        middle_kernel, [ring, (3, 64, 128), (64, 128), (5, 64, 128)], pos, got, w_hi, w_lo, coarse_right, acts
    )
    pre, image = call(image_kernel, [(M, ROWS, COLS), rim], pos, ext, consts, s0.reshape(3, NB, 8, 128))
    swept, pre, image = lax.optimization_barrier((swept, pre, image))
    got = lax.all_to_all(swept, "z", 0, 0)
    message, smooth, scalar = call(
        step_kernel, [(32, 4, 256), (M, ROWS, COLS), (8, 128)], pos, got, ext, consts, image, *pivot_rows
    )
    got = lax.all_to_all(message, ("x", "y", "c"), 0, 0)
    dots, s1 = call(
        last_kernel, [(NZ, 4, 128), (64, 128)], pos, got, w_hi, w_lo, s0, coarse_right, coarse_image, t, acts, scalar
    )
    got = lax.all_to_all(dots, "z", 0, 0)
    (out,) = call(finish_kernel, [(M, ROWS, COLS)], pos, got, scalar, pre, smooth, stack, s1.reshape(NB, 8, 128))
    return out


def solution(mesh):
    fine = Mesh(mesh.devices.reshape(NZ, NX, 4, 2), ("z", "x", "y", "c"))
    lat, lon = ("y", "c"), ("z", "x")
    in_specs = (
        P(None, lat, lon),
        P(lat, lon),
        P(lat, lon),
        P(lat, lon),
        P(lat, lon),
        P(lat, lon, None),
        P(lat, lon, None, None, None),
        P(lat, lon, None),
    )
    return jax.shard_map(body, mesh=fine, in_specs=in_specs, out_specs=P(None, lat, lon), check_vma=False)
```

```python
import jax
import jax.numpy as jnp
from jax import lax
from jax.experimental import pallas as pl
from jax.experimental.pallas import tpu as pltpu
from jax.sharding import Mesh
from jax.sharding import PartitionSpec as P

F32 = jnp.float32
BF16 = jnp.bfloat16
M = 4
NB = 8
NX = 4
NZ = 16
NG = 5
ROWS = 32
COLS = 128
HALO = 3
EXT_ROWS = 40
EXT_COLS = 256
NT = (((1,), (1,)), ((), ()))
NN = (((1,), (0,)), ((), ()))
VMEM_BYTES = 12 * 1024 * 1024
FETCH_BYTES = 63 * 1024 * 1024


def call(kernel, outs, *arrays, fetch=(), room=VMEM_BYTES):
    outs = [o if o[1] == BF16 else (o, F32) for o in outs]
    vmem, hbm = pl.BlockSpec(memory_space=pltpu.VMEM), pl.BlockSpec(memory_space=pltpu.HBM)
    n, count = len(arrays), len(fetch)

    def whole(*refs):
        given, rest, held = list(refs[:n]), refs[n : n + len(outs)], refs[n + len(outs) :]
        copies = [pltpu.make_async_copy(given[i], held[j], held[count].at[j]) for j, i in enumerate(fetch)]
        for copy in copies:
            copy.start()
        for copy in copies:
            copy.wait()
        for j, i in enumerate(fetch):
            given[i] = held[j]
        z, x = lax.axis_index("z"), lax.axis_index("x")
        b = 2 * lax.axis_index("y") + lax.axis_index("c")
        kernel((z, x, b), *given, *rest)

    scratch = [pltpu.VMEM(arrays[i].shape, arrays[i].dtype) for i in fetch]
    if fetch:
        scratch.append(pltpu.SemaphoreType.DMA((count,)))
    return pl.pallas_call(
        whole,
        out_shape=[jax.ShapeDtypeStruct(s, d) for s, d in outs],
        in_specs=[hbm if i in fetch else vmem for i in range(n)],
        out_specs=[vmem] * len(outs),
        scratch_shapes=scratch,
        compiler_params=pltpu.CompilerParams(vmem_limit_bytes=room),
    )(*arrays)


def iota(shape, dim):
    return lax.broadcasted_iota(jnp.int32, shape, dim)


def roll(value, shift, axis):
    shift = shift % value.shape[axis]
    return value if shift == 0 else pltpu.roll(value, shift, axis)


def mm(a, b, dims):
    return lax.dot_general(a, b, dims, preferred_element_type=F32)


def halves(value):
    hi = value.astype(BF16)
    return hi, (value - hi.astype(F32)).astype(BF16)


def dot3(a, b_hi, b_lo, dims):
    hi = a.astype(BF16).astype(F32)
    both = jnp.concatenate([hi, a - hi], axis=0).astype(BF16)
    n = a.shape[0]
    top = mm(both, b_hi, dims)
    low = mm(both, b_lo, dims)
    return top[:n] + top[n:] + low[:n]


def dot_exact(a, b):
    hi = a.astype(BF16).astype(F32)
    rest = a - hi
    mid = rest.astype(BF16).astype(F32)
    parts = jnp.concatenate([hi, mid, rest - mid], axis=0).astype(BF16)
    out = mm(parts, b, NN)
    n = a.shape[0]
    return out[:n] + out[n : 2 * n] + out[2 * n :]


def lane_group():
    return iota((8, 128), 1) // 32


def pick(values):
    group = lane_group()
    out = values[-1]
    for i in range(len(values) - 2, -1, -1):
        out = jnp.where(group == i, values[i], out)
    return out


def block_sums(fields):
    rows = [jnp.sum(f.reshape(4, 8, COLS), axis=1) for f in fields]
    stacked = jnp.concatenate(rows, axis=0)
    pad = -stacked.shape[0] % 16
    if pad:
        stacked = jnp.concatenate([stacked, jnp.zeros((pad, COLS), F32)], axis=0)
    gather = (iota((COLS, COLS), 0) // 16 == iota((COLS, COLS), 1) % 8).astype(F32).astype(BF16)
    sums = dot_exact(stacked, gather)
    kr = (iota((1, COLS), 1) // 8) % 4
    out = []
    for i in range(len(fields)):
        row = jnp.zeros((1, COLS), F32)
        for j in range(4):
            row = jnp.where(kr == j, sums[4 * i + j : 4 * i + j + 1], row)
        out.append(row)
    return out


def member_rows(rows):
    sub = iota((8, 128), 0)
    out = jnp.zeros((8, 128), F32)
    for m, row in enumerate(rows):
        out = jnp.where(sub == m, row, out)
    return out


def full_sum(value):
    return jnp.sum(jnp.sum(value, axis=1, keepdims=True), axis=0, keepdims=True)


def operate(v, fields):
    fe, fw, fn, fs, centre = fields
    return (
        centre * v
        + fe * (v - roll(v, -1, 1))
        + fw * (v - roll(v, 1, 1))
        + fn * (v - roll(v, -1, 0))
        + fs * (v - roll(v, 1, 0))
    )


def main(value):
    return value[:ROWS, :COLS]


def start_kernel(pos, right, diag, east, north, wet, active, coupling, stack, tile, small, rims):
    mask = wet[...].astype(F32)
    act = jnp.concatenate([jnp.broadcast_to(active[...].astype(F32), (8, 32))] * 4, axis=1)
    fields = [right[m] for m in range(M)] + [diag[...], east[...], north[...], mask]
    for f, v in enumerate(fields):
        stack[f] = v
    tail = jnp.concatenate([coupling[e, 24:, :] for e in range(3)], axis=0)
    tile[:24, :] = jnp.concatenate([coupling[e, :24, :] for e in range(3)] + [tail], axis=1)
    every = jnp.concatenate(fields, axis=0)
    hi = every.astype(BF16).astype(F32)
    mid = (every - hi).astype(BF16).astype(F32)
    parts = jnp.concatenate([hi, mid, every - hi - mid], axis=0).astype(BF16)
    row, lane = iota((16, COLS), 0), iota((16, COLS), 1)
    column = jnp.where(row < 8, row, row - 8 + COLS - HALO)
    chosen = jnp.logical_and(lane == column, row % 8 < HALO).astype(F32).astype(BF16)
    columns = mm(chosen, parts, NT)
    columns = columns[:, :256] + columns[:, 256:512] + columns[:, 512:]
    upper = iota((8, 128), 0) >= 4
    for i in range(2):
        part = columns[8 * i : 8 * i + 8]
        tile[32 + 8 * i : 40 + 8 * i, :] = jnp.where(upper, roll(part[:, 128:], 4, 0), part[:, :128])
    for i, start in enumerate((0, ROWS - HALO)):
        rims[i] = jnp.concatenate([v[start + j : start + j + 1] for j in range(HALO) for v in fields], axis=0)
    rows = block_sums([fields[m] * mask for m in range(M)])
    packed = pick([jnp.broadcast_to(r, (8, 128)) for r in rows]) * act
    row = iota((8, 128), 0)
    tile[24:32, :] = jnp.where(row == 0, packed, jnp.where(row == 1, act, 0.0))
    small[...] = tile[:32, :]


def gather_kernel(pos, t0, t1, t2, t3, t4, rims, out):
    x, y, c = pos[1], lax.div(pos[2], 2), lax.rem(pos[2], 2)
    onward = jnp.where(x == NX - 1, t1[40:48, :], t2[40:48, :])
    back = jnp.where(x == 0, t3[32:40, :], t2[32:40, :])
    tiles = (t0, t1, t2, t3, t4)
    rows = [t[:24, :] for t in tiles] + [t[24:25, :] for t in tiles] + [t[25:26, :] for t in (t1, t2, t3)]
    rows = jnp.concatenate(rows, axis=0)
    far = jnp.where(c == 0, rims[0], rims[1])
    near = jnp.where(c == 0, rims[1], rims[0])
    for d in range(NX * 4):
        out[d, :128, :] = rows
        rim = jnp.where(y == d % 4, near, far)
        out[d, 136:, :] = rim[8:]
        columns = jnp.where(lax.rem(x + 1, NX) == d // 4, onward, back)
        out[d, 128:136, :] = jnp.where(x == d // 4, rim[:8], columns)


def side(blocks, band, sender, rows=8):
    return blocks[lax.rem(band, 2) * 16 + sender * 4 + lax.div(band, 2), 128 : 128 + rows, :]


def fields_kernel(pos, stack, blocks, ext, consts, early):
    x, b = pos[1], pos[2]
    after, before = lax.rem(x + 1, NX), lax.rem(x + NX - 1, NX)
    up, down = lax.rem(b + 1, NB), lax.rem(b + NB - 1, NB)
    north_rows, south_rows = side(blocks, up, x, 24), side(blocks, down, x, 24)
    sub = iota((8, 128), 0)
    sides = []
    for band in (b, up, down):
        sides += [side(blocks, band, after), side(blocks, band, before)]
    turned = jnp.transpose(jnp.concatenate(sides + [jnp.zeros((80, 128), F32)], axis=0))
    first = iota((8, 128), 0) < 4

    def columns(rows, slot, h):
        lane = iota(rows.shape, 1)
        east_part = roll(rows, -(16 * slot + 4 * h), 1)
        west_part = roll(rows, 128 - HALO - (16 * slot + 8 + 4 * h), 1)
        return jnp.where(lane < HALO, east_part, jnp.where(lane >= 128 - HALO, west_part, 0.0))

    fields = []
    for f in range(8):
        rows = turned[32 * (f % 4) : 32 * (f % 4) + 32]
        h = f // 4
        corner = jnp.where(first, columns(rows[:8], 1, h), columns(rows[24:], 2, h))
        beyond = jnp.zeros((8, 128), F32)
        for j in range(HALO):
            at = 8 * j + f
            beyond = jnp.where(sub == j, north_rows[at : at + 1], beyond)
            beyond = jnp.where(sub == 8 - HALO + j, south_rows[at : at + 1], beyond)
        left = jnp.concatenate([stack[f], beyond], axis=0)
        right = jnp.concatenate([columns(rows, 0, h), corner], axis=0)
        fields.append(jnp.concatenate([left, right], axis=1))
    for m in range(M):
        ext[m] = fields[m]
    diag, east, north, wet = fields[4:]
    row = iota((EXT_ROWS, EXT_COLS), 0)
    grid_row = b * ROWS + jnp.where(row >= 36, row - EXT_ROWS, row)
    inside = jnp.logical_and(grid_row >= 0, grid_row < NB * ROWS - 1)
    fe = east * wet * roll(wet, -1, 1)
    fw = roll(fe, 1, 1)
    fn = jnp.where(inside, north * wet * roll(wet, -1, 0), 0.0)
    fs = roll(fn, 1, 0)
    own = wet * diag
    centre = own + (1.0 - wet)
    inverse = 1.0 / (centre + fe + fw + fn + fs)
    for i, v in enumerate((fe, fw, fn, fs, centre, inverse, wet)):
        consts[i] = v
    mask = main(wet)
    row = iota((ROWS, COLS), 0)
    col = iota((ROWS, COLS), 1)
    sums = [
        jnp.where(col % 16 == 15, main(fe), 0.0),
        jnp.where(col % 16 == 0, main(fw), 0.0),
        jnp.where(row % 8 == 7, main(fn), 0.0),
        jnp.where(row % 8 == 0, main(fs), 0.0),
        main(own),
    ]
    energy, smooth = [], []
    for m in range(M):
        r = fields[m]
        y = inverse * r
        image = main(operate(y, (fe, fw, fn, fs, centre)))
        sums.append(mask * image)
        energy.append(full_sum(main(y) * image))
        smooth.append(full_sum(main(y) * main(r)))
    rows = block_sums(sums)
    lane = iota((8, 128), 1) % 32
    scalars = jnp.where(lane == 0, member_rows(energy), jnp.where(lane == 1, member_rows(smooth), 0.0))
    early[0] = pick([member_rows(rows[5:])] * 2 + [jnp.broadcast_to(rows[0], (8, 128)), jnp.broadcast_to(rows[1], (8, 128))])
    early[1] = pick([jnp.broadcast_to(rows[i], (8, 128)) for i in (2, 3, 4)] + [scalars])


def unpack_tile(tile, x):
    group = iota((24, 128), 1) // 32
    top = roll(jnp.where(group < 3, tile, 0.0), 32 * (x - 1), 1)
    group = lane_group()
    rest = jnp.zeros((8, 128), F32)
    for e in range(3):
        to = (e + x - 1) % 4
        rest = jnp.where(group == to, roll(tile[8 * e : 8 * e + 8], 32 * (to - 3), 1), rest)
    return jnp.concatenate([top, rest], axis=0)


def unpack_weights(blocks, b, g):
    c, y = b % 2, b // 2
    tiles = [unpack_tile(blocks[c * 16 + x * 4 + y, 24 * g : 24 * g + 24, :], x) for x in range(NX)]
    return halves(jnp.concatenate(tiles, axis=0))


def forward_sweep(coarse, weights, mine, live):
    group = lane_group()
    zero = jnp.zeros((8, 128), F32)
    s = [zero if v is None else v for v in coarse[0]]
    out = s
    for b in range(1, NB):
        new = []
        for g in range(NG):
            if not live(b, g):
                new.append(zero)
                continue
            left = s[g - 1] if g > 0 else zero
            right = s[g + 1] if g < NG - 1 else zero
            lhs = jnp.concatenate(
                [jnp.where(group == 3, left, s[g]), s[g], s[g], jnp.where(group == 0, right, s[g])], axis=0
            )
            hi, lo = weights(b, g)
            o = dot3(lhs, hi, lo, NT)
            carried = pick([o[8 * x : 8 * x + 8] for x in range(NX)])
            new.append(-carried if coarse[b][g] is None else coarse[b][g] - carried)
        s = new
        out = [jnp.where(mine == b, s[g], out[g]) for g in range(NG)]
    return out


def distance(g):
    return max(0, 4 * abs(g - 2) - 4) if g != 2 else -1


def inward(b, g):
    return distance(g) < NB - 1 - b


def outward(b, g):
    return distance(g) < b


def rimward(b, g):
    return distance(g) < b + 1


def backward_sweep(pivoted, weights):
    group = lane_group()
    zero = jnp.zeros((8, 128), F32)
    s = pivoted[NB - 1]
    out = [None] * NB
    out[NB - 1] = s
    for b in range(NB - 2, -1, -1):
        o = []
        for g in range(NG):
            if not rimward(b + 1, g):
                o.append(None)
                continue
            lhs = jnp.concatenate([jnp.where(group == x, s[g], 0.0) for x in range(NX)], axis=0)
            hi, lo = weights(b + 1, g)
            o.append(dot3(lhs, hi, lo, NN))
        s = []
        for g in range(NG):
            if o[g] is None or not rimward(b, g):
                s.append(zero)
                continue
            own = o[g][8:16] + o[g][16:24]
            own = own + jnp.where(group == 3, 0.0, o[g][0:8]) + jnp.where(group == 0, 0.0, o[g][24:32])
            after = o[g + 1][0:8] if g < NG - 1 and o[g + 1] is not None else zero
            before = o[g - 1][24:32] if g > 0 and o[g - 1] is not None else zero
            own = own + jnp.where(group == 3, after, 0.0) + jnp.where(group == 0, before, 0.0)
            s.append(pivoted[b][g] - own)
        out[b] = s
    return out


def pack_window(s, extra, out):
    parts = [jnp.where(lane_group() == 0, extra, s[0])] + list(s[1:])
    for g in range(NG):
        rows = parts[g][:4]
        for z in range(NZ):
            out[z, g] = rows


def to_plane(values, out):
    for d in range(NX * NB):
        for i, v in enumerate(values):
            out[d, :, 128 * i : 128 * i + 128] = v[:4]


def unpack_swept(got):
    if len(got.shape) == 3:
        out = [got[z] for z in range(NZ)]
    else:
        reached = iota((4, 128), 1) >= 32
        out = []
        for z in range(NZ):
            acc = jnp.where(reached, got[(z + 2) % NZ, 0], 0.0)
            for g in range(1, NG):
                acc = acc + got[(z + 2 - g) % NZ, g]
            out.append(acc)
    out = jnp.concatenate(out, axis=1)
    return jnp.concatenate([out, jnp.zeros_like(out)], axis=0)


def pivot_product(swept, pivots):
    rows = jnp.concatenate([p[...] for p in pivots], axis=0)
    hi, lo = halves(rows)
    out = dot3(swept, hi, lo, NT)
    return out[:, :128], jnp.concatenate([out[:, 128:160]] * 4, axis=1)


def unpack_plane(got, field):
    group = iota((64, 128), 1) // 32
    half = field // 4 * 128
    out = None
    for x in range(NX):
        bands = [got[x * NB + b, :, half : half + 128] for b in range(NB)]
        bands = [jnp.concatenate([v, jnp.zeros_like(v)], axis=0) for v in bands]
        piece = roll(jnp.concatenate(bands, axis=0), 32 * (x - field % 4), 1)
        out = piece if out is None else jnp.where(group == x, piece, out)
    return out


def coarse_operate(s, before, after, t):
    fe, fw, fn, fs, dg = t
    lane = iota((64, 128), 1)
    kc, kr = lane % 8, (lane // 8) % 4
    east = jnp.where(kc < 7, roll(s, -1, 1), jnp.where(lane < 96, roll(s, -25, 1), roll(after, -25, 1)))
    west = jnp.where(kc > 0, roll(s, 1, 1), jnp.where(lane >= 32, roll(s, 25, 1), roll(before, 25, 1)))
    north = jnp.where(kr < 3, roll(s, -8, 1), roll(roll(s, 24, 1), -8, 0))
    south = jnp.where(kr > 0, roll(s, 8, 1), roll(roll(s, -24, 1), 8, 0))
    return dg * s + fe * (s - east) + fw * (s - west) + fn * (s - north) + fs * (s - south)


def band_sum(value):
    acc = value[0:8]
    for b in range(1, NB):
        acc = acc + value[8 * b : 8 * b + 8]
    return jnp.sum(acc, axis=1, keepdims=True)


def stored(w_hi, w_lo):
    return lambda b, g: (w_hi[b * NG + g], w_lo[b * NG + g])


def plane_rows(blocks, at):
    return [
        jnp.concatenate([blocks[b % 2 * 16 + x * 4 + b // 2, at : at + 1, :] for b in range(NB)], axis=0) for x in range(NX)
    ]


def forward_kernel(pos, blocks, out, coarse_out, acts_out, w_hi, w_lo):
    coarse = [[] for _ in range(NB)]
    for g in range(NG):
        rows = plane_rows(blocks, 120 + g)
        members = [pick([roll(rows[x], 32 * (x - m), 1) for x in range(NX)]) for m in range(M)]
        for b in range(NB):
            coarse[b].append(member_rows([v[b : b + 1] for v in members]))
    for b in range(NB):
        coarse_out[8 * b : 8 * b + 8, :] = coarse[b][2]
    for i in range(3):
        act = pick(plane_rows(blocks, 125 + i))
        for b in range(NB):
            acts_out[i, 8 * b : 8 * b + 8, :] = jnp.broadcast_to(act[b : b + 1], (8, 128))

    def weights(b, g):
        hi, lo = unpack_weights(blocks, b, g)
        w_hi[b * NG + g] = hi
        w_lo[b * NG + g] = lo
        return hi, lo

    for b in range(1, NB):
        for g in range(NG):
            if not inward(b, g) and (rimward(b, g) or outward(b, g)):
                weights(b, g)
    own = forward_sweep(coarse, weights, pos[2], inward)[2][:4]
    for z in range(NZ):
        out[z] = own


def pivot_kernel(pos, got, early, p0, p1, p2, p3, p4, out):
    first, last = pivot_product(unpack_swept(got), (p0, p1, p2, p3, p4))
    to_plane([first, jnp.where(lane_group() == 0, last, early[0]), early[1]], out)


def middle_kernel(pos, got, w_hi, w_lo, coarse_right, acts, out, s_out, coarse_image_out, t_out):
    windows = [unpack_plane(got, f) for f in range(12)]
    pivoted = [[windows[g][8 * b : 8 * b + 8] for g in range(NG)] for b in range(NB)]
    settled = backward_sweep(pivoted, stored(w_hi, w_lo))
    s1, s2, s3 = (
        jnp.concatenate([settled[b][g] for b in range(NB)], axis=0) * acts[g - 1] for g in (1, 2, 3)
    )
    smooth, t, scalars = windows[5], windows[6:11], windows[11]
    t_s = coarse_operate(s2, s1, s3, t)
    coarse_image = acts[1] * (smooth + t_s)
    lane = iota((64, 128), 1) % 32
    weight = band_sum(coarse_right[...] * s2 + jnp.where(lane == 1, scalars, 0.0))
    energy = band_sum((2.0 * smooth + t_s) * s2 + jnp.where(lane == 0, scalars, 0.0))
    lane = iota((8, 128), 1)
    extra = jnp.where(lane == 0, weight, jnp.where(lane == 1, energy, 0.0))
    for i, v in enumerate((s1, s2, s3)):
        s_out[i] = v
    coarse_image_out[...] = coarse_image
    for i, v in enumerate(t):
        t_out[i] = v
    coarse = [[None, None, coarse_image[8 * b : 8 * b + 8], None, None] for b in range(NB)]
    pack_window(forward_sweep(coarse, stored(w_hi, w_lo), pos[2], outward), extra, out)


def spread_rows(s, x, kr):
    lane = iota((8, 128), 1)
    return jnp.take_along_axis(s, x * 32 + kr * 8 + lane // 16, axis=1)


def spread_sides(s1, s2, s3, x, kr):
    lane = iota((8, 128), 1)
    east = jnp.take_along_axis(jnp.where(x < 3, s2, s3), jnp.zeros_like(lane) + lax.rem(x + 1, 4) * 32 + kr * 8, axis=1)
    west = jnp.take_along_axis(jnp.where(x > 0, s2, s1), jnp.zeros_like(lane) + lax.rem(x + 3, 4) * 32 + kr * 8 + 7, axis=1)
    return jnp.where(lane < 64, east, west)


def image_kernel(pos, ext, consts, s_ref, pre_out, image_out):
    x, b = pos[1], pos[2]
    north_band, south_band = lax.rem(b + 1, NB), lax.rem(b + NB - 1, NB)
    own = [s_ref[g, b] for g in range(3)]
    up = [s_ref[g, north_band] for g in range(3)]
    down = [s_ref[g, south_band] for g in range(3)]
    mains = [spread_rows(own[1], x, kr) for kr in range(4)]
    sides = [spread_sides(*own, x, kr) for kr in range(4)]
    first = iota((8, 128), 0) < 4
    up_main, up_side = spread_rows(up[1], x, 0), spread_sides(*up, x, 0)
    down_main, down_side = spread_rows(down[1], x, 3), spread_sides(*down, x, 3)
    fields = tuple(consts[i] for i in range(5))
    inverse, wet = consts[5], consts[6]
    for m in range(M):
        wide = lambda v: jnp.broadcast_to(v[m : m + 1], (8, 128))
        left = [wide(v) for v in mains] + [jnp.where(first, wide(up_main), wide(down_main))]
        right = [wide(v) for v in sides] + [jnp.where(first, wide(up_side), wide(down_side))]
        spread = jnp.concatenate([jnp.concatenate(left, axis=0), jnp.concatenate(right, axis=0)], axis=1)
        pre = inverse * ext[m] + wet * spread
        pre_out[m] = main(pre)
        image_out[m] = operate(pre, fields)


def step_kernel(pos, got, ext, consts, image, p0, p1, p2, p3, p4, out, smooth_out, scalar_out):
    first, last = pivot_product(unpack_swept(got), (p0, p1, p2, p3, p4))
    sums = got[0, 0]
    for z in range(1, NZ):
        sums = sums + got[z, 0]
    sums = jnp.concatenate([sums, jnp.ones_like(sums)], axis=0)
    weight, energy = sums[:, 0:1], sums[:, 1:2]
    step = weight / energy
    fields = tuple(consts[i] for i in range(5))
    inverse, wet = consts[5], consts[6]
    mask = main(wet)
    blocks, dots = [], ([], [], [])
    for m in range(M):
        residual = ext[m] - step[m : m + 1] * image[m]
        smooth = inverse * residual
        applied = main(operate(smooth, fields))
        smooth = main(smooth)
        smooth_out[m] = smooth
        blocks.append(mask * applied)
        dots[0].append(full_sum(smooth * main(residual)))
        dots[1].append(full_sum(smooth * applied))
        dots[2].append(full_sum(smooth * main(image[m])))
    rows = member_rows(block_sums(blocks))
    lane = iota((8, 128), 1) % 32
    scalars = jnp.zeros((8, 128), F32)
    for i in range(3):
        scalars = jnp.where(lane == i, member_rows(dots[i]), scalars)
    to_plane([first, pick([last, rows, scalars, jnp.zeros((8, 128), F32)])], out)
    lane = iota((8, 128), 1)
    scalar_out[...] = jnp.where(lane == 0, weight, jnp.where(lane == 1, energy, jnp.where(lane == 2, step, 0.0)))


def last_kernel(pos, got, w_hi, w_lo, s_ref, coarse_right, coarse_image, t_ref, acts, scalar, out, s_out):
    windows = [unpack_plane(got, f) for f in range(7)]
    pivoted = [[windows[g][8 * b : 8 * b + 8] for g in range(NG)] for b in range(NB)]
    settled = backward_sweep(pivoted, stored(w_hi, w_lo))
    t = tuple(t_ref[i] for i in range(5))
    step = jnp.concatenate([scalar[:, 2:3]] * NB, axis=0)
    s1, s2, s3 = (
        s_ref[g - 1] - step * (jnp.concatenate([settled[b][g] for b in range(NB)], axis=0) * acts[g - 1])
        for g in (1, 2, 3)
    )
    s_out[...] = s2
    t_s = coarse_operate(s2, s1, s3, t)
    smooth, scalars = windows[5], windows[6]
    lane = iota((64, 128), 1) % 32
    dots = (
        band_sum((coarse_right[...] - step * coarse_image[...]) * s2 + jnp.where(lane == 0, scalars, 0.0)),
        band_sum((2.0 * smooth + t_s) * s2 + jnp.where(lane == 1, scalars, 0.0)),
        band_sum(coarse_image[...] * s2 + jnp.where(lane == 2, scalars, 0.0)),
    )
    lane = iota((8, 128), 1)
    res = jnp.zeros((8, 128), F32)
    for i in range(3):
        res = jnp.where(lane == i, dots[i], res)
    for z in range(NZ):
        out[z] = res[:4]


def finish_kernel(pos, got, scalar, pre, smooth, stack, s_ref, out):
    x, b = pos[1], pos[2]
    sums = got[0]
    for z in range(1, NZ):
        sums = sums + got[z]
    renewed, energy, cross = sums[:, 0:1], sums[:, 1:2], sums[:, 2:3]
    weight, first_energy, step = scalar[:4, 0:1], scalar[:4, 1:2], scalar[:4, 2:3]
    ratio = renewed / weight
    second = renewed / (energy + 2.0 * ratio * cross + ratio * ratio * first_energy)
    own = s_ref[b]
    mains = [spread_rows(own, x, kr) for kr in range(4)]
    mask = stack[7]
    for m in range(M):
        spread = jnp.concatenate([jnp.broadcast_to(v[m : m + 1], (8, 128)) for v in mains], axis=0)
        z1 = smooth[m] + mask * spread
        z0 = pre[m]
        out[m] = step[m : m + 1] * z0 + second[m : m + 1] * (z1 + ratio[m : m + 1] * z0)


def shift(value, axes, count, by):
    return lax.ppermute(value, axes, [(i, (i + by) % count) for i in range(count)])


def to_all(value, axes, count):
    return lax.all_to_all(jnp.broadcast_to(value[None], (count,) + value.shape), axes, 0, 0)


def body(right_side, diagonal, east_face, north_face, wet, active, coupling, pivots):
    stack, tile, part, rims = call(
        start_kernel,
        [(8, ROWS, COLS), (48, 128), (32, 128), (2, 24, 128)],
        right_side, diagonal, east_face, north_face, wet, active[0], coupling[0, 0],
        fetch=range(7),
        room=FETCH_BYTES,
    )
    window = [tile if g == 2 else shift(tile if g in (1, 3) else part, "z", NZ, 2 - g) for g in range(NG)]
    (plane,) = call(gather_kernel, [(NX * 4, 152, 128)], *window, rims, fetch=(2, 5))
    plane = lax.all_to_all(plane, ("x", "y"), 0, 0)
    blocks = to_all(plane, "c", 2).reshape(32, 152, 128)

    pivot_rows = [pivots[0] if g == 2 else shift(pivots[0], "z", NZ, 2 - g) for g in range(NG)]

    ring, rim = (NZ, NG, 4, 128), (M, EXT_ROWS, EXT_COLS)
    weights = ((NB * NG, 128, 128), BF16)
    ext, consts, early = call(
        fields_kernel, [rim, (7, EXT_ROWS, EXT_COLS), (2, 8, 128)], stack, blocks
    )
    swept, coarse_right, acts, w_hi, w_lo = call(
        forward_kernel, [(NZ, 4, 128), (64, 128), (3, 64, 128), weights, weights], blocks
    )
    swept, early, pivot_rows = lax.optimization_barrier((swept, early, pivot_rows))
    got = lax.all_to_all(swept, "z", 0, 0)
    (message,) = call(pivot_kernel, [(32, 4, 384)], got, early, *pivot_rows)
    got = lax.all_to_all(message, ("x", "y", "c"), 0, 0)
    swept, s0, coarse_image, t = call(
        middle_kernel, [ring, (3, 64, 128), (64, 128), (5, 64, 128)], got, w_hi, w_lo, coarse_right, acts
    )
    pre, image = call(image_kernel, [(M, ROWS, COLS), rim], ext, consts, s0.reshape(3, NB, 8, 128))
    swept, pre, image = lax.optimization_barrier((swept, pre, image))
    got = lax.all_to_all(swept, "z", 0, 0)
    message, smooth, scalar = call(
        step_kernel, [(32, 4, 256), (M, ROWS, COLS), (8, 128)], got, ext, consts, image, *pivot_rows
    )
    got = lax.all_to_all(message, ("x", "y", "c"), 0, 0)
    dots, s1 = call(
        last_kernel, [(NZ, 4, 128), (64, 128)], got, w_hi, w_lo, s0, coarse_right, coarse_image, t, acts, scalar
    )
    got = lax.all_to_all(dots, "z", 0, 0)
    (out,) = call(finish_kernel, [(M, ROWS, COLS)], got, scalar, pre, smooth, stack, s1.reshape(NB, 8, 128))
    return out


def solution(mesh):
    fine = Mesh(mesh.devices.reshape(NZ, NX, 4, 2), ("z", "x", "y", "c"))
    lat, lon = ("y", "c"), ("z", "x")
    in_specs = (
        P(None, lat, lon),
        P(lat, lon),
        P(lat, lon),
        P(lat, lon),
        P(lat, lon),
        P(lat, lon, None),
        P(lat, lon, None, None, None),
        P(lat, lon, None),
    )
    return jax.shard_map(body, mesh=fine, in_specs=in_specs, out_specs=P(None, lat, lon), check_vma=False)
```

```python
import jax
import jax.numpy as jnp
from jax import lax
from jax.experimental import pallas as pl
from jax.experimental.pallas import tpu as pltpu
from jax.sharding import Mesh
from jax.sharding import PartitionSpec as P

F32 = jnp.float32
BF16 = jnp.bfloat16
M = 4
NB = 8
NX = 4
NZ = 16
NG = 5
ROWS = 32
COLS = 128
HALO = 3
EXT_ROWS = 40
EXT_COLS = 256
NT = (((1,), (1,)), ((), ()))
NN = (((1,), (0,)), ((), ()))
VMEM_BYTES = 12 * 1024 * 1024
FETCH_BYTES = 63 * 1024 * 1024


def call(kernel, outs, *arrays, fetch=(), room=VMEM_BYTES):
    outs = [o if o[1] == BF16 else (o, F32) for o in outs]
    vmem, hbm = pl.BlockSpec(memory_space=pltpu.VMEM), pl.BlockSpec(memory_space=pltpu.HBM)
    n, count = len(arrays), len(fetch)

    def whole(*refs):
        given, rest, held = list(refs[:n]), refs[n : n + len(outs)], refs[n + len(outs) :]
        copies = [pltpu.make_async_copy(given[i], held[j], held[count].at[j]) for j, i in enumerate(fetch)]
        for copy in copies:
            copy.start()
        for copy in copies:
            copy.wait()
        for j, i in enumerate(fetch):
            given[i] = held[j]
        z, x = lax.axis_index("z"), lax.axis_index("x")
        b = 2 * lax.axis_index("y") + lax.axis_index("c")
        kernel((z, x, b), *given, *rest)

    scratch = [pltpu.VMEM(arrays[i].shape, arrays[i].dtype) for i in fetch]
    if fetch:
        scratch.append(pltpu.SemaphoreType.DMA((count,)))
    return pl.pallas_call(
        whole,
        out_shape=[jax.ShapeDtypeStruct(s, d) for s, d in outs],
        in_specs=[hbm if i in fetch else vmem for i in range(n)],
        out_specs=[vmem] * len(outs),
        scratch_shapes=scratch,
        compiler_params=pltpu.CompilerParams(vmem_limit_bytes=room),
    )(*arrays)


def iota(shape, dim):
    return lax.broadcasted_iota(jnp.int32, shape, dim)


def roll(value, shift, axis):
    shift = shift % value.shape[axis]
    return value if shift == 0 else pltpu.roll(value, shift, axis)


def mm(a, b, dims):
    return lax.dot_general(a, b, dims, preferred_element_type=F32)


def halves(value):
    hi = value.astype(BF16)
    return hi, (value - hi.astype(F32)).astype(BF16)


def dot3(a, b_hi, b_lo, dims):
    hi = a.astype(BF16).astype(F32)
    both = jnp.concatenate([hi, a - hi], axis=0).astype(BF16)
    n = a.shape[0]
    top = mm(both, b_hi, dims)
    low = mm(both, b_lo, dims)
    return top[:n] + top[n:] + low[:n]


def dot_exact(a, b):
    hi = a.astype(BF16).astype(F32)
    rest = a - hi
    mid = rest.astype(BF16).astype(F32)
    parts = jnp.concatenate([hi, mid, rest - mid], axis=0).astype(BF16)
    out = mm(parts, b, NN)
    n = a.shape[0]
    return out[:n] + out[n : 2 * n] + out[2 * n :]


def lane_group():
    return iota((8, 128), 1) // 32


def pick(values):
    group = lane_group()
    out = values[-1]
    for i in range(len(values) - 2, -1, -1):
        out = jnp.where(group == i, values[i], out)
    return out


def block_sums(fields):
    rows = [jnp.sum(f.reshape(4, 8, COLS), axis=1) for f in fields]
    stacked = jnp.concatenate(rows, axis=0)
    pad = -stacked.shape[0] % 16
    if pad:
        stacked = jnp.concatenate([stacked, jnp.zeros((pad, COLS), F32)], axis=0)
    gather = (iota((COLS, COLS), 0) // 16 == iota((COLS, COLS), 1) % 8).astype(F32).astype(BF16)
    sums = dot_exact(stacked, gather)
    kr = (iota((1, COLS), 1) // 8) % 4
    out = []
    for i in range(len(fields)):
        row = jnp.zeros((1, COLS), F32)
        for j in range(4):
            row = jnp.where(kr == j, sums[4 * i + j : 4 * i + j + 1], row)
        out.append(row)
    return out


def member_rows(rows):
    sub = iota((8, 128), 0)
    out = jnp.zeros((8, 128), F32)
    for m, row in enumerate(rows):
        out = jnp.where(sub == m, row, out)
    return out


def full_sum(value):
    return jnp.sum(jnp.sum(value, axis=1, keepdims=True), axis=0, keepdims=True)


def operate(v, fields):
    fe, fw, fn, fs, centre = fields
    return (
        centre * v
        + fe * (v - roll(v, -1, 1))
        + fw * (v - roll(v, 1, 1))
        + fn * (v - roll(v, -1, 0))
        + fs * (v - roll(v, 1, 0))
    )


def main(value):
    return value[:ROWS, :COLS]


def start_kernel(pos, right, diag, east, north, wet, active, coupling, stack, tile, rims):
    mask = wet[...].astype(F32)
    act = jnp.concatenate([jnp.broadcast_to(active[...].astype(F32), (8, 32))] * 4, axis=1)
    fields = [right[m] for m in range(M)] + [diag[...], east[...], north[...], mask]
    for f, v in enumerate(fields):
        stack[f] = v
    tail = jnp.concatenate([coupling[e, 24:, :] for e in range(3)], axis=0)
    tile[:24, :] = jnp.concatenate([coupling[e, :24, :] for e in range(3)] + [tail], axis=1)
    every = jnp.concatenate(fields, axis=0)
    hi = every.astype(BF16).astype(F32)
    mid = (every - hi).astype(BF16).astype(F32)
    parts = jnp.concatenate([hi, mid, every - hi - mid], axis=0).astype(BF16)
    row, lane = iota((16, COLS), 0), iota((16, COLS), 1)
    column = jnp.where(row < 8, row, row - 8 + COLS - HALO)
    chosen = jnp.logical_and(lane == column, row % 8 < HALO).astype(F32).astype(BF16)
    columns = mm(chosen, parts, NT)
    columns = columns[:, :256] + columns[:, 256:512] + columns[:, 512:]
    upper = iota((8, 128), 0) >= 4
    for i in range(2):
        part = columns[8 * i : 8 * i + 8]
        tile[32 + 8 * i : 40 + 8 * i, :] = jnp.where(upper, roll(part[:, 128:], 4, 0), part[:, :128])
    for i, start in enumerate((0, ROWS - HALO)):
        rims[i] = jnp.concatenate([v[start + j : start + j + 1] for j in range(HALO) for v in fields], axis=0)
    rows = block_sums([fields[m] * mask for m in range(M)])
    packed = pick([jnp.broadcast_to(r, (8, 128)) for r in rows]) * act
    row = iota((8, 128), 0)
    tile[24:32, :] = jnp.where(row == 0, packed, jnp.where(row == 1, act, 0.0))


def gather_kernel(pos, t0, t1, t2, t3, t4, rims, out):
    x, y, c = pos[1], lax.div(pos[2], 2), lax.rem(pos[2], 2)
    onward = jnp.where(x == NX - 1, t1[40:48, :], t2[40:48, :])
    back = jnp.where(x == 0, t3[32:40, :], t2[32:40, :])
    tiles = (t0, t1, t2, t3, t4)
    rows = [t[:24, :] for t in tiles] + [t[24:25, :] for t in tiles] + [t[25:26, :] for t in (t1, t2, t3)]
    rows = jnp.concatenate(rows, axis=0)
    far = jnp.where(c == 0, rims[0], rims[1])
    near = jnp.where(c == 0, rims[1], rims[0])
    for d in range(NX * 4):
        out[d, :128, :] = rows
        rim = jnp.where(y == d % 4, near, far)
        out[d, 136:, :] = rim[8:]
        columns = jnp.where(lax.rem(x + 1, NX) == d // 4, onward, back)
        out[d, 128:136, :] = jnp.where(x == d // 4, rim[:8], columns)


def side(blocks, band, sender, rows=8):
    return blocks[lax.rem(band, 2) * 16 + sender * 4 + lax.div(band, 2), 128 : 128 + rows, :]


def fields_kernel(pos, stack, blocks, ext, consts, early):
    x, b = pos[1], pos[2]
    after, before = lax.rem(x + 1, NX), lax.rem(x + NX - 1, NX)
    up, down = lax.rem(b + 1, NB), lax.rem(b + NB - 1, NB)
    north_rows, south_rows = side(blocks, up, x, 24), side(blocks, down, x, 24)
    sub = iota((8, 128), 0)
    sides = []
    for band in (b, up, down):
        sides += [side(blocks, band, after), side(blocks, band, before)]
    turned = jnp.transpose(jnp.concatenate(sides + [jnp.zeros((80, 128), F32)], axis=0))
    first = iota((8, 128), 0) < 4

    def columns(rows, slot, h):
        lane = iota(rows.shape, 1)
        east_part = roll(rows, -(16 * slot + 4 * h), 1)
        west_part = roll(rows, 128 - HALO - (16 * slot + 8 + 4 * h), 1)
        return jnp.where(lane < HALO, east_part, jnp.where(lane >= 128 - HALO, west_part, 0.0))

    fields = []
    for f in range(8):
        rows = turned[32 * (f % 4) : 32 * (f % 4) + 32]
        h = f // 4
        corner = jnp.where(first, columns(rows[:8], 1, h), columns(rows[24:], 2, h))
        beyond = jnp.zeros((8, 128), F32)
        for j in range(HALO):
            at = 8 * j + f
            beyond = jnp.where(sub == j, north_rows[at : at + 1], beyond)
            beyond = jnp.where(sub == 8 - HALO + j, south_rows[at : at + 1], beyond)
        left = jnp.concatenate([stack[f], beyond], axis=0)
        right = jnp.concatenate([columns(rows, 0, h), corner], axis=0)
        fields.append(jnp.concatenate([left, right], axis=1))
    for m in range(M):
        ext[m] = fields[m]
    diag, east, north, wet = fields[4:]
    row = iota((EXT_ROWS, EXT_COLS), 0)
    grid_row = b * ROWS + jnp.where(row >= 36, row - EXT_ROWS, row)
    inside = jnp.logical_and(grid_row >= 0, grid_row < NB * ROWS - 1)
    fe = east * wet * roll(wet, -1, 1)
    fw = roll(fe, 1, 1)
    fn = jnp.where(inside, north * wet * roll(wet, -1, 0), 0.0)
    fs = roll(fn, 1, 0)
    own = wet * diag
    centre = own + (1.0 - wet)
    inverse = 1.0 / (centre + fe + fw + fn + fs)
    for i, v in enumerate((fe, fw, fn, fs, centre, inverse, wet)):
        consts[i] = v
    mask = main(wet)
    row = iota((ROWS, COLS), 0)
    col = iota((ROWS, COLS), 1)
    sums = [
        jnp.where(col % 16 == 15, main(fe), 0.0),
        jnp.where(col % 16 == 0, main(fw), 0.0),
        jnp.where(row % 8 == 7, main(fn), 0.0),
        jnp.where(row % 8 == 0, main(fs), 0.0),
        main(own),
    ]
    energy, smooth = [], []
    for m in range(M):
        r = fields[m]
        y = inverse * r
        image = main(operate(y, (fe, fw, fn, fs, centre)))
        sums.append(mask * image)
        energy.append(full_sum(main(y) * image))
        smooth.append(full_sum(main(y) * main(r)))
    rows = block_sums(sums)
    lane = iota((8, 128), 1) % 32
    scalars = jnp.where(lane == 0, member_rows(energy), jnp.where(lane == 1, member_rows(smooth), 0.0))
    early[0] = pick([member_rows(rows[5:])] * 2 + [jnp.broadcast_to(rows[0], (8, 128)), jnp.broadcast_to(rows[1], (8, 128))])
    early[1] = pick([jnp.broadcast_to(rows[i], (8, 128)) for i in (2, 3, 4)] + [scalars])


def unpack_tile(tile, x):
    group = iota((24, 128), 1) // 32
    top = roll(jnp.where(group < 3, tile, 0.0), 32 * (x - 1), 1)
    group = lane_group()
    rest = jnp.zeros((8, 128), F32)
    for e in range(3):
        to = (e + x - 1) % 4
        rest = jnp.where(group == to, roll(tile[8 * e : 8 * e + 8], 32 * (to - 3), 1), rest)
    return jnp.concatenate([top, rest], axis=0)


def unpack_weights(blocks, b, g):
    c, y = b % 2, b // 2
    tiles = [unpack_tile(blocks[c * 16 + x * 4 + y, 24 * g : 24 * g + 24, :], x) for x in range(NX)]
    return halves(jnp.concatenate(tiles, axis=0))


def forward_sweep(coarse, weights, mine, live):
    group = lane_group()
    zero = jnp.zeros((8, 128), F32)
    s = [zero if v is None else v for v in coarse[0]]
    out = s
    for b in range(1, NB):
        new = []
        for g in range(NG):
            if not live(b, g):
                new.append(zero)
                continue
            left = s[g - 1] if g > 0 else zero
            right = s[g + 1] if g < NG - 1 else zero
            lhs = jnp.concatenate(
                [jnp.where(group == 3, left, s[g]), s[g], s[g], jnp.where(group == 0, right, s[g])], axis=0
            )
            hi, lo = weights(b, g)
            o = dot3(lhs, hi, lo, NT)
            carried = pick([o[8 * x : 8 * x + 8] for x in range(NX)])
            new.append(-carried if coarse[b][g] is None else coarse[b][g] - carried)
        s = new
        out = [jnp.where(mine == b, s[g], out[g]) for g in range(NG)]
    return out


def distance(g):
    return max(0, 4 * abs(g - 2) - 4) if g != 2 else -1


def inward(b, g):
    return distance(g) < NB - 1 - b


def outward(b, g):
    return distance(g) < b


def rimward(b, g):
    return distance(g) < b + 1


def backward_sweep(pivoted, weights):
    group = lane_group()
    zero = jnp.zeros((8, 128), F32)
    s = pivoted[NB - 1]
    out = [None] * NB
    out[NB - 1] = s
    for b in range(NB - 2, -1, -1):
        o = []
        for g in range(NG):
            if not rimward(b + 1, g):
                o.append(None)
                continue
            lhs = jnp.concatenate([jnp.where(group == x, s[g], 0.0) for x in range(NX)], axis=0)
            hi, lo = weights(b + 1, g)
            o.append(dot3(lhs, hi, lo, NN))
        s = []
        for g in range(NG):
            if o[g] is None or not rimward(b, g):
                s.append(zero)
                continue
            own = o[g][8:16] + o[g][16:24]
            own = own + jnp.where(group == 3, 0.0, o[g][0:8]) + jnp.where(group == 0, 0.0, o[g][24:32])
            after = o[g + 1][0:8] if g < NG - 1 and o[g + 1] is not None else zero
            before = o[g - 1][24:32] if g > 0 and o[g - 1] is not None else zero
            own = own + jnp.where(group == 3, after, 0.0) + jnp.where(group == 0, before, 0.0)
            s.append(pivoted[b][g] - own)
        out[b] = s
    return out


def pack_window(s, extra, out):
    parts = [jnp.where(lane_group() == 0, extra, s[0])] + list(s[1:])
    for g in range(NG):
        rows = parts[g][:4]
        for z in range(NZ):
            out[z, g] = rows


def to_plane(values, out):
    for d in range(NX * NB):
        for i, v in enumerate(values):
            out[d, :, 128 * i : 128 * i + 128] = v[:4]


def unpack_swept(got):
    if len(got.shape) == 3:
        out = [got[z] for z in range(NZ)]
    else:
        reached = iota((4, 128), 1) >= 32
        out = []
        for z in range(NZ):
            acc = jnp.where(reached, got[(z + 2) % NZ, 0], 0.0)
            for g in range(1, NG):
                acc = acc + got[(z + 2 - g) % NZ, g]
            out.append(acc)
    out = jnp.concatenate(out, axis=1)
    return jnp.concatenate([out, jnp.zeros_like(out)], axis=0)


def pivot_product(swept, pivots):
    rows = jnp.concatenate([p[...] for p in pivots], axis=0)
    hi, lo = halves(rows)
    out = dot3(swept, hi, lo, NT)
    return out[:, :128], jnp.concatenate([out[:, 128:160]] * 4, axis=1)


def unpack_plane(got, field):
    group = iota((64, 128), 1) // 32
    half = field // 4 * 128
    out = None
    for x in range(NX):
        bands = [got[x * NB + b, :, half : half + 128] for b in range(NB)]
        bands = [jnp.concatenate([v, jnp.zeros_like(v)], axis=0) for v in bands]
        piece = roll(jnp.concatenate(bands, axis=0), 32 * (x - field % 4), 1)
        out = piece if out is None else jnp.where(group == x, piece, out)
    return out


def coarse_operate(s, before, after, t):
    fe, fw, fn, fs, dg = t
    lane = iota((64, 128), 1)
    kc, kr = lane % 8, (lane // 8) % 4
    east = jnp.where(kc < 7, roll(s, -1, 1), jnp.where(lane < 96, roll(s, -25, 1), roll(after, -25, 1)))
    west = jnp.where(kc > 0, roll(s, 1, 1), jnp.where(lane >= 32, roll(s, 25, 1), roll(before, 25, 1)))
    north = jnp.where(kr < 3, roll(s, -8, 1), roll(roll(s, 24, 1), -8, 0))
    south = jnp.where(kr > 0, roll(s, 8, 1), roll(roll(s, -24, 1), 8, 0))
    return dg * s + fe * (s - east) + fw * (s - west) + fn * (s - north) + fs * (s - south)


def band_sum(value):
    acc = value[0:8]
    for b in range(1, NB):
        acc = acc + value[8 * b : 8 * b + 8]
    return jnp.sum(acc, axis=1, keepdims=True)


def stored(w_hi, w_lo):
    return lambda b, g: (w_hi[b * NG + g], w_lo[b * NG + g])


def plane_rows(blocks, at):
    return [
        jnp.concatenate([blocks[b % 2 * 16 + x * 4 + b // 2, at : at + 1, :] for b in range(NB)], axis=0) for x in range(NX)
    ]


def forward_kernel(pos, blocks, out, coarse_out, acts_out, w_hi, w_lo):
    coarse = [[] for _ in range(NB)]
    for g in range(NG):
        rows = plane_rows(blocks, 120 + g)
        members = [pick([roll(rows[x], 32 * (x - m), 1) for x in range(NX)]) for m in range(M)]
        for b in range(NB):
            coarse[b].append(member_rows([v[b : b + 1] for v in members]))
    for b in range(NB):
        coarse_out[8 * b : 8 * b + 8, :] = coarse[b][2]
    for i in range(3):
        act = pick(plane_rows(blocks, 125 + i))
        for b in range(NB):
            acts_out[i, 8 * b : 8 * b + 8, :] = jnp.broadcast_to(act[b : b + 1], (8, 128))

    def weights(b, g):
        hi, lo = unpack_weights(blocks, b, g)
        w_hi[b * NG + g] = hi
        w_lo[b * NG + g] = lo
        return hi, lo

    for b in range(1, NB):
        for g in range(NG):
            if not inward(b, g) and (rimward(b, g) or outward(b, g)):
                weights(b, g)
    own = forward_sweep(coarse, weights, pos[2], inward)[2][:4]
    for z in range(NZ):
        out[z] = own


def pivot_kernel(pos, got, early, p0, p1, p2, p3, p4, out):
    first, last = pivot_product(unpack_swept(got), (p0, p1, p2, p3, p4))
    to_plane([first, jnp.where(lane_group() == 0, last, early[0]), early[1]], out)


def middle_kernel(pos, got, w_hi, w_lo, coarse_right, acts, out, s_out, coarse_image_out, t_out):
    windows = [unpack_plane(got, f) for f in range(12)]
    pivoted = [[windows[g][8 * b : 8 * b + 8] for g in range(NG)] for b in range(NB)]
    settled = backward_sweep(pivoted, stored(w_hi, w_lo))
    s1, s2, s3 = (
        jnp.concatenate([settled[b][g] for b in range(NB)], axis=0) * acts[g - 1] for g in (1, 2, 3)
    )
    smooth, t, scalars = windows[5], windows[6:11], windows[11]
    t_s = coarse_operate(s2, s1, s3, t)
    coarse_image = acts[1] * (smooth + t_s)
    lane = iota((64, 128), 1) % 32
    weight = band_sum(coarse_right[...] * s2 + jnp.where(lane == 1, scalars, 0.0))
    energy = band_sum((2.0 * smooth + t_s) * s2 + jnp.where(lane == 0, scalars, 0.0))
    lane = iota((8, 128), 1)
    extra = jnp.where(lane == 0, weight, jnp.where(lane == 1, energy, 0.0))
    for i, v in enumerate((s1, s2, s3)):
        s_out[i] = v
    coarse_image_out[...] = coarse_image
    for i, v in enumerate(t):
        t_out[i] = v
    coarse = [[None, None, coarse_image[8 * b : 8 * b + 8], None, None] for b in range(NB)]
    pack_window(forward_sweep(coarse, stored(w_hi, w_lo), pos[2], outward), extra, out)


def spread_rows(s, x, kr):
    lane = iota((8, 128), 1)
    return jnp.take_along_axis(s, x * 32 + kr * 8 + lane // 16, axis=1)


def spread_sides(s1, s2, s3, x, kr):
    lane = iota((8, 128), 1)
    east = jnp.take_along_axis(jnp.where(x < 3, s2, s3), jnp.zeros_like(lane) + lax.rem(x + 1, 4) * 32 + kr * 8, axis=1)
    west = jnp.take_along_axis(jnp.where(x > 0, s2, s1), jnp.zeros_like(lane) + lax.rem(x + 3, 4) * 32 + kr * 8 + 7, axis=1)
    return jnp.where(lane < 64, east, west)


def image_kernel(pos, ext, consts, s_ref, pre_out, image_out):
    x, b = pos[1], pos[2]
    north_band, south_band = lax.rem(b + 1, NB), lax.rem(b + NB - 1, NB)
    own = [s_ref[g, b] for g in range(3)]
    up = [s_ref[g, north_band] for g in range(3)]
    down = [s_ref[g, south_band] for g in range(3)]
    mains = [spread_rows(own[1], x, kr) for kr in range(4)]
    sides = [spread_sides(*own, x, kr) for kr in range(4)]
    first = iota((8, 128), 0) < 4
    up_main, up_side = spread_rows(up[1], x, 0), spread_sides(*up, x, 0)
    down_main, down_side = spread_rows(down[1], x, 3), spread_sides(*down, x, 3)
    fields = tuple(consts[i] for i in range(5))
    inverse, wet = consts[5], consts[6]
    for m in range(M):
        wide = lambda v: jnp.broadcast_to(v[m : m + 1], (8, 128))
        left = [wide(v) for v in mains] + [jnp.where(first, wide(up_main), wide(down_main))]
        right = [wide(v) for v in sides] + [jnp.where(first, wide(up_side), wide(down_side))]
        spread = jnp.concatenate([jnp.concatenate(left, axis=0), jnp.concatenate(right, axis=0)], axis=1)
        pre = inverse * ext[m] + wet * spread
        pre_out[m] = main(pre)
        image_out[m] = operate(pre, fields)


def step_kernel(pos, got, ext, consts, image, p0, p1, p2, p3, p4, out, smooth_out, scalar_out):
    first, last = pivot_product(unpack_swept(got), (p0, p1, p2, p3, p4))
    sums = got[0, 0]
    for z in range(1, NZ):
        sums = sums + got[z, 0]
    sums = jnp.concatenate([sums, jnp.ones_like(sums)], axis=0)
    weight, energy = sums[:, 0:1], sums[:, 1:2]
    step = weight / energy
    fields = tuple(consts[i] for i in range(5))
    inverse, wet = consts[5], consts[6]
    mask = main(wet)
    blocks, dots = [], ([], [], [])
    for m in range(M):
        residual = ext[m] - step[m : m + 1] * image[m]
        smooth = inverse * residual
        applied = main(operate(smooth, fields))
        smooth = main(smooth)
        smooth_out[m] = smooth
        blocks.append(mask * applied)
        dots[0].append(full_sum(smooth * main(residual)))
        dots[1].append(full_sum(smooth * applied))
        dots[2].append(full_sum(smooth * main(image[m])))
    rows = member_rows(block_sums(blocks))
    lane = iota((8, 128), 1) % 32
    scalars = jnp.zeros((8, 128), F32)
    for i in range(3):
        scalars = jnp.where(lane == i, member_rows(dots[i]), scalars)
    to_plane([first, pick([last, rows, scalars, jnp.zeros((8, 128), F32)])], out)
    lane = iota((8, 128), 1)
    scalar_out[...] = jnp.where(lane == 0, weight, jnp.where(lane == 1, energy, jnp.where(lane == 2, step, 0.0)))


def last_kernel(pos, got, w_hi, w_lo, s_ref, coarse_right, coarse_image, t_ref, acts, scalar, out, s_out):
    windows = [unpack_plane(got, f) for f in range(7)]
    pivoted = [[windows[g][8 * b : 8 * b + 8] for g in range(NG)] for b in range(NB)]
    settled = backward_sweep(pivoted, stored(w_hi, w_lo))
    t = tuple(t_ref[i] for i in range(5))
    step = jnp.concatenate([scalar[:, 2:3]] * NB, axis=0)
    s1, s2, s3 = (
        s_ref[g - 1] - step * (jnp.concatenate([settled[b][g] for b in range(NB)], axis=0) * acts[g - 1])
        for g in (1, 2, 3)
    )
    s_out[...] = s2
    t_s = coarse_operate(s2, s1, s3, t)
    smooth, scalars = windows[5], windows[6]
    lane = iota((64, 128), 1) % 32
    dots = (
        band_sum((coarse_right[...] - step * coarse_image[...]) * s2 + jnp.where(lane == 0, scalars, 0.0)),
        band_sum((2.0 * smooth + t_s) * s2 + jnp.where(lane == 1, scalars, 0.0)),
        band_sum(coarse_image[...] * s2 + jnp.where(lane == 2, scalars, 0.0)),
    )
    lane = iota((8, 128), 1)
    res = jnp.zeros((8, 128), F32)
    for i in range(3):
        res = jnp.where(lane == i, dots[i], res)
    for z in range(NZ):
        out[z] = res[:4]


def finish_kernel(pos, got, scalar, pre, smooth, stack, s_ref, out):
    x, b = pos[1], pos[2]
    sums = got[0]
    for z in range(1, NZ):
        sums = sums + got[z]
    renewed, energy, cross = sums[:, 0:1], sums[:, 1:2], sums[:, 2:3]
    weight, first_energy, step = scalar[:4, 0:1], scalar[:4, 1:2], scalar[:4, 2:3]
    ratio = renewed / weight
    second = renewed / (energy + 2.0 * ratio * cross + ratio * ratio * first_energy)
    own = s_ref[b]
    mains = [spread_rows(own, x, kr) for kr in range(4)]
    mask = stack[7]
    for m in range(M):
        spread = jnp.concatenate([jnp.broadcast_to(v[m : m + 1], (8, 128)) for v in mains], axis=0)
        z1 = smooth[m] + mask * spread
        z0 = pre[m]
        out[m] = step[m : m + 1] * z0 + second[m : m + 1] * (z1 + ratio[m : m + 1] * z0)


def shift(value, axes, count, by):
    return lax.ppermute(value, axes, [(i, (i + by) % count) for i in range(count)])


def ring_window(value):
    before, after = shift(value, "z", NZ, 1), shift(value, "z", NZ, -1)
    return [shift(before, "z", NZ, 1), before, value, after, shift(after, "z", NZ, -1)]


def to_all(value, axes, count):
    return lax.all_to_all(jnp.broadcast_to(value[None], (count,) + value.shape), axes, 0, 0)


def body(right_side, diagonal, east_face, north_face, wet, active, coupling, pivots):
    stack, tile, rims = call(
        start_kernel,
        [(8, ROWS, COLS), (48, 128), (2, 24, 128)],
        right_side, diagonal, east_face, north_face, wet, active[0], coupling[0, 0],
        fetch=range(7),
        room=FETCH_BYTES,
    )
    window = ring_window(tile)
    (plane,) = call(gather_kernel, [(NX * 4, 152, 128)], *window, rims, fetch=(2, 5))
    plane = lax.all_to_all(plane, ("x", "y"), 0, 0)
    blocks = to_all(plane, "c", 2).reshape(32, 152, 128)

    pivot_rows = ring_window(pivots[0])

    ring, rim = (NZ, NG, 4, 128), (M, EXT_ROWS, EXT_COLS)
    weights = ((NB * NG, 128, 128), BF16)
    ext, consts, early = call(
        fields_kernel, [rim, (7, EXT_ROWS, EXT_COLS), (2, 8, 128)], stack, blocks
    )
    swept, coarse_right, acts, w_hi, w_lo = call(
        forward_kernel, [(NZ, 4, 128), (64, 128), (3, 64, 128), weights, weights], blocks
    )
    swept, early, pivot_rows = lax.optimization_barrier((swept, early, pivot_rows))
    got = lax.all_to_all(swept, "z", 0, 0)
    (message,) = call(pivot_kernel, [(32, 4, 384)], got, early, *pivot_rows)
    got = lax.all_to_all(message, ("x", "y", "c"), 0, 0)
    swept, s0, coarse_image, t = call(
        middle_kernel, [ring, (3, 64, 128), (64, 128), (5, 64, 128)], got, w_hi, w_lo, coarse_right, acts
    )
    pre, image = call(image_kernel, [(M, ROWS, COLS), rim], ext, consts, s0.reshape(3, NB, 8, 128))
    swept, pre, image = lax.optimization_barrier((swept, pre, image))
    got = lax.all_to_all(swept, "z", 0, 0)
    message, smooth, scalar = call(
        step_kernel, [(32, 4, 256), (M, ROWS, COLS), (8, 128)], got, ext, consts, image, *pivot_rows
    )
    got = lax.all_to_all(message, ("x", "y", "c"), 0, 0)
    dots, s1 = call(
        last_kernel, [(NZ, 4, 128), (64, 128)], got, w_hi, w_lo, s0, coarse_right, coarse_image, t, acts, scalar
    )
    got = lax.all_to_all(dots, "z", 0, 0)
    (out,) = call(finish_kernel, [(M, ROWS, COLS)], got, scalar, pre, smooth, stack, s1.reshape(NB, 8, 128))
    return out


def solution(mesh):
    fine = Mesh(mesh.devices.reshape(NZ, NX, 4, 2), ("z", "x", "y", "c"))
    lat, lon = ("y", "c"), ("z", "x")
    in_specs = (
        P(None, lat, lon),
        P(lat, lon),
        P(lat, lon),
        P(lat, lon),
        P(lat, lon),
        P(lat, lon, None),
        P(lat, lon, None, None, None),
        P(lat, lon, None),
    )
    return jax.shard_map(body, mesh=fine, in_specs=in_specs, out_specs=P(None, lat, lon), check_vma=False)
```

```python
import jax
import jax.numpy as jnp
from jax import lax
from jax.experimental import pallas as pl
from jax.experimental.pallas import tpu as pltpu
from jax.sharding import Mesh
from jax.sharding import PartitionSpec as P

F32 = jnp.float32
BF16 = jnp.bfloat16
M = 4
NB = 8
NX = 4
NZ = 16
NG = 5
ROWS = 32
COLS = 128
HALO = 3
EXT_ROWS = 40
EXT_COLS = 256
NT = (((1,), (1,)), ((), ()))
NN = (((1,), (0,)), ((), ()))
VMEM_BYTES = 12 * 1024 * 1024
FETCH_BYTES = 63 * 1024 * 1024


def call(kernel, outs, *arrays, fetch=(), room=VMEM_BYTES):
    outs = [o if o[1] == BF16 else (o, F32) for o in outs]
    vmem, hbm = pl.BlockSpec(memory_space=pltpu.VMEM), pl.BlockSpec(memory_space=pltpu.HBM)
    n, count = len(arrays), len(fetch)

    def whole(*refs):
        given, rest, held = list(refs[:n]), refs[n : n + len(outs)], refs[n + len(outs) :]
        copies = [pltpu.make_async_copy(given[i], held[j], held[count].at[j]) for j, i in enumerate(fetch)]
        for copy in copies:
            copy.start()
        for copy in copies:
            copy.wait()
        for j, i in enumerate(fetch):
            given[i] = held[j]
        z, x = lax.axis_index("z"), lax.axis_index("x")
        b = 2 * lax.axis_index("y") + lax.axis_index("c")
        kernel((z, x, b), *given, *rest)

    scratch = [pltpu.VMEM(arrays[i].shape, arrays[i].dtype) for i in fetch]
    if fetch:
        scratch.append(pltpu.SemaphoreType.DMA((count,)))
    return pl.pallas_call(
        whole,
        out_shape=[jax.ShapeDtypeStruct(s, d) for s, d in outs],
        in_specs=[hbm if i in fetch else vmem for i in range(n)],
        out_specs=[vmem] * len(outs),
        scratch_shapes=scratch,
        compiler_params=pltpu.CompilerParams(vmem_limit_bytes=room),
    )(*arrays)


def iota(shape, dim):
    return lax.broadcasted_iota(jnp.int32, shape, dim)


def roll(value, shift, axis):
    shift = shift % value.shape[axis]
    return value if shift == 0 else pltpu.roll(value, shift, axis)


def mm(a, b, dims):
    return lax.dot_general(a, b, dims, preferred_element_type=F32)


def halves(value):
    hi = value.astype(BF16)
    return hi, (value - hi.astype(F32)).astype(BF16)


def dot3(a, b_hi, b_lo, dims):
    hi = a.astype(BF16).astype(F32)
    both = jnp.concatenate([hi, a - hi], axis=0).astype(BF16)
    n = a.shape[0]
    top = mm(both, b_hi, dims)
    low = mm(both, b_lo, dims)
    return top[:n] + top[n:] + low[:n]


def dot_exact(a, b):
    hi = a.astype(BF16).astype(F32)
    rest = a - hi
    mid = rest.astype(BF16).astype(F32)
    parts = jnp.concatenate([hi, mid, rest - mid], axis=0).astype(BF16)
    out = mm(parts, b, NN)
    n = a.shape[0]
    return out[:n] + out[n : 2 * n] + out[2 * n :]


def lane_group():
    return iota((8, 128), 1) // 32


def pick(values):
    group = lane_group()
    out = values[-1]
    for i in range(len(values) - 2, -1, -1):
        out = jnp.where(group == i, values[i], out)
    return out


def block_sums(fields):
    rows = [jnp.sum(f.reshape(4, 8, COLS), axis=1) for f in fields]
    stacked = jnp.concatenate(rows, axis=0)
    pad = -stacked.shape[0] % 16
    if pad:
        stacked = jnp.concatenate([stacked, jnp.zeros((pad, COLS), F32)], axis=0)
    gather = (iota((COLS, COLS), 0) // 16 == iota((COLS, COLS), 1) % 8).astype(F32).astype(BF16)
    sums = dot_exact(stacked, gather)
    kr = (iota((1, COLS), 1) // 8) % 4
    out = []
    for i in range(len(fields)):
        row = jnp.zeros((1, COLS), F32)
        for j in range(4):
            row = jnp.where(kr == j, sums[4 * i + j : 4 * i + j + 1], row)
        out.append(row)
    return out


def member_rows(rows):
    sub = iota((8, 128), 0)
    out = jnp.zeros((8, 128), F32)
    for m, row in enumerate(rows):
        out = jnp.where(sub == m, row, out)
    return out


def full_sum(value):
    return jnp.sum(jnp.sum(value, axis=1, keepdims=True), axis=0, keepdims=True)


def operate(v, fields):
    fe, fw, fn, fs, centre = fields
    return (
        centre * v
        + fe * (v - roll(v, -1, 1))
        + fw * (v - roll(v, 1, 1))
        + fn * (v - roll(v, -1, 0))
        + fs * (v - roll(v, 1, 0))
    )


def main(value):
    return value[:ROWS, :COLS]


def start_kernel(pos, right, diag, east, north, wet, active, coupling, stack, tile, rims):
    mask = wet[...].astype(F32)
    act = jnp.concatenate([jnp.broadcast_to(active[...].astype(F32), (8, 32))] * 4, axis=1)
    fields = [right[m] for m in range(M)] + [diag[...], east[...], north[...], mask]
    for f, v in enumerate(fields):
        stack[f] = v
    tail = jnp.concatenate([coupling[e, 24:, :] for e in range(3)], axis=0)
    tile[:24, :] = jnp.concatenate([coupling[e, :24, :] for e in range(3)] + [tail], axis=1)
    every = jnp.concatenate(fields, axis=0)
    hi = every.astype(BF16).astype(F32)
    mid = (every - hi).astype(BF16).astype(F32)
    parts = jnp.concatenate([hi, mid, every - hi - mid], axis=0).astype(BF16)
    row, lane = iota((16, COLS), 0), iota((16, COLS), 1)
    column = jnp.where(row < 8, row, row - 8 + COLS - HALO)
    chosen = jnp.logical_and(lane == column, row % 8 < HALO).astype(F32).astype(BF16)
    columns = mm(chosen, parts, NT)
    columns = columns[:, :256] + columns[:, 256:512] + columns[:, 512:]
    upper = iota((8, 128), 0) >= 4
    for i in range(2):
        part = columns[8 * i : 8 * i + 8]
        tile[32 + 8 * i : 40 + 8 * i, :] = jnp.where(upper, roll(part[:, 128:], 4, 0), part[:, :128])
    for i, start in enumerate((0, ROWS - HALO)):
        rims[i] = jnp.concatenate([v[start + j : start + j + 1] for j in range(HALO) for v in fields], axis=0)
    rows = block_sums([fields[m] * mask for m in range(M)])
    packed = pick([jnp.broadcast_to(r, (8, 128)) for r in rows]) * act
    row = iota((8, 128), 0)
    tile[24:32, :] = jnp.where(row == 0, packed, jnp.where(row == 1, act, 0.0))


def own_kernel(pos, tile, rims, tile_out, rims_out):
    tile_out[...] = tile[...]
    rims_out[...] = rims[...]


def gather_kernel(pos, t0, t1, t2, t3, t4, rims, out):
    x, y, c = pos[1], lax.div(pos[2], 2), lax.rem(pos[2], 2)
    onward = jnp.where(x == NX - 1, t1[40:48, :], t2[40:48, :])
    back = jnp.where(x == 0, t3[32:40, :], t2[32:40, :])
    tiles = (t0, t1, t2, t3, t4)
    rows = [t[:24, :] for t in tiles] + [t[24:25, :] for t in tiles] + [t[25:26, :] for t in (t1, t2, t3)]
    rows = jnp.concatenate(rows, axis=0)
    far = jnp.where(c == 0, rims[0], rims[1])
    near = jnp.where(c == 0, rims[1], rims[0])
    for d in range(NX * 4):
        out[d, :128, :] = rows
        rim = jnp.where(y == d % 4, near, far)
        out[d, 136:, :] = rim[8:]
        columns = jnp.where(lax.rem(x + 1, NX) == d // 4, onward, back)
        out[d, 128:136, :] = jnp.where(x == d // 4, rim[:8], columns)


def side(blocks, band, sender, rows=8):
    return blocks[lax.rem(band, 2) * 16 + sender * 4 + lax.div(band, 2), 128 : 128 + rows, :]


def fields_kernel(pos, stack, blocks, ext, consts, early):
    x, b = pos[1], pos[2]
    after, before = lax.rem(x + 1, NX), lax.rem(x + NX - 1, NX)
    up, down = lax.rem(b + 1, NB), lax.rem(b + NB - 1, NB)
    north_rows, south_rows = side(blocks, up, x, 24), side(blocks, down, x, 24)
    sub = iota((8, 128), 0)
    sides = []
    for band in (b, up, down):
        sides += [side(blocks, band, after), side(blocks, band, before)]
    turned = jnp.transpose(jnp.concatenate(sides + [jnp.zeros((80, 128), F32)], axis=0))
    first = iota((8, 128), 0) < 4

    def columns(rows, slot, h):
        lane = iota(rows.shape, 1)
        east_part = roll(rows, -(16 * slot + 4 * h), 1)
        west_part = roll(rows, 128 - HALO - (16 * slot + 8 + 4 * h), 1)
        return jnp.where(lane < HALO, east_part, jnp.where(lane >= 128 - HALO, west_part, 0.0))

    fields = []
    for f in range(8):
        rows = turned[32 * (f % 4) : 32 * (f % 4) + 32]
        h = f // 4
        corner = jnp.where(first, columns(rows[:8], 1, h), columns(rows[24:], 2, h))
        beyond = jnp.zeros((8, 128), F32)
        for j in range(HALO):
            at = 8 * j + f
            beyond = jnp.where(sub == j, north_rows[at : at + 1], beyond)
            beyond = jnp.where(sub == 8 - HALO + j, south_rows[at : at + 1], beyond)
        left = jnp.concatenate([stack[f], beyond], axis=0)
        right = jnp.concatenate([columns(rows, 0, h), corner], axis=0)
        fields.append(jnp.concatenate([left, right], axis=1))
    for m in range(M):
        ext[m] = fields[m]
    diag, east, north, wet = fields[4:]
    row = iota((EXT_ROWS, EXT_COLS), 0)
    grid_row = b * ROWS + jnp.where(row >= 36, row - EXT_ROWS, row)
    inside = jnp.logical_and(grid_row >= 0, grid_row < NB * ROWS - 1)
    fe = east * wet * roll(wet, -1, 1)
    fw = roll(fe, 1, 1)
    fn = jnp.where(inside, north * wet * roll(wet, -1, 0), 0.0)
    fs = roll(fn, 1, 0)
    own = wet * diag
    centre = own + (1.0 - wet)
    inverse = 1.0 / (centre + fe + fw + fn + fs)
    for i, v in enumerate((fe, fw, fn, fs, centre, inverse, wet)):
        consts[i] = v
    mask = main(wet)
    row = iota((ROWS, COLS), 0)
    col = iota((ROWS, COLS), 1)
    sums = [
        jnp.where(col % 16 == 15, main(fe), 0.0),
        jnp.where(col % 16 == 0, main(fw), 0.0),
        jnp.where(row % 8 == 7, main(fn), 0.0),
        jnp.where(row % 8 == 0, main(fs), 0.0),
        main(own),
    ]
    energy, smooth = [], []
    for m in range(M):
        r = fields[m]
        y = inverse * r
        image = main(operate(y, (fe, fw, fn, fs, centre)))
        sums.append(mask * image)
        energy.append(full_sum(main(y) * image))
        smooth.append(full_sum(main(y) * main(r)))
    rows = block_sums(sums)
    lane = iota((8, 128), 1) % 32
    scalars = jnp.where(lane == 0, member_rows(energy), jnp.where(lane == 1, member_rows(smooth), 0.0))
    early[0] = pick([member_rows(rows[5:])] * 2 + [jnp.broadcast_to(rows[0], (8, 128)), jnp.broadcast_to(rows[1], (8, 128))])
    early[1] = pick([jnp.broadcast_to(rows[i], (8, 128)) for i in (2, 3, 4)] + [scalars])


def unpack_tile(tile, x):
    group = iota((24, 128), 1) // 32
    top = roll(jnp.where(group < 3, tile, 0.0), 32 * (x - 1), 1)
    group = lane_group()
    rest = jnp.zeros((8, 128), F32)
    for e in range(3):
        to = (e + x - 1) % 4
        rest = jnp.where(group == to, roll(tile[8 * e : 8 * e + 8], 32 * (to - 3), 1), rest)
    return jnp.concatenate([top, rest], axis=0)


def unpack_weights(blocks, b, g):
    c, y = b % 2, b // 2
    tiles = [unpack_tile(blocks[c * 16 + x * 4 + y, 24 * g : 24 * g + 24, :], x) for x in range(NX)]
    return halves(jnp.concatenate(tiles, axis=0))


def forward_sweep(coarse, weights, mine, live):
    group = lane_group()
    zero = jnp.zeros((8, 128), F32)
    s = [zero if v is None else v for v in coarse[0]]
    out = s
    for b in range(1, NB):
        new = []
        for g in range(NG):
            if not live(b, g):
                new.append(zero)
                continue
            left = s[g - 1] if g > 0 else zero
            right = s[g + 1] if g < NG - 1 else zero
            lhs = jnp.concatenate(
                [jnp.where(group == 3, left, s[g]), s[g], s[g], jnp.where(group == 0, right, s[g])], axis=0
            )
            hi, lo = weights(b, g)
            o = dot3(lhs, hi, lo, NT)
            carried = pick([o[8 * x : 8 * x + 8] for x in range(NX)])
            new.append(-carried if coarse[b][g] is None else coarse[b][g] - carried)
        s = new
        out = [jnp.where(mine == b, s[g], out[g]) for g in range(NG)]
    return out


def distance(g):
    return max(0, 4 * abs(g - 2) - 4) if g != 2 else -1


def inward(b, g):
    return distance(g) < NB - 1 - b


def outward(b, g):
    return distance(g) < b


def rimward(b, g):
    return distance(g) < b + 1


def backward_sweep(pivoted, weights):
    group = lane_group()
    zero = jnp.zeros((8, 128), F32)
    s = pivoted[NB - 1]
    out = [None] * NB
    out[NB - 1] = s
    for b in range(NB - 2, -1, -1):
        o = []
        for g in range(NG):
            if not rimward(b + 1, g):
                o.append(None)
                continue
            lhs = jnp.concatenate([jnp.where(group == x, s[g], 0.0) for x in range(NX)], axis=0)
            hi, lo = weights(b + 1, g)
            o.append(dot3(lhs, hi, lo, NN))
        s = []
        for g in range(NG):
            if o[g] is None or not rimward(b, g):
                s.append(zero)
                continue
            own = o[g][8:16] + o[g][16:24]
            own = own + jnp.where(group == 3, 0.0, o[g][0:8]) + jnp.where(group == 0, 0.0, o[g][24:32])
            after = o[g + 1][0:8] if g < NG - 1 and o[g + 1] is not None else zero
            before = o[g - 1][24:32] if g > 0 and o[g - 1] is not None else zero
            own = own + jnp.where(group == 3, after, 0.0) + jnp.where(group == 0, before, 0.0)
            s.append(pivoted[b][g] - own)
        out[b] = s
    return out


def pack_window(s, extra, out):
    parts = [jnp.where(lane_group() == 0, extra, s[0])] + list(s[1:])
    for g in range(NG):
        rows = parts[g][:4]
        for z in range(NZ):
            out[z, g] = rows


def to_plane(values, out):
    for d in range(NX * NB):
        for i, v in enumerate(values):
            out[d, :, 128 * i : 128 * i + 128] = v[:4]


def unpack_swept(got):
    if len(got.shape) == 3:
        out = [got[z] for z in range(NZ)]
    else:
        reached = iota((4, 128), 1) >= 32
        out = []
        for z in range(NZ):
            acc = jnp.where(reached, got[(z + 2) % NZ, 0], 0.0)
            for g in range(1, NG):
                acc = acc + got[(z + 2 - g) % NZ, g]
            out.append(acc)
    out = jnp.concatenate(out, axis=1)
    return jnp.concatenate([out, jnp.zeros_like(out)], axis=0)


def pivot_product(swept, pivots):
    rows = jnp.concatenate([p[...] for p in pivots], axis=0)
    hi, lo = halves(rows)
    out = dot3(swept, hi, lo, NT)
    return out[:, :128], jnp.concatenate([out[:, 128:160]] * 4, axis=1)


def unpack_plane(got, field):
    group = iota((64, 128), 1) // 32
    half = field // 4 * 128
    out = None
    for x in range(NX):
        bands = [got[x * NB + b, :, half : half + 128] for b in range(NB)]
        bands = [jnp.concatenate([v, jnp.zeros_like(v)], axis=0) for v in bands]
        piece = roll(jnp.concatenate(bands, axis=0), 32 * (x - field % 4), 1)
        out = piece if out is None else jnp.where(group == x, piece, out)
    return out


def coarse_operate(s, before, after, t):
    fe, fw, fn, fs, dg = t
    lane = iota((64, 128), 1)
    kc, kr = lane % 8, (lane // 8) % 4
    east = jnp.where(kc < 7, roll(s, -1, 1), jnp.where(lane < 96, roll(s, -25, 1), roll(after, -25, 1)))
    west = jnp.where(kc > 0, roll(s, 1, 1), jnp.where(lane >= 32, roll(s, 25, 1), roll(before, 25, 1)))
    north = jnp.where(kr < 3, roll(s, -8, 1), roll(roll(s, 24, 1), -8, 0))
    south = jnp.where(kr > 0, roll(s, 8, 1), roll(roll(s, -24, 1), 8, 0))
    return dg * s + fe * (s - east) + fw * (s - west) + fn * (s - north) + fs * (s - south)


def band_sum(value):
    acc = value[0:8]
    for b in range(1, NB):
        acc = acc + value[8 * b : 8 * b + 8]
    return jnp.sum(acc, axis=1, keepdims=True)


def stored(w_hi, w_lo):
    return lambda b, g: (w_hi[b * NG + g], w_lo[b * NG + g])


def plane_rows(blocks, at):
    return [
        jnp.concatenate([blocks[b % 2 * 16 + x * 4 + b // 2, at : at + 1, :] for b in range(NB)], axis=0) for x in range(NX)
    ]


def forward_kernel(pos, blocks, out, coarse_out, acts_out, w_hi, w_lo):
    coarse = [[] for _ in range(NB)]
    for g in range(NG):
        rows = plane_rows(blocks, 120 + g)
        members = [pick([roll(rows[x], 32 * (x - m), 1) for x in range(NX)]) for m in range(M)]
        for b in range(NB):
            coarse[b].append(member_rows([v[b : b + 1] for v in members]))
    for b in range(NB):
        coarse_out[8 * b : 8 * b + 8, :] = coarse[b][2]
    for i in range(3):
        act = pick(plane_rows(blocks, 125 + i))
        for b in range(NB):
            acts_out[i, 8 * b : 8 * b + 8, :] = jnp.broadcast_to(act[b : b + 1], (8, 128))

    def weights(b, g):
        hi, lo = unpack_weights(blocks, b, g)
        w_hi[b * NG + g] = hi
        w_lo[b * NG + g] = lo
        return hi, lo

    for b in range(1, NB):
        for g in range(NG):
            if not inward(b, g) and (rimward(b, g) or outward(b, g)):
                weights(b, g)
    own = forward_sweep(coarse, weights, pos[2], inward)[2][:4]
    for z in range(NZ):
        out[z] = own


def pivot_kernel(pos, got, early, p0, p1, p2, p3, p4, out):
    first, last = pivot_product(unpack_swept(got), (p0, p1, p2, p3, p4))
    to_plane([first, jnp.where(lane_group() == 0, last, early[0]), early[1]], out)


def middle_kernel(pos, got, w_hi, w_lo, coarse_right, acts, out, s_out, coarse_image_out, t_out):
    windows = [unpack_plane(got, f) for f in range(12)]
    pivoted = [[windows[g][8 * b : 8 * b + 8] for g in range(NG)] for b in range(NB)]
    settled = backward_sweep(pivoted, stored(w_hi, w_lo))
    s1, s2, s3 = (
        jnp.concatenate([settled[b][g] for b in range(NB)], axis=0) * acts[g - 1] for g in (1, 2, 3)
    )
    smooth, t, scalars = windows[5], windows[6:11], windows[11]
    t_s = coarse_operate(s2, s1, s3, t)
    coarse_image = acts[1] * (smooth + t_s)
    lane = iota((64, 128), 1) % 32
    weight = band_sum(coarse_right[...] * s2 + jnp.where(lane == 1, scalars, 0.0))
    energy = band_sum((2.0 * smooth + t_s) * s2 + jnp.where(lane == 0, scalars, 0.0))
    lane = iota((8, 128), 1)
    extra = jnp.where(lane == 0, weight, jnp.where(lane == 1, energy, 0.0))
    for i, v in enumerate((s1, s2, s3)):
        s_out[i] = v
    coarse_image_out[...] = coarse_image
    for i, v in enumerate(t):
        t_out[i] = v
    coarse = [[None, None, coarse_image[8 * b : 8 * b + 8], None, None] for b in range(NB)]
    pack_window(forward_sweep(coarse, stored(w_hi, w_lo), pos[2], outward), extra, out)


def spread_rows(s, x, kr):
    lane = iota((8, 128), 1)
    return jnp.take_along_axis(s, x * 32 + kr * 8 + lane // 16, axis=1)


def spread_sides(s1, s2, s3, x, kr):
    lane = iota((8, 128), 1)
    east = jnp.take_along_axis(jnp.where(x < 3, s2, s3), jnp.zeros_like(lane) + lax.rem(x + 1, 4) * 32 + kr * 8, axis=1)
    west = jnp.take_along_axis(jnp.where(x > 0, s2, s1), jnp.zeros_like(lane) + lax.rem(x + 3, 4) * 32 + kr * 8 + 7, axis=1)
    return jnp.where(lane < 64, east, west)


def image_kernel(pos, ext, consts, s_ref, pre_out, image_out):
    x, b = pos[1], pos[2]
    north_band, south_band = lax.rem(b + 1, NB), lax.rem(b + NB - 1, NB)
    own = [s_ref[g, b] for g in range(3)]
    up = [s_ref[g, north_band] for g in range(3)]
    down = [s_ref[g, south_band] for g in range(3)]
    mains = [spread_rows(own[1], x, kr) for kr in range(4)]
    sides = [spread_sides(*own, x, kr) for kr in range(4)]
    first = iota((8, 128), 0) < 4
    up_main, up_side = spread_rows(up[1], x, 0), spread_sides(*up, x, 0)
    down_main, down_side = spread_rows(down[1], x, 3), spread_sides(*down, x, 3)
    fields = tuple(consts[i] for i in range(5))
    inverse, wet = consts[5], consts[6]
    for m in range(M):
        wide = lambda v: jnp.broadcast_to(v[m : m + 1], (8, 128))
        left = [wide(v) for v in mains] + [jnp.where(first, wide(up_main), wide(down_main))]
        right = [wide(v) for v in sides] + [jnp.where(first, wide(up_side), wide(down_side))]
        spread = jnp.concatenate([jnp.concatenate(left, axis=0), jnp.concatenate(right, axis=0)], axis=1)
        pre = inverse * ext[m] + wet * spread
        pre_out[m] = main(pre)
        image_out[m] = operate(pre, fields)


def step_kernel(pos, got, ext, consts, image, p0, p1, p2, p3, p4, out, smooth_out, scalar_out):
    first, last = pivot_product(unpack_swept(got), (p0, p1, p2, p3, p4))
    sums = got[0, 0]
    for z in range(1, NZ):
        sums = sums + got[z, 0]
    sums = jnp.concatenate([sums, jnp.ones_like(sums)], axis=0)
    weight, energy = sums[:, 0:1], sums[:, 1:2]
    step = weight / energy
    fields = tuple(consts[i] for i in range(5))
    inverse, wet = consts[5], consts[6]
    mask = main(wet)
    blocks, dots = [], ([], [], [])
    for m in range(M):
        residual = ext[m] - step[m : m + 1] * image[m]
        smooth = inverse * residual
        applied = main(operate(smooth, fields))
        smooth = main(smooth)
        smooth_out[m] = smooth
        blocks.append(mask * applied)
        dots[0].append(full_sum(smooth * main(residual)))
        dots[1].append(full_sum(smooth * applied))
        dots[2].append(full_sum(smooth * main(image[m])))
    rows = member_rows(block_sums(blocks))
    lane = iota((8, 128), 1) % 32
    scalars = jnp.zeros((8, 128), F32)
    for i in range(3):
        scalars = jnp.where(lane == i, member_rows(dots[i]), scalars)
    to_plane([first, pick([last, rows, scalars, jnp.zeros((8, 128), F32)])], out)
    lane = iota((8, 128), 1)
    scalar_out[...] = jnp.where(lane == 0, weight, jnp.where(lane == 1, energy, jnp.where(lane == 2, step, 0.0)))


def last_kernel(pos, got, w_hi, w_lo, s_ref, coarse_right, coarse_image, t_ref, acts, scalar, out, s_out):
    windows = [unpack_plane(got, f) for f in range(7)]
    pivoted = [[windows[g][8 * b : 8 * b + 8] for g in range(NG)] for b in range(NB)]
    settled = backward_sweep(pivoted, stored(w_hi, w_lo))
    t = tuple(t_ref[i] for i in range(5))
    step = jnp.concatenate([scalar[:, 2:3]] * NB, axis=0)
    s1, s2, s3 = (
        s_ref[g - 1] - step * (jnp.concatenate([settled[b][g] for b in range(NB)], axis=0) * acts[g - 1])
        for g in (1, 2, 3)
    )
    s_out[...] = s2
    t_s = coarse_operate(s2, s1, s3, t)
    smooth, scalars = windows[5], windows[6]
    lane = iota((64, 128), 1) % 32
    dots = (
        band_sum((coarse_right[...] - step * coarse_image[...]) * s2 + jnp.where(lane == 0, scalars, 0.0)),
        band_sum((2.0 * smooth + t_s) * s2 + jnp.where(lane == 1, scalars, 0.0)),
        band_sum(coarse_image[...] * s2 + jnp.where(lane == 2, scalars, 0.0)),
    )
    lane = iota((8, 128), 1)
    res = jnp.zeros((8, 128), F32)
    for i in range(3):
        res = jnp.where(lane == i, dots[i], res)
    for z in range(NZ):
        out[z] = res[:4]


def finish_kernel(pos, got, scalar, pre, smooth, stack, s_ref, out):
    x, b = pos[1], pos[2]
    sums = got[0]
    for z in range(1, NZ):
        sums = sums + got[z]
    renewed, energy, cross = sums[:, 0:1], sums[:, 1:2], sums[:, 2:3]
    weight, first_energy, step = scalar[:4, 0:1], scalar[:4, 1:2], scalar[:4, 2:3]
    ratio = renewed / weight
    second = renewed / (energy + 2.0 * ratio * cross + ratio * ratio * first_energy)
    own = s_ref[b]
    mains = [spread_rows(own, x, kr) for kr in range(4)]
    mask = stack[7]
    for m in range(M):
        spread = jnp.concatenate([jnp.broadcast_to(v[m : m + 1], (8, 128)) for v in mains], axis=0)
        z1 = smooth[m] + mask * spread
        z0 = pre[m]
        out[m] = step[m : m + 1] * z0 + second[m : m + 1] * (z1 + ratio[m : m + 1] * z0)


def shift(value, axes, count, by):
    return lax.ppermute(value, axes, [(i, (i + by) % count) for i in range(count)])


def ring_window(value):
    before, after = shift(value, "z", NZ, 1), shift(value, "z", NZ, -1)
    return [shift(before, "z", NZ, 1), before, value, after, shift(after, "z", NZ, -1)]


def to_all(value, axes, count):
    return lax.all_to_all(jnp.broadcast_to(value[None], (count,) + value.shape), axes, 0, 0)


def body(right_side, diagonal, east_face, north_face, wet, active, coupling, pivots):
    stack, tile, rims = call(
        start_kernel,
        [(8, ROWS, COLS), (48, 128), (2, 24, 128)],
        right_side, diagonal, east_face, north_face, wet, active[0], coupling[0, 0],
        fetch=range(7),
        room=FETCH_BYTES,
    )
    window = ring_window(tile)
    window[2], rims = call(own_kernel, [(48, 128), (2, 24, 128)], tile, rims)
    (plane,) = call(gather_kernel, [(NX * 4, 152, 128)], *window, rims)
    plane = lax.all_to_all(plane, ("x", "y"), 0, 0)
    blocks = to_all(plane, "c", 2).reshape(32, 152, 128)

    pivot_rows = ring_window(pivots[0])

    ring, rim = (NZ, NG, 4, 128), (M, EXT_ROWS, EXT_COLS)
    weights = ((NB * NG, 128, 128), BF16)
    ext, consts, early = call(
        fields_kernel, [rim, (7, EXT_ROWS, EXT_COLS), (2, 8, 128)], stack, blocks
    )
    swept, coarse_right, acts, w_hi, w_lo = call(
        forward_kernel, [(NZ, 4, 128), (64, 128), (3, 64, 128), weights, weights], blocks
    )
    swept, early, pivot_rows = lax.optimization_barrier((swept, early, pivot_rows))
    got = lax.all_to_all(swept, "z", 0, 0)
    (message,) = call(pivot_kernel, [(32, 4, 384)], got, early, *pivot_rows)
    got = lax.all_to_all(message, ("x", "y", "c"), 0, 0)
    swept, s0, coarse_image, t = call(
        middle_kernel, [ring, (3, 64, 128), (64, 128), (5, 64, 128)], got, w_hi, w_lo, coarse_right, acts
    )
    pre, image = call(image_kernel, [(M, ROWS, COLS), rim], ext, consts, s0.reshape(3, NB, 8, 128))
    swept, pre, image = lax.optimization_barrier((swept, pre, image))
    got = lax.all_to_all(swept, "z", 0, 0)
    message, smooth, scalar = call(
        step_kernel, [(32, 4, 256), (M, ROWS, COLS), (8, 128)], got, ext, consts, image, *pivot_rows
    )
    got = lax.all_to_all(message, ("x", "y", "c"), 0, 0)
    dots, s1 = call(
        last_kernel, [(NZ, 4, 128), (64, 128)], got, w_hi, w_lo, s0, coarse_right, coarse_image, t, acts, scalar
    )
    got = lax.all_to_all(dots, "z", 0, 0)
    (out,) = call(finish_kernel, [(M, ROWS, COLS)], got, scalar, pre, smooth, stack, s1.reshape(NB, 8, 128))
    return out


def solution(mesh):
    fine = Mesh(mesh.devices.reshape(NZ, NX, 4, 2), ("z", "x", "y", "c"))
    lat, lon = ("y", "c"), ("z", "x")
    in_specs = (
        P(None, lat, lon),
        P(lat, lon),
        P(lat, lon),
        P(lat, lon),
        P(lat, lon),
        P(lat, lon, None),
        P(lat, lon, None, None, None),
        P(lat, lon, None),
    )
    return jax.shard_map(body, mesh=fine, in_specs=in_specs, out_specs=P(None, lat, lon), check_vma=False)
```

```python
import jax
import jax.numpy as jnp
from jax import lax
from jax.experimental import pallas as pl
from jax.experimental.pallas import tpu as pltpu
from jax.sharding import Mesh
from jax.sharding import PartitionSpec as P

F32 = jnp.float32
BF16 = jnp.bfloat16
M = 4
NB = 8
NX = 4
NZ = 16
NG = 5
ROWS = 32
COLS = 128
HALO = 3
EXT_ROWS = 40
EXT_COLS = 256
NT = (((1,), (1,)), ((), ()))
NN = (((1,), (0,)), ((), ()))
VMEM_BYTES = 12 * 1024 * 1024
FETCH_BYTES = 63 * 1024 * 1024


def call(kernel, outs, *arrays, fetch=(), room=VMEM_BYTES):
    outs = [o if o[1] == BF16 else (o, F32) for o in outs]
    vmem, hbm = pl.BlockSpec(memory_space=pltpu.VMEM), pl.BlockSpec(memory_space=pltpu.HBM)
    n, count = len(arrays), len(fetch)

    def whole(*refs):
        given, rest, held = list(refs[:n]), refs[n : n + len(outs)], refs[n + len(outs) :]
        copies = [pltpu.make_async_copy(given[i], held[j], held[count].at[j]) for j, i in enumerate(fetch)]
        for copy in copies:
            copy.start()
        for copy in copies:
            copy.wait()
        for j, i in enumerate(fetch):
            given[i] = held[j]
        z, x = lax.axis_index("z"), lax.axis_index("x")
        b = 2 * lax.axis_index("y") + lax.axis_index("c")
        kernel((z, x, b), *given, *rest)

    scratch = [pltpu.VMEM(arrays[i].shape, arrays[i].dtype) for i in fetch]
    if fetch:
        scratch.append(pltpu.SemaphoreType.DMA((count,)))
    return pl.pallas_call(
        whole,
        out_shape=[jax.ShapeDtypeStruct(s, d) for s, d in outs],
        in_specs=[hbm if i in fetch else vmem for i in range(n)],
        out_specs=[vmem] * len(outs),
        scratch_shapes=scratch,
        compiler_params=pltpu.CompilerParams(vmem_limit_bytes=room),
    )(*arrays)


def iota(shape, dim):
    return lax.broadcasted_iota(jnp.int32, shape, dim)


def roll(value, shift, axis):
    shift = shift % value.shape[axis]
    return value if shift == 0 else pltpu.roll(value, shift, axis)


def mm(a, b, dims):
    return lax.dot_general(a, b, dims, preferred_element_type=F32)


def halves(value):
    hi = value.astype(BF16)
    return hi, (value - hi.astype(F32)).astype(BF16)


def dot3(a, b_hi, b_lo, dims):
    hi = a.astype(BF16).astype(F32)
    both = jnp.concatenate([hi, a - hi], axis=0).astype(BF16)
    n = a.shape[0]
    top = mm(both, b_hi, dims)
    low = mm(both, b_lo, dims)
    return top[:n] + top[n:] + low[:n]


def dot_exact(a, b):
    hi = a.astype(BF16).astype(F32)
    rest = a - hi
    mid = rest.astype(BF16).astype(F32)
    parts = jnp.concatenate([hi, mid, rest - mid], axis=0).astype(BF16)
    out = mm(parts, b, NN)
    n = a.shape[0]
    return out[:n] + out[n : 2 * n] + out[2 * n :]


def lane_group():
    return iota((8, 128), 1) // 32


def pick(values):
    group = lane_group()
    out = values[-1]
    for i in range(len(values) - 2, -1, -1):
        out = jnp.where(group == i, values[i], out)
    return out


def block_sums(fields):
    rows = [jnp.sum(f.reshape(4, 8, COLS), axis=1) for f in fields]
    stacked = jnp.concatenate(rows, axis=0)
    pad = -stacked.shape[0] % 16
    if pad:
        stacked = jnp.concatenate([stacked, jnp.zeros((pad, COLS), F32)], axis=0)
    gather = (iota((COLS, COLS), 0) // 16 == iota((COLS, COLS), 1) % 8).astype(F32).astype(BF16)
    sums = dot_exact(stacked, gather)
    kr = (iota((1, COLS), 1) // 8) % 4
    out = []
    for i in range(len(fields)):
        row = jnp.zeros((1, COLS), F32)
        for j in range(4):
            row = jnp.where(kr == j, sums[4 * i + j : 4 * i + j + 1], row)
        out.append(row)
    return out


def member_rows(rows):
    sub = iota((8, 128), 0)
    out = jnp.zeros((8, 128), F32)
    for m, row in enumerate(rows):
        out = jnp.where(sub == m, row, out)
    return out


def full_sum(value):
    return jnp.sum(jnp.sum(value, axis=1, keepdims=True), axis=0, keepdims=True)


def operate(v, fields):
    fe, fw, fn, fs, centre = fields
    return (
        centre * v
        + fe * (v - roll(v, -1, 1))
        + fw * (v - roll(v, 1, 1))
        + fn * (v - roll(v, -1, 0))
        + fs * (v - roll(v, 1, 0))
    )


def main(value):
    return value[:ROWS, :COLS]


def start_kernel(pos, right, diag, east, north, wet, active, coupling, stack, tile, rims):
    mask = wet[...].astype(F32)
    act = jnp.concatenate([jnp.broadcast_to(active[...].astype(F32), (8, 32))] * 4, axis=1)
    fields = [right[m] for m in range(M)] + [diag[...], east[...], north[...], mask]
    for f, v in enumerate(fields):
        stack[f] = v
    tail = jnp.concatenate([coupling[e, 24:, :] for e in range(3)], axis=0)
    tile[:24, :] = jnp.concatenate([coupling[e, :24, :] for e in range(3)] + [tail], axis=1)
    every = jnp.concatenate(fields, axis=0)
    hi = every.astype(BF16).astype(F32)
    mid = (every - hi).astype(BF16).astype(F32)
    parts = jnp.concatenate([hi, mid, every - hi - mid], axis=0).astype(BF16)
    row, lane = iota((16, COLS), 0), iota((16, COLS), 1)
    column = jnp.where(row < 8, row, row - 8 + COLS - HALO)
    chosen = jnp.logical_and(lane == column, row % 8 < HALO).astype(F32).astype(BF16)
    columns = mm(chosen, parts, NT)
    columns = columns[:, :256] + columns[:, 256:512] + columns[:, 512:]
    upper = iota((8, 128), 0) >= 4
    for i in range(2):
        part = columns[8 * i : 8 * i + 8]
        tile[32 + 8 * i : 40 + 8 * i, :] = jnp.where(upper, roll(part[:, 128:], 4, 0), part[:, :128])
    for i, start in enumerate((0, ROWS - HALO)):
        rims[i] = jnp.concatenate([v[start + j : start + j + 1] for j in range(HALO) for v in fields], axis=0)
    rows = block_sums([fields[m] * mask for m in range(M)])
    packed = pick([jnp.broadcast_to(r, (8, 128)) for r in rows]) * act
    row = iota((8, 128), 0)
    tile[24:32, :] = jnp.where(row == 0, packed, jnp.where(row == 1, act, 0.0))


def own_kernel(pos, tile, rims, tile_out, rims_out):
    tile_out[...] = tile[...]
    rims_out[...] = rims[...]


def gather_kernel(pos, t0, t1, t2, t3, t4, rims, out):
    x, y, c = pos[1], lax.div(pos[2], 2), lax.rem(pos[2], 2)
    onward = jnp.where(x == NX - 1, t1[40:48, :], t2[40:48, :])
    back = jnp.where(x == 0, t3[32:40, :], t2[32:40, :])
    tiles = (t0, t1, t2, t3, t4)
    rows = [t[:24, :] for t in tiles] + [t[24:25, :] for t in tiles] + [t[25:26, :] for t in (t1, t2, t3)]
    rows = jnp.concatenate(rows, axis=0)
    far = jnp.where(c == 0, rims[0], rims[1])
    near = jnp.where(c == 0, rims[1], rims[0])
    for d in range(NX * 4):
        out[d, :128, :] = rows
        rim = jnp.where(y == d % 4, near, far)
        out[d, 136:, :] = rim[8:]
        columns = jnp.where(lax.rem(x + 1, NX) == d // 4, onward, back)
        out[d, 128:136, :] = jnp.where(x == d // 4, rim[:8], columns)


def side(blocks, band, sender, rows=8):
    return blocks[lax.rem(band, 2) * 16 + sender * 4 + lax.div(band, 2), 128 : 128 + rows, :]


def fields_kernel(pos, stack, blocks, ext, consts, early):
    x, b = pos[1], pos[2]
    after, before = lax.rem(x + 1, NX), lax.rem(x + NX - 1, NX)
    up, down = lax.rem(b + 1, NB), lax.rem(b + NB - 1, NB)
    north_rows, south_rows = side(blocks, up, x, 24), side(blocks, down, x, 24)
    sub = iota((8, 128), 0)
    sides = []
    for band in (b, up, down):
        sides += [side(blocks, band, after), side(blocks, band, before)]
    turned = jnp.transpose(jnp.concatenate(sides + [jnp.zeros((80, 128), F32)], axis=0))
    first = iota((8, 128), 0) < 4

    def columns(rows, slot, h):
        lane = iota(rows.shape, 1)
        east_part = roll(rows, -(16 * slot + 4 * h), 1)
        west_part = roll(rows, 128 - HALO - (16 * slot + 8 + 4 * h), 1)
        return jnp.where(lane < HALO, east_part, jnp.where(lane >= 128 - HALO, west_part, 0.0))

    fields = []
    for f in range(8):
        rows = turned[32 * (f % 4) : 32 * (f % 4) + 32]
        h = f // 4
        corner = jnp.where(first, columns(rows[:8], 1, h), columns(rows[24:], 2, h))
        beyond = jnp.zeros((8, 128), F32)
        for j in range(HALO):
            at = 8 * j + f
            beyond = jnp.where(sub == j, north_rows[at : at + 1], beyond)
            beyond = jnp.where(sub == 8 - HALO + j, south_rows[at : at + 1], beyond)
        left = jnp.concatenate([stack[f], beyond], axis=0)
        right = jnp.concatenate([columns(rows, 0, h), corner], axis=0)
        fields.append(jnp.concatenate([left, right], axis=1))
    for m in range(M):
        ext[m] = fields[m]
    diag, east, north, wet = fields[4:]
    row = iota((EXT_ROWS, EXT_COLS), 0)
    grid_row = b * ROWS + jnp.where(row >= 36, row - EXT_ROWS, row)
    inside = jnp.logical_and(grid_row >= 0, grid_row < NB * ROWS - 1)
    fe = east * wet * roll(wet, -1, 1)
    fw = roll(fe, 1, 1)
    fn = jnp.where(inside, north * wet * roll(wet, -1, 0), 0.0)
    fs = roll(fn, 1, 0)
    own = wet * diag
    centre = own + (1.0 - wet)
    inverse = 1.0 / (centre + fe + fw + fn + fs)
    for i, v in enumerate((fe, fw, fn, fs, centre, inverse, wet)):
        consts[i] = v
    mask = main(wet)
    row = iota((ROWS, COLS), 0)
    col = iota((ROWS, COLS), 1)
    sums = [
        jnp.where(col % 16 == 15, main(fe), 0.0),
        jnp.where(col % 16 == 0, main(fw), 0.0),
        jnp.where(row % 8 == 7, main(fn), 0.0),
        jnp.where(row % 8 == 0, main(fs), 0.0),
        main(own),
    ]
    energy, smooth = [], []
    for m in range(M):
        r = fields[m]
        y = inverse * r
        image = main(operate(y, (fe, fw, fn, fs, centre)))
        sums.append(mask * image)
        energy.append(full_sum(main(y) * image))
        smooth.append(full_sum(main(y) * main(r)))
    rows = block_sums(sums)
    lane = iota((8, 128), 1) % 32
    scalars = jnp.where(lane == 0, member_rows(energy), jnp.where(lane == 1, member_rows(smooth), 0.0))
    early[0] = pick([member_rows(rows[5:])] * 2 + [jnp.broadcast_to(rows[0], (8, 128)), jnp.broadcast_to(rows[1], (8, 128))])
    early[1] = pick([jnp.broadcast_to(rows[i], (8, 128)) for i in (2, 3, 4)] + [scalars])


def unpack_tile(tile, x):
    group = iota((24, 128), 1) // 32
    top = roll(jnp.where(group < 3, tile, 0.0), 32 * (x - 1), 1)
    group = lane_group()
    rest = jnp.zeros((8, 128), F32)
    for e in range(3):
        to = (e + x - 1) % 4
        rest = jnp.where(group == to, roll(tile[8 * e : 8 * e + 8], 32 * (to - 3), 1), rest)
    return jnp.concatenate([top, rest], axis=0)


def unpack_weights(blocks, b, g):
    c, y = b % 2, b // 2
    tiles = [unpack_tile(blocks[c * 16 + x * 4 + y, 24 * g : 24 * g + 24, :], x) for x in range(NX)]
    return halves(jnp.concatenate(tiles, axis=0))


def forward_sweep(coarse, weights, mine, live):
    group = lane_group()
    zero = jnp.zeros((8, 128), F32)
    s = [zero if v is None else v for v in coarse[0]]
    out = s
    for b in range(1, NB):
        new = []
        for g in range(NG):
            if not live(b, g):
                new.append(zero)
                continue
            left = s[g - 1] if g > 0 else zero
            right = s[g + 1] if g < NG - 1 else zero
            lhs = jnp.concatenate(
                [jnp.where(group == 3, left, s[g]), s[g], s[g], jnp.where(group == 0, right, s[g])], axis=0
            )
            hi, lo = weights(b, g)
            o = dot3(lhs, hi, lo, NT)
            carried = pick([o[8 * x : 8 * x + 8] for x in range(NX)])
            new.append(-carried if coarse[b][g] is None else coarse[b][g] - carried)
        s = new
        out = [jnp.where(mine == b, s[g], out[g]) for g in range(NG)]
    return out


def distance(g):
    return max(0, 4 * abs(g - 2) - 4) if g != 2 else -1


def inward(b, g):
    return distance(g) < NB - 1 - b


def outward(b, g):
    return distance(g) < b


def rimward(b, g):
    return distance(g) < b + 1


def backward_sweep(pivoted, weights):
    group = lane_group()
    zero = jnp.zeros((8, 128), F32)
    s = pivoted[NB - 1]
    out = [None] * NB
    out[NB - 1] = s
    for b in range(NB - 2, -1, -1):
        o = []
        for g in range(NG):
            if not rimward(b + 1, g):
                o.append(None)
                continue
            lhs = jnp.concatenate([jnp.where(group == x, s[g], 0.0) for x in range(NX)], axis=0)
            hi, lo = weights(b + 1, g)
            o.append(dot3(lhs, hi, lo, NN))
        s = []
        for g in range(NG):
            if o[g] is None or not rimward(b, g):
                s.append(zero)
                continue
            own = o[g][8:16] + o[g][16:24]
            own = own + jnp.where(group == 3, 0.0, o[g][0:8]) + jnp.where(group == 0, 0.0, o[g][24:32])
            after = o[g + 1][0:8] if g < NG - 1 and o[g + 1] is not None else zero
            before = o[g - 1][24:32] if g > 0 and o[g - 1] is not None else zero
            own = own + jnp.where(group == 3, after, 0.0) + jnp.where(group == 0, before, 0.0)
            s.append(pivoted[b][g] - own)
        out[b] = s
    return out


def pack_window(s, extra, out):
    parts = [jnp.where(lane_group() == 0, extra, s[0])] + list(s[1:])
    for g in range(NG):
        rows = parts[g][:4]
        for z in range(NZ):
            out[z, g] = rows


def to_plane(values, out):
    for d in range(NX * NB):
        for i, v in enumerate(values):
            out[d, :, 128 * i : 128 * i + 128] = v[:4]


def unpack_swept(got):
    if len(got.shape) == 3:
        out = [got[z] for z in range(NZ)]
    else:
        reached = iota((4, 128), 1) >= 32
        out = []
        for z in range(NZ):
            acc = jnp.where(reached, got[(z + 2) % NZ, 0], 0.0)
            for g in range(1, NG):
                acc = acc + got[(z + 2 - g) % NZ, g]
            out.append(acc)
    out = jnp.concatenate(out, axis=1)
    return jnp.concatenate([out, jnp.zeros_like(out)], axis=0)


def pivot_product(swept, pivots):
    rows = jnp.concatenate([p[...] for p in pivots], axis=0)
    hi, lo = halves(rows)
    out = dot3(swept, hi, lo, NT)
    return out[:, :128], jnp.concatenate([out[:, 128:160]] * 4, axis=1)


def unpack_plane(got, field):
    group = iota((64, 128), 1) // 32
    half = field // 4 * 128
    out = None
    for x in range(NX):
        bands = [got[x * NB + b, :, half : half + 128] for b in range(NB)]
        bands = [jnp.concatenate([v, jnp.zeros_like(v)], axis=0) for v in bands]
        piece = roll(jnp.concatenate(bands, axis=0), 32 * (x - field % 4), 1)
        out = piece if out is None else jnp.where(group == x, piece, out)
    return out


def coarse_operate(s, before, after, t):
    fe, fw, fn, fs, dg = t
    lane = iota((64, 128), 1)
    kc, kr = lane % 8, (lane // 8) % 4
    east = jnp.where(kc < 7, roll(s, -1, 1), jnp.where(lane < 96, roll(s, -25, 1), roll(after, -25, 1)))
    west = jnp.where(kc > 0, roll(s, 1, 1), jnp.where(lane >= 32, roll(s, 25, 1), roll(before, 25, 1)))
    north = jnp.where(kr < 3, roll(s, -8, 1), roll(roll(s, 24, 1), -8, 0))
    south = jnp.where(kr > 0, roll(s, 8, 1), roll(roll(s, -24, 1), 8, 0))
    return dg * s + fe * (s - east) + fw * (s - west) + fn * (s - north) + fs * (s - south)


def band_sum(value):
    acc = value[0:8]
    for b in range(1, NB):
        acc = acc + value[8 * b : 8 * b + 8]
    return jnp.sum(acc, axis=1, keepdims=True)


def stored(w_hi, w_lo):
    return lambda b, g: (w_hi[b * NG + g], w_lo[b * NG + g])


def plane_rows(blocks, at):
    return [
        jnp.concatenate([blocks[b % 2 * 16 + x * 4 + b // 2, at : at + 1, :] for b in range(NB)], axis=0) for x in range(NX)
    ]


def forward_kernel(pos, blocks, out, coarse_out, acts_out, w_hi, w_lo):
    coarse = [[] for _ in range(NB)]
    for g in range(NG):
        rows = plane_rows(blocks, 120 + g)
        members = [pick([roll(rows[x], 32 * (x - m), 1) for x in range(NX)]) for m in range(M)]
        for b in range(NB):
            coarse[b].append(member_rows([v[b : b + 1] for v in members]))
    for b in range(NB):
        coarse_out[8 * b : 8 * b + 8, :] = coarse[b][2]
    for i in range(3):
        act = pick(plane_rows(blocks, 125 + i))
        for b in range(NB):
            acts_out[i, 8 * b : 8 * b + 8, :] = jnp.broadcast_to(act[b : b + 1], (8, 128))

    def weights(b, g):
        hi, lo = unpack_weights(blocks, b, g)
        w_hi[b * NG + g] = hi
        w_lo[b * NG + g] = lo
        return hi, lo

    for b in range(1, NB):
        for g in range(NG):
            if not inward(b, g) and (rimward(b, g) or outward(b, g)):
                weights(b, g)
    own = forward_sweep(coarse, weights, pos[2], inward)[2][:4]
    for z in range(NZ):
        out[z] = own


def pivot_kernel(pos, got, early, p0, p1, p2, p3, p4, out):
    first, last = pivot_product(unpack_swept(got), (p0, p1, p2, p3, p4))
    to_plane([first, jnp.where(lane_group() == 0, last, early[0]), early[1]], out)


def middle_kernel(pos, got, w_hi, w_lo, coarse_right, acts, out, s_out, coarse_image_out, t_out):
    windows = [unpack_plane(got, f) for f in range(12)]
    pivoted = [[windows[g][8 * b : 8 * b + 8] for g in range(NG)] for b in range(NB)]
    settled = backward_sweep(pivoted, stored(w_hi, w_lo))
    s1, s2, s3 = (
        jnp.concatenate([settled[b][g] for b in range(NB)], axis=0) * acts[g - 1] for g in (1, 2, 3)
    )
    smooth, t, scalars = windows[5], windows[6:11], windows[11]
    t_s = coarse_operate(s2, s1, s3, t)
    coarse_image = acts[1] * (smooth + t_s)
    lane = iota((64, 128), 1) % 32
    weight = band_sum(coarse_right[...] * s2 + jnp.where(lane == 1, scalars, 0.0))
    energy = band_sum((2.0 * smooth + t_s) * s2 + jnp.where(lane == 0, scalars, 0.0))
    lane = iota((8, 128), 1)
    extra = jnp.where(lane == 0, weight, jnp.where(lane == 1, energy, 0.0))
    for i, v in enumerate((s1, s2, s3)):
        s_out[i] = v
    coarse_image_out[...] = coarse_image
    for i, v in enumerate(t):
        t_out[i] = v
    coarse = [[None, None, coarse_image[8 * b : 8 * b + 8], None, None] for b in range(NB)]
    pack_window(forward_sweep(coarse, stored(w_hi, w_lo), pos[2], outward), extra, out)


def spread_rows(s, x, kr):
    lane = iota((8, 128), 1)
    return jnp.take_along_axis(s, x * 32 + kr * 8 + lane // 16, axis=1)


def spread_sides(s1, s2, s3, x, kr):
    lane = iota((8, 128), 1)
    east = jnp.take_along_axis(jnp.where(x < 3, s2, s3), jnp.zeros_like(lane) + lax.rem(x + 1, 4) * 32 + kr * 8, axis=1)
    west = jnp.take_along_axis(jnp.where(x > 0, s2, s1), jnp.zeros_like(lane) + lax.rem(x + 3, 4) * 32 + kr * 8 + 7, axis=1)
    return jnp.where(lane < 64, east, west)


def image_kernel(pos, ext, consts, s_ref, pre_out, image_out):
    x, b = pos[1], pos[2]
    north_band, south_band = lax.rem(b + 1, NB), lax.rem(b + NB - 1, NB)
    own = [s_ref[g, b] for g in range(3)]
    up = [s_ref[g, north_band] for g in range(3)]
    down = [s_ref[g, south_band] for g in range(3)]
    mains = [spread_rows(own[1], x, kr) for kr in range(4)]
    sides = [spread_sides(*own, x, kr) for kr in range(4)]
    first = iota((8, 128), 0) < 4
    up_main, up_side = spread_rows(up[1], x, 0), spread_sides(*up, x, 0)
    down_main, down_side = spread_rows(down[1], x, 3), spread_sides(*down, x, 3)
    fields = tuple(consts[i] for i in range(5))
    inverse, wet = consts[5], consts[6]
    for m in range(M):
        wide = lambda v: jnp.broadcast_to(v[m : m + 1], (8, 128))
        left = [wide(v) for v in mains] + [jnp.where(first, wide(up_main), wide(down_main))]
        right = [wide(v) for v in sides] + [jnp.where(first, wide(up_side), wide(down_side))]
        spread = jnp.concatenate([jnp.concatenate(left, axis=0), jnp.concatenate(right, axis=0)], axis=1)
        pre = inverse * ext[m] + wet * spread
        pre_out[m] = main(pre)
        image_out[m] = operate(pre, fields)


def step_kernel(pos, got, ext, consts, image, p0, p1, p2, p3, p4, out, smooth_out, scalar_out):
    first, last = pivot_product(unpack_swept(got), (p0, p1, p2, p3, p4))
    sums = got[0, 0]
    for z in range(1, NZ):
        sums = sums + got[z, 0]
    sums = jnp.concatenate([sums, jnp.ones_like(sums)], axis=0)
    weight, energy = sums[:, 0:1], sums[:, 1:2]
    step = weight / energy
    fields = tuple(consts[i] for i in range(5))
    inverse, wet = consts[5], consts[6]
    mask = main(wet)
    blocks, dots = [], ([], [], [])
    for m in range(M):
        residual = ext[m] - step[m : m + 1] * image[m]
        smooth = inverse * residual
        applied = main(operate(smooth, fields))
        smooth = main(smooth)
        smooth_out[m] = smooth
        blocks.append(mask * applied)
        dots[0].append(full_sum(smooth * main(residual)))
        dots[1].append(full_sum(smooth * applied))
        dots[2].append(full_sum(smooth * main(image[m])))
    rows = member_rows(block_sums(blocks))
    lane = iota((8, 128), 1) % 32
    scalars = jnp.zeros((8, 128), F32)
    for i in range(3):
        scalars = jnp.where(lane == i, member_rows(dots[i]), scalars)
    to_plane([first, pick([last, rows, scalars, jnp.zeros((8, 128), F32)])], out)
    lane = iota((8, 128), 1)
    scalar_out[...] = jnp.where(lane == 0, weight, jnp.where(lane == 1, energy, jnp.where(lane == 2, step, 0.0)))


def last_kernel(pos, got, w_hi, w_lo, s_ref, coarse_right, coarse_image, t_ref, acts, scalar, out, s_out):
    windows = [unpack_plane(got, f) for f in range(7)]
    pivoted = [[windows[g][8 * b : 8 * b + 8] for g in range(NG)] for b in range(NB)]
    settled = backward_sweep(pivoted, stored(w_hi, w_lo))
    t = tuple(t_ref[i] for i in range(5))
    step = jnp.concatenate([scalar[:, 2:3]] * NB, axis=0)
    s1, s2, s3 = (
        s_ref[g - 1] - step * (jnp.concatenate([settled[b][g] for b in range(NB)], axis=0) * acts[g - 1])
        for g in (1, 2, 3)
    )
    s_out[...] = s2
    t_s = coarse_operate(s2, s1, s3, t)
    smooth, scalars = windows[5], windows[6]
    lane = iota((64, 128), 1) % 32
    dots = (
        band_sum((coarse_right[...] - step * coarse_image[...]) * s2 + jnp.where(lane == 0, scalars, 0.0)),
        band_sum((2.0 * smooth + t_s) * s2 + jnp.where(lane == 1, scalars, 0.0)),
        band_sum(coarse_image[...] * s2 + jnp.where(lane == 2, scalars, 0.0)),
    )
    lane = iota((1, 128), 1)
    res = jnp.zeros((1, 128), F32)
    for m in range(M):
        for i in range(3):
            res = jnp.where(lane == 32 * m + i, dots[i][m : m + 1], res)
    for z in range(NZ):
        out[z] = res


def finish_kernel(pos, got, scalar, pre, smooth, stack, s_ref, out):
    x, b = pos[1], pos[2]
    sums = got[0]
    for z in range(1, NZ):
        sums = sums + got[z]
    renewed, energy, cross = (
        jnp.concatenate([sums[:, 32 * m + i : 32 * m + i + 1] for m in range(M)], axis=0) for i in range(3)
    )
    weight, first_energy, step = scalar[:4, 0:1], scalar[:4, 1:2], scalar[:4, 2:3]
    ratio = renewed / weight
    second = renewed / (energy + 2.0 * ratio * cross + ratio * ratio * first_energy)
    own = s_ref[b]
    mains = [spread_rows(own, x, kr) for kr in range(4)]
    mask = stack[7]
    for m in range(M):
        spread = jnp.concatenate([jnp.broadcast_to(v[m : m + 1], (8, 128)) for v in mains], axis=0)
        z1 = smooth[m] + mask * spread
        z0 = pre[m]
        out[m] = step[m : m + 1] * z0 + second[m : m + 1] * (z1 + ratio[m : m + 1] * z0)


def shift(value, axes, count, by):
    return lax.ppermute(value, axes, [(i, (i + by) % count) for i in range(count)])


def ring_window(value):
    before, after = shift(value, "z", NZ, 1), shift(value, "z", NZ, -1)
    return [shift(before, "z", NZ, 1), before, value, after, shift(after, "z", NZ, -1)]


def to_all(value, axes, count):
    return lax.all_to_all(jnp.broadcast_to(value[None], (count,) + value.shape), axes, 0, 0)


def body(right_side, diagonal, east_face, north_face, wet, active, coupling, pivots):
    stack, tile, rims = call(
        start_kernel,
        [(8, ROWS, COLS), (48, 128), (2, 24, 128)],
        right_side, diagonal, east_face, north_face, wet, active[0], coupling[0, 0],
        fetch=range(7),
        room=FETCH_BYTES,
    )
    window = ring_window(tile)
    window[2], rims = call(own_kernel, [(48, 128), (2, 24, 128)], tile, rims)
    (plane,) = call(gather_kernel, [(NX * 4, 152, 128)], *window, rims)
    plane = lax.all_to_all(plane, ("x", "y"), 0, 0)
    blocks = to_all(plane, "c", 2).reshape(32, 152, 128)

    pivot_rows = ring_window(pivots[0])

    ring, rim = (NZ, NG, 4, 128), (M, EXT_ROWS, EXT_COLS)
    weights = ((NB * NG, 128, 128), BF16)
    ext, consts, early = call(
        fields_kernel, [rim, (7, EXT_ROWS, EXT_COLS), (2, 8, 128)], stack, blocks
    )
    swept, coarse_right, acts, w_hi, w_lo = call(
        forward_kernel, [(NZ, 4, 128), (64, 128), (3, 64, 128), weights, weights], blocks
    )
    swept, early, pivot_rows = lax.optimization_barrier((swept, early, pivot_rows))
    got = lax.all_to_all(swept, "z", 0, 0)
    (message,) = call(pivot_kernel, [(32, 4, 384)], got, early, *pivot_rows)
    got = lax.all_to_all(message, ("x", "y", "c"), 0, 0)
    swept, s0, coarse_image, t = call(
        middle_kernel, [ring, (3, 64, 128), (64, 128), (5, 64, 128)], got, w_hi, w_lo, coarse_right, acts
    )
    pre, image = call(image_kernel, [(M, ROWS, COLS), rim], ext, consts, s0.reshape(3, NB, 8, 128))
    swept, pre, image = lax.optimization_barrier((swept, pre, image))
    got = lax.all_to_all(swept, "z", 0, 0)
    message, smooth, scalar = call(
        step_kernel, [(32, 4, 256), (M, ROWS, COLS), (8, 128)], got, ext, consts, image, *pivot_rows
    )
    got = lax.all_to_all(message, ("x", "y", "c"), 0, 0)
    dots, s1 = call(
        last_kernel, [(NZ, 1, 128), (64, 128)], got, w_hi, w_lo, s0, coarse_right, coarse_image, t, acts, scalar
    )
    got = lax.all_to_all(dots, "z", 0, 0)
    (out,) = call(finish_kernel, [(M, ROWS, COLS)], got, scalar, pre, smooth, stack, s1.reshape(NB, 8, 128))
    return out


def solution(mesh):
    fine = Mesh(mesh.devices.reshape(NZ, NX, 4, 2), ("z", "x", "y", "c"))
    lat, lon = ("y", "c"), ("z", "x")
    in_specs = (
        P(None, lat, lon),
        P(lat, lon),
        P(lat, lon),
        P(lat, lon),
        P(lat, lon),
        P(lat, lon, None),
        P(lat, lon, None, None, None),
        P(lat, lon, None),
    )
    return jax.shard_map(body, mesh=fine, in_specs=in_specs, out_specs=P(None, lat, lon), check_vma=False)
```
